32 devices in a mesh: dp: 8 (over z, y), tensor: 4 (over x, core).
Axes of the slice: x: 2, y: 2, z: 4, core: 2. Of those that a mesh axis runs over, the one named last changes fastest.
Arguments:
- tokens: bfloat16 [16384, 1024], P('dp'), may hold values from -6 to 6
- prefix: int32 [8], P('dp'), may hold values from 204 to 1024
- gain_attn: bfloat16 [1024], replicated, may hold values from 0.5 to 1.5
- w_query: bfloat16 [1024, 1024], P(None, 'tensor'), may hold values from -0.1875 to 0.1875
- w_key: bfloat16 [1024, 512], P(None, 'tensor'), may hold values from -0.1875 to 0.1875
- w_value: bfloat16 [1024, 512], P(None, 'tensor'), may hold values from -0.1875 to 0.1875
- w_out: bfloat16 [1024, 1024], P('tensor'), may hold values from -3 to 3
- gain_moe: bfloat16 [1024], replicated, may hold values from 0.5 to 1.5
- w_router: bfloat16 [1024, 32], replicated, may hold values from -0.09375 to 0.09375
- routes: int32 [16384, 8], P(('dp', 'tensor')), may hold values from 0 to 31, all different within a row
- fill_order: int32 [32, 512], P(('dp', 'tensor')), may hold values from 0 to 511, each once within a row
- w_gate: bfloat16 [32, 1024, 512], P('dp', None, 'tensor'), may hold values from -0.1875 to 0.1875
- w_up: bfloat16 [32, 1024, 512], P('dp', None, 'tensor'), may hold values from -0.1875 to 0.1875
- w_down: bfloat16 [32, 512, 1024], P('dp', 'tensor'), may hold values from -1 to 1
- cotangent: bfloat16 [16384, 1024], P(('dp', 'tensor')), may hold values from -6 to 6
Outputs:
- block_output: bfloat16 [16384, 1024], P(('dp', 'tensor'))
- grad_tokens: float32 [16384, 1024], P('dp')
- grad_gain_attn: float32 [1024], replicated
- grad_query: float32 [1024, 1024], P(None, 'tensor')
- grad_key: float32 [1024, 512], P(None, 'tensor')
- grad_value: float32 [1024, 512], P(None, 'tensor')
- grad_out: float32 [1024, 1024], P('tensor')
- grad_gain_moe: float32 [1024], replicated
- grad_router: float32 [1024, 32], replicated
- grad_gate: float32 [32, 1024, 512], P('dp', None, 'tensor')
- grad_up: float32 [32, 1024, 512], P('dp', None, 'tensor')
- grad_down: float32 [32, 512, 1024], P('dp', 'tensor')
The draws below stay inside these ranges and needn't reach their ends.
Inputs may be any that keep to these rules, and one draw needn't show every extreme that they name: `routes`: each row names 8 different experts, and every expert is named by some row. `fill_order`: each row is a permutation of 0 to 511.
All inputs are finite; a program needn't handle non-finite values.
Results may differ from the reference program's by a relative error of at most 0.023.
Values may be sent and summed in bfloat16 or wider, within the bound.
No kernel may reach another device: no remote copies, remote signals or barrier semaphores. Data moves between devices by JAX's collectives and lax.ppermute only.
A program may use at most 512 MiB of HBM per device.

```python
import functools
import jax
import jax.numpy as jnp
from jax import lax

D = 1024
QH = 16
KVH = 8
HD = 64
FF = 512
EXPERTS = 32
TOPK = 8
TOK_DEV = 2048
SEQS = 8
TOKENS = 16384
ROWS = 512
CAP = 128
N_DP = 8
N_TENSOR = 4


def plant(array, stream_key, smallest, high):
    longest = array.shape.index(max(array.shape))
    spots = []
    for shift in (0, 1):
        where = [jax.random.randint(jax.random.fold_in(stream_key, axis), (), 0, length) for axis, length in enumerate(array.shape)]
        where[longest] = (where[longest] + shift) % array.shape[longest]
        spots.append(tuple(where))
    return array.at[spots[0]].set(smallest).at[spots[1]].set(high)


def levels(rng, shape, pieces, low, largest):
    level = 1.0
    for position, shards_of in pieces:
        draws = jax.random.uniform(jax.random.fold_in(jax.random.fold_in(rng, 6), position), (shards_of,), jnp.float32, low / len(pieces), largest / len(pieces))
        level = level * jnp.repeat(jnp.exp(draws), shape[position] // shards_of).reshape((-1,) + (1,) * (len(shape) - 1 - position))
    return level


def choose_distinct(rng, rows, count, top, lift):
    ranking = jax.random.permutation(jax.random.fold_in(rng, 1), count)
    boost = ranking
    for power in range(3):
        boost = boost * boost // count
    boost = boost * lift // count
    chance = jax.random.randint(jax.random.fold_in(rng, 2), (rows, count), 0, 4096) + boost
    fixed_rows = jax.random.permutation(jax.random.fold_in(rng, 3), rows)[jnp.arange(count) % rows]
    chance = jnp.where(jnp.arange(rows)[:, None] == fixed_rows[None, :], 1 << 14, chance)
    score = chance * count + jnp.arange(count)
    return lax.top_k(score.astype(jnp.int32), top)[1].astype(jnp.int32)


def scatter_about(own_key, extent, width, reach, split=(), held_as=jnp.bfloat16):
    entries = jax.random.normal(own_key, extent, jnp.float32) * width
    if len(split) > 0:
        entries = levels(own_key, extent, split, -0.22, 0.18) * entries
    return jnp.clip(entries, min=-reach, max=reach).astype(held_as)


def setup_inputs(seed: int = 0) -> dict:
    streams_of = jax.random.split(jax.random.key(seed), 16)
    return {
        "tokens": scatter_about(streams_of[0], (TOKENS, D), 1.0, 6.0, ((0, 8),)),
        "prefix": plant(jax.random.randint(streams_of[1], (SEQS,), TOK_DEV // 10, TOK_DEV // 2 + 1), jax.random.fold_in(streams_of[1], 1), TOK_DEV // 10, (TOK_DEV // 2 + 1) - 1).astype(jnp.int32),
        "gain_attn": jnp.clip(1.0 + 0.1 * jax.random.normal(streams_of[2], (D,), jnp.float32), 0.5, 1.5).astype(jnp.bfloat16),
        "w_query": scatter_about(streams_of[3], (D, QH * HD), D ** -0.5, 0.1875, ((1, 4),)),
        "w_key": scatter_about(streams_of[4], (D, KVH * HD), D ** -0.5, 0.1875, ((1, 4),)),
        "w_value": scatter_about(streams_of[5], (D, KVH * HD), D ** -0.5, 0.1875, ((1, 4),)),
        "w_out": scatter_about(streams_of[6], (QH * HD, D), 4 ** -0.5, 3.0, ((0, 4),)),
        "gain_moe": jnp.clip(1.0 + 0.1 * jax.random.normal(streams_of[7], (D,), jnp.float32), 0.5, 1.5).astype(jnp.bfloat16),
        "w_router": scatter_about(streams_of[8], (D, EXPERTS), (4 * D) ** -0.5, 0.09375),
        "routes": choose_distinct(streams_of[9], TOKENS, EXPERTS, TOPK, 2048),
        "fill_order": jax.vmap(lambda own: jax.random.permutation(own, ROWS))(jax.random.split(streams_of[10], (N_DP * N_TENSOR))).reshape((N_DP * N_TENSOR, ROWS)).astype(jnp.int32),
        "w_gate": scatter_about(streams_of[11], (EXPERTS, D, FF), D ** -0.5, 0.1875, ((0, 8), (2, 4))),
        "w_up": scatter_about(streams_of[12], (EXPERTS, D, FF), D ** -0.5, 0.1875, ((0, 8), (2, 4))),
        "w_down": scatter_about(streams_of[13], (EXPERTS, FF, D), (FF // 16) ** -0.5, 1.0, ((0, 8), (1, 4))),
        "cotangent": scatter_about(streams_of[14], (TOKENS, D), 1.0, 6.0, ((0, 32),)),
    }


EPSILON = 1e-06
THETA_BASE = 10000.0
HIGHEST = lax.Precision.HIGHEST

@jax.custom_vjp
def low(v):
    return lax.optimization_barrier(v.astype(jnp.bfloat16)).astype(jnp.float32)

@jax.custom_vjp
def low_back(v):
    return v

def low_keep(v):
    return (low(v), None)

def low_pass(kept, grad):
    return (grad,)

def back_keep(v):
    return (v, None)

def back_low(kept, grad):
    return (low(grad),)
low.defvjp(low_keep, low_pass)
low_back.defvjp(back_keep, back_low)

def rope_tables(length, width_in):
    half_width = width_in // 2
    frequency = THETA_BASE ** (-(jnp.arange(half_width, dtype=jnp.float32) / half_width))
    angles = jnp.arange(length, dtype=jnp.float32)[:, None] * frequency[None, :]
    return (jnp.cos(angles), jnp.sin(angles))

def rotate(vectors, cosine, sine, direction):
    half_width = vectors.shape[-1] // 2
    front_half = vectors[..., :half_width]
    back_half = vectors[..., half_width:]
    cos_part = cosine[:, None, :]
    sin_part = sine[:, None, :] * direction
    return jnp.concatenate([front_half * cos_part - back_half * sin_part, back_half * cos_part + front_half * sin_part], -1)

def count_earlier(inputs):
    priority_row, member_rows = inputs
    earlier = (priority_row[None, :] < priority_row[:, None]).astype(jnp.float32)
    return lax.optimization_barrier(jnp.sum(earlier[:, :, None] * member_rows[None, :, :], 1))

def slot_layout(routes, fill_order):
    sources = N_DP * N_TENSOR
    expert_ids = jnp.arange(EXPERTS, dtype=jnp.int32)
    choice_hot = (routes[:, :, None] == expert_ids[None, None, :]).astype(jnp.float32)
    member = lax.optimization_barrier(jnp.sum(choice_hot, 1)).reshape(sources, ROWS, EXPERTS)
    priority = fill_order.reshape(sources, ROWS)
    slot_full = lax.map(count_earlier, (priority, member)).reshape(TOKENS, EXPERTS)
    slot_pair = lax.optimization_barrier(jnp.sum(choice_hot * slot_full[:, None, :], -1)).astype(jnp.int32)
    kept_pair = slot_pair < CAP
    source = jnp.arange(TOKENS, dtype=jnp.int32) // ROWS
    dump_slot = EXPERTS * sources * CAP
    target = routes * (sources * CAP) + source[:, None] * CAP + slot_pair
    target = jnp.where(kept_pair, target, dump_slot).astype(jnp.int32)
    token_ids = jnp.broadcast_to(jnp.arange(TOKENS, dtype=jnp.int32)[:, None], target.shape)
    token_of = jnp.zeros((dump_slot + 1,), jnp.int32).at[target.reshape(-1)].set(token_ids.reshape(-1))
    filled = jnp.zeros((dump_slot + 1,), jnp.float32).at[target.reshape(-1)].set(1.0)
    return (choice_hot, target, token_of[:dump_slot], filled[:dump_slot])

def forward(layout, prefix, x_full, gain_attn, w_query, w_key, w_value, w_out, gain_moe, w_router, w_gate, w_up, w_down):
    choice_hot, target, token_of, filled = layout
    cosine, sine = rope_tables(TOK_DEV, HD)
    positions = jnp.arange(TOK_DEV, dtype=jnp.int32)
    group_size = QH // KVH

    def attend(inputs):
        seq_rows, prefix_len = inputs
        inv_rms = lax.rsqrt(lax.optimization_barrier(jnp.mean(seq_rows * seq_rows, -1, keepdims=True)) + EPSILON)
        normed = low(seq_rows * inv_rms * gain_attn)
        queries = low_back(jnp.dot(normed, w_query, precision=HIGHEST)).reshape(TOK_DEV, QH, HD)
        keys_raw = low_back(jnp.dot(normed, w_key, precision=HIGHEST)).reshape(TOK_DEV, KVH, HD)
        values = low(low_back(jnp.dot(normed, w_value, precision=HIGHEST))).reshape(TOK_DEV, KVH, HD)
        query_rot = low(rotate(queries, cosine, sine, 1.0)).reshape(TOK_DEV, KVH, group_size, HD)
        key_rot = low(rotate(keys_raw, cosine, sine, 1.0))
        scores = jnp.einsum('igjd,kgd->gjik', query_rot, key_rot, precision=HIGHEST) * HD ** (-0.5)
        scores = low_back(scores)
        visible = (positions[None, :] <= positions[:, None]) | (positions[None, :] < prefix_len)
        scores = jnp.where(visible[None, None], scores, -1e+30)
        row_peak = lax.optimization_barrier(jnp.max(scores, -1, keepdims=True))
        weights = jnp.exp(scores - row_peak)
        probabilities = weights / lax.optimization_barrier(jnp.sum(weights, -1, keepdims=True))
        attended = jnp.einsum('gjik,kgd->igjd', low(probabilities), values, precision=HIGHEST).reshape(TOK_DEV, QH * HD)
        attended = low(low_back(attended))
        return jnp.dot(attended, w_out, precision=HIGHEST)
    attention = lax.map(jax.checkpoint(attend), (x_full.reshape(N_DP, TOK_DEV, D), prefix)).reshape(TOKENS, D)
    attention = low_back(attention)
    hidden_in = x_full + attention
    rms_two = lax.rsqrt(lax.optimization_barrier(jnp.mean(hidden_in * hidden_in, -1, keepdims=True)) + EPSILON)
    normed_two = low(hidden_in * rms_two * gain_moe)
    logits = jnp.dot(normed_two, w_router, precision=HIGHEST)
    chosen = lax.optimization_barrier(jnp.sum(choice_hot * logits[:, None, :], -1))
    top_logit = lax.optimization_barrier(jnp.max(chosen, -1, keepdims=True))
    raised = jnp.exp(chosen - top_logit)
    gate_weights = raised / lax.optimization_barrier(jnp.sum(raised, -1, keepdims=True))
    expert_rows = low_back(jnp.take(normed_two, token_of, 0) * filled[:, None])
    expert_rows = expert_rows.reshape(EXPERTS, N_DP * N_TENSOR * CAP, D)
    gate_pre = low_back(jnp.einsum('erd,edf->erf', expert_rows, w_gate, precision=HIGHEST))
    up_pre = low_back(jnp.einsum('erd,edf->erf', expert_rows, w_up, precision=HIGHEST))
    activated = low(gate_pre / (1.0 + jnp.exp(-gate_pre)) * up_pre)
    expert_out = jnp.einsum('erf,efd->erd', activated, w_down, precision=HIGHEST).reshape(-1, D)
    expert_out = low(low_back(expert_out))
    padded = jnp.concatenate([expert_out, jnp.zeros((1, D), jnp.float32)], 0)
    combined = hidden_in
    for slot_index in range(TOPK):
        combined = combined + gate_weights[:, slot_index:slot_index + 1] * jnp.take(padded, target[:, slot_index], 0)
    return combined

def reference(tokens, prefix, gain_attn, w_query, w_key, w_value, w_out, gain_moe, w_router, routes, fill_order, w_gate, w_up, w_down, cotangent):
    layout = slot_layout(routes, fill_order)
    floats = tuple((element.astype(jnp.float32) for element in (tokens, gain_attn, w_query, w_key, w_value, w_out, gain_moe, w_router, w_gate, w_up, w_down)))
    result, pullback = jax.vjp(functools.partial(forward, layout, prefix), *floats)
    gradients = pullback(cotangent.astype(jnp.float32))
    return (result.astype(jnp.bfloat16), gradients[0], gradients[1], gradients[2], gradients[3], gradients[4], gradients[5], gradients[6], gradients[7], gradients[8], gradients[9], gradients[10])
```

```python
import jax
import jax.numpy as jnp
from jax import lax
from jax.sharding import PartitionSpec as P

HD = 64
EXPERTS = 32
TOPK = 8


EPSILON = 1e-06
THETA_BASE = 10000.0
HIGHEST = lax.Precision.HIGHEST


def rope_tables(length, width_in):
    half_width = width_in // 2
    frequency = THETA_BASE ** (-(jnp.arange(half_width, dtype=jnp.float32) / half_width))
    angles = jnp.arange(length, dtype=jnp.float32)[:, None] * frequency[None, :]
    return (jnp.cos(angles), jnp.sin(angles))


def rotate(vectors, cosine, sine, direction):
    half_width = vectors.shape[-1] // 2
    front_half = vectors[..., :half_width]
    back_half = vectors[..., half_width:]
    cos_part = cosine[:, None, :]
    sin_part = sine[:, None, :] * direction
    return jnp.concatenate(
        [
            front_half * cos_part - back_half * sin_part,
            back_half * cos_part + front_half * sin_part,
        ],
        -1,
    )


def group_gather(x, axes):
    return lax.all_gather(x, axes, axis=0, tiled=False)


def per_device(
    tokens,
    prefix,
    gain_attn,
    w_query,
    w_key,
    w_value,
    w_out,
    gain_moe,
    w_router,
    routes,
    fill_order,
    w_gate,
    w_up,
    w_down,
    cotangent,
):
    f32 = jnp.float32
    bf16 = jnp.bfloat16
    z_count = lax.axis_size("z")
    y_count = lax.axis_size("y")
    shards = lax.axis_size("x") * lax.axis_size("c")
    z_rank = lax.axis_index("z")
    tensor_rank = lax.axis_index("x") * lax.axis_size("c") + lax.axis_index("c")
    length = tokens.shape[0]
    model_width = tokens.shape[1]
    own_rows = routes.shape[0]
    local_experts = w_gate.shape[0]
    group_experts = local_experts * y_count
    capacity = own_rows * TOPK // EXPERTS
    heads_local = w_query.shape[1] // HD
    kv_local = w_key.shape[1] // HD
    group_size = heads_local // kv_local
    block_rows = min(512, length)
    block_count = length // block_rows
    score_scale = HD ** (-0.5)
    hidden = w_gate.shape[2] * shards

    expert_ids = jnp.arange(EXPERTS, dtype=jnp.int32)
    member = jnp.sum((routes[:, :, None] == expert_ids[None, None, :]).astype(f32), 1)
    priority = fill_order[0]
    earlier = (priority[None, :] < priority[:, None]).astype(bf16)
    slot_full = jnp.dot(earlier, member.astype(bf16), preferred_element_type=f32)
    slot_code = jnp.where(member > 0, jnp.minimum(slot_full, float(capacity)), -1.0).astype(bf16)

    weights_gate = group_gather(w_gate, ("y", "x", "c")).reshape(
        y_count, shards, local_experts, model_width, -1
    )
    weights_up = group_gather(w_up, ("y", "x", "c")).reshape(
        y_count, shards, local_experts, model_width, -1
    )
    weights_down = group_gather(w_down, ("y", "x", "c")).reshape(
        y_count, shards, local_experts, -1, model_width
    )
    weights_gate = weights_gate.transpose(0, 2, 3, 1, 4).reshape(group_experts, model_width, hidden)
    weights_up = weights_up.transpose(0, 2, 3, 1, 4).reshape(group_experts, model_width, hidden)
    weights_down = weights_down.transpose(0, 2, 1, 3, 4).reshape(group_experts, hidden, model_width)
    cot_all = lax.all_gather(cotangent, "z", axis=0, tiled=False)
    code_all = lax.all_gather(slot_code, "z", axis=0, tiled=False)

    x_full = tokens.astype(f32)
    rms_one = lax.rsqrt(jnp.mean(x_full * x_full, -1, keepdims=True) + EPSILON)
    gain_one = gain_attn.astype(f32)
    normed_one = (x_full * rms_one * gain_one).astype(bf16)
    query_raw = jnp.dot(normed_one, w_query, preferred_element_type=f32)
    key_raw = jnp.dot(normed_one, w_key, preferred_element_type=f32)
    values = (
        jnp.dot(normed_one, w_value, preferred_element_type=f32)
        .astype(bf16)
        .reshape(length, kv_local, HD)
    )
    cosine, sine = rope_tables(length, HD)
    query_rot = rotate(query_raw.reshape(length, heads_local, HD), cosine, sine, 1.0).astype(bf16)
    key_rot = rotate(key_raw.reshape(length, kv_local, HD), cosine, sine, 1.0).astype(bf16)
    query_blocks = query_rot.reshape(block_count, block_rows, kv_local, group_size, HD)
    block_starts = jnp.arange(block_count, dtype=jnp.int32) * block_rows
    positions = jnp.arange(length, dtype=jnp.int32)
    prefix_len = prefix[0]

    def block_scores(query_block, offset):
        query_pos = offset + jnp.arange(block_rows, dtype=jnp.int32)
        raw_scores = (
            jnp.einsum("igjd,kgd->gjik", query_block, key_rot, preferred_element_type=jnp.float32)
            * score_scale
        )
        visible = (positions[None, :] <= query_pos[:, None]) | (positions[None, :] < prefix_len)
        return jnp.where(visible[None, None], raw_scores, -1e30)

    def attend_block(inputs):
        query_block, offset = inputs
        scores = block_scores(query_block, offset)
        row_peak = jnp.max(scores, -1, keepdims=True)
        weights = jnp.exp(scores - row_peak)
        row_total = jnp.sum(weights, -1, keepdims=True)
        probabilities = (weights / row_total).astype(jnp.bfloat16)
        attended = jnp.einsum(
            "gjik,kgd->igjd", probabilities, values, preferred_element_type=jnp.float32
        )
        return (attended.astype(jnp.bfloat16), (row_peak + jnp.log(row_total))[..., 0])

    attended_blocks, log_totals = lax.map(attend_block, (query_blocks, block_starts))
    attended_all = attended_blocks.reshape(length, heads_local * HD)
    attention_rows = lax.psum_scatter(
        jnp.dot(attended_all, w_out, preferred_element_type=f32).astype(bf16),
        ("x", "c"),
        scatter_dimension=0,
        tiled=True,
    ).astype(f32)
    x_rows = lax.dynamic_slice_in_dim(tokens, tensor_rank * own_rows, own_rows, 0).astype(f32)
    hidden_in = x_rows + attention_rows
    rms_two = lax.rsqrt(jnp.mean(hidden_in * hidden_in, -1, keepdims=True) + EPSILON)
    gain_two = gain_moe.astype(f32)
    normed_two = (hidden_in * rms_two * gain_two).astype(bf16)
    normed_all = lax.all_gather(normed_two, "z", axis=0, tiled=False)

    def gates(rows, code):
        logits = jnp.dot(rows, w_router, preferred_element_type=f32)
        chosen = jnp.where(code >= 0, logits, -jnp.inf)
        raised = jnp.exp(chosen - jnp.max(chosen, -1, keepdims=True))
        return raised / jnp.sum(raised, -1, keepdims=True)

    gate_own = gates(normed_two, slot_code)
    first = z_rank * group_experts
    gate_all = jax.vmap(gates)(normed_all, code_all)
    gate_group = lax.dynamic_slice_in_dim(gate_all, first, group_experts, 2)
    code_group = lax.dynamic_slice_in_dim(code_all, first, group_experts, 2).astype(jnp.int32)
    slot_ids = jnp.arange(capacity, dtype=jnp.int32)
    hot = code_group.transpose(2, 0, 1)[:, :, None, :] == slot_ids[None, None, :, None]
    pick = hot.astype(bf16)
    pick_gate = jnp.where(hot, gate_group.transpose(2, 0, 1)[:, :, None, :], 0.0)
    gate_slot = jnp.sum(pick_gate, -1)
    rows_in = jnp.einsum("esci,sid->escd", pick, normed_all, preferred_element_type=f32).astype(bf16)
    rows_dy = jnp.einsum("esci,sid->escd", pick, cot_all, preferred_element_type=f32)
    gate_pre = jnp.einsum("escd,edf->escf", rows_in, weights_gate, preferred_element_type=f32)
    up_pre = jnp.einsum("escd,edf->escf", rows_in, weights_up, preferred_element_type=f32)
    activated = (gate_pre / (1.0 + jnp.exp(-gate_pre)) * up_pre).astype(bf16)
    expert_out = jnp.einsum(
        "escf,efd->escd", activated, weights_down, preferred_element_type=f32
    ).astype(bf16)
    out_grad_rows = (rows_dy * gate_slot[..., None]).astype(bf16)
    gate_grad_slot = jnp.sum(rows_dy * expert_out.astype(f32), -1)
    gate_grad = jnp.einsum("esci,esc->sie", pick.astype(f32), gate_grad_slot, precision=HIGHEST)
    moe_part = jnp.einsum(
        "esci,escd->sid", pick_gate.astype(bf16), expert_out, preferred_element_type=f32
    ).astype(bf16)
    hid_grad = jnp.einsum("escd,efd->escf", out_grad_rows, weights_down, preferred_element_type=f32)
    sigmoid_g = 1.0 / (1.0 + jnp.exp(-gate_pre))
    back_gate = (hid_grad * up_pre * sigmoid_g * (1.0 + gate_pre * (1.0 - sigmoid_g))).astype(bf16)
    back_up = (hid_grad * gate_pre * sigmoid_g).astype(bf16)
    rows_grad = (
        jnp.einsum("escf,edf->escd", back_gate, weights_gate, preferred_element_type=f32)
        + jnp.einsum("escf,edf->escd", back_up, weights_up, preferred_element_type=f32)
    ).astype(bf16)
    rows_part = jnp.einsum("esci,escd->sid", pick, rows_grad, preferred_element_type=f32).astype(bf16)
    down_part = jnp.einsum("escf,escd->efd", activated, out_grad_rows, preferred_element_type=f32)
    gate_part = jnp.einsum("escd,escf->edf", rows_in, back_gate, preferred_element_type=f32)
    up_part = jnp.einsum("escd,escf->edf", rows_in, back_up, preferred_element_type=f32)

    gate_grad_wide = lax.dynamic_update_slice_in_dim(
        jnp.zeros((z_count, own_rows, EXPERTS), f32), gate_grad, first, 2
    )
    back_pack = jnp.concatenate([rows_part, gate_grad_wide.astype(bf16)], -1)
    back_own = lax.psum_scatter(back_pack, "z", scatter_dimension=0, tiled=False).astype(f32)
    moe_own = lax.psum_scatter(moe_part, "z", scatter_dimension=0, tiled=False).astype(f32)
    block_output = (hidden_in + moe_own).astype(bf16)

    def shard_sum(part, dim):
        width = part.shape[dim] // shards
        split = part.reshape((y_count, local_experts) + part.shape[1:dim] + (shards, width) + part.shape[dim + 1 :])
        split = jnp.moveaxis(split, dim + 1, 1).astype(bf16)
        split = split.reshape((y_count * shards,) + split.shape[2:])
        return lax.psum_scatter(split, ("y", "x", "c"), scatter_dimension=0, tiled=False).astype(f32)

    grad_gate = shard_sum(gate_part, 2)
    grad_up = shard_sum(up_part, 2)
    grad_down = shard_sum(down_part, 1)

    normed_two_grad = back_own[:, :model_width]
    gate_grad_own = back_own[:, model_width:]
    logit_grad = gate_own * (
        gate_grad_own - jnp.sum(gate_own * gate_grad_own, -1, keepdims=True)
    )
    router_part = jnp.dot(normed_two.astype(f32).T, logit_grad, precision=HIGHEST)
    normed_two_grad = normed_two_grad + jnp.dot(
        logit_grad, w_router.astype(f32).T, precision=HIGHEST
    )
    gain_two_part = jnp.sum(normed_two_grad * hidden_in * rms_two, 0)
    scaled_two = normed_two_grad * gain_two
    grad_rows = cotangent.astype(f32)
    hidden_grad = (
        grad_rows
        + rms_two * scaled_two
        - hidden_in * rms_two**3 * jnp.mean(scaled_two * hidden_in, -1, keepdims=True)
    )
    shard_part = lax.all_gather(
        hidden_grad.astype(bf16), ("x", "c"), axis=0, tiled=True
    ).astype(f32)
    attended_part = jnp.einsum(
        "id,hd->ih", shard_part.astype(jnp.bfloat16), w_out, preferred_element_type=jnp.float32
    )
    attended_grad = attended_part.astype(jnp.bfloat16)
    out_grad = jnp.einsum(
        "ih,id->hd",
        attended_all,
        shard_part.astype(jnp.bfloat16),
        preferred_element_type=jnp.float32,
    )
    grad_blocks = attended_grad.reshape(block_count, block_rows, kv_local, group_size, HD)

    def back_block(running, inputs):
        key_acc, value_acc = running
        query_block, grad_block, log_block, offset = inputs
        scores = block_scores(query_block, offset)
        probabilities = jnp.exp(scores - log_block[..., None])
        prob_grad = jnp.einsum(
            "igjd,kgd->gjik", grad_block, values, preferred_element_type=jnp.float32
        )
        center = jnp.sum(prob_grad * probabilities, -1, keepdims=True)
        score_grad = (probabilities * (prob_grad - center)).astype(jnp.bfloat16)
        query_grad = (
            jnp.einsum("gjik,kgd->igjd", score_grad, key_rot, preferred_element_type=jnp.float32)
            * score_scale
        )
        key_acc = (
            key_acc
            + jnp.einsum(
                "gjik,igjd->kgd", score_grad, query_block, preferred_element_type=jnp.float32
            )
            * score_scale
        )
        value_acc = value_acc + jnp.einsum(
            "gjik,igjd->kgd",
            probabilities.astype(jnp.bfloat16),
            grad_block,
            preferred_element_type=jnp.float32,
        )
        return ((key_acc, value_acc), query_grad)

    zero_kv = jnp.zeros((length, kv_local, HD), jnp.float32)
    (key_grad, value_grad), query_grads = lax.scan(
        back_block, (zero_kv, zero_kv), (query_blocks, grad_blocks, log_totals, block_starts)
    )
    query_back = (
        rotate(query_grads.reshape(length, heads_local, HD), cosine, sine, -1.0)
        .reshape(length, heads_local * HD)
        .astype(jnp.bfloat16)
    )
    key_back = (
        rotate(key_grad, cosine, sine, -1.0).reshape(length, kv_local * HD).astype(jnp.bfloat16)
    )
    value_back = value_grad.reshape(length, kv_local * HD).astype(jnp.bfloat16)
    query_weight = jnp.einsum(
        "id,ih->dh", normed_one, query_back, preferred_element_type=jnp.float32
    )
    key_weight = jnp.einsum("id,ih->dh", normed_one, key_back, preferred_element_type=jnp.float32)
    value_weight = jnp.einsum(
        "id,ih->dh", normed_one, value_back, preferred_element_type=jnp.float32
    )
    normed_one_grad = jnp.einsum(
        "ih,dh->id", query_back, w_query, preferred_element_type=jnp.float32
    )
    normed_one_grad = normed_one_grad + jnp.einsum(
        "ih,dh->id", key_back, w_key, preferred_element_type=jnp.float32
    )
    normed_one_grad = normed_one_grad + jnp.einsum(
        "ih,dh->id", value_back, w_value, preferred_element_type=jnp.float32
    )
    total_one = lax.psum(normed_one_grad.astype(bf16), ("x", "c")).astype(f32)
    gain_one_part = jnp.sum(normed_one_grad * x_full * rms_one, 0)
    scaled_one = total_one * gain_one
    input_grad = (
        shard_part
        + rms_one * scaled_one
        - x_full * rms_one**3 * jnp.mean(scaled_one * x_full, -1, keepdims=True)
    )
    dp = ("z", "y")
    everyone = ("z", "y", "x", "c")
    summed = [
        lax.psum(part.astype(bf16), dp).astype(f32)
        for part in (query_weight, key_weight, value_weight, out_grad)
    ]
    router_total, gain_one_total, gain_two_total = (
        lax.psum(part.astype(bf16), everyone).astype(f32)
        for part in (router_part, gain_one_part, gain_two_part)
    )
    return (
        block_output,
        input_grad,
        gain_one_total,
        summed[0],
        summed[1],
        summed[2],
        summed[3],
        gain_two_total,
        router_total,
        grad_gate,
        grad_up,
        grad_down,
    )


def solution(mesh):
    dp_count, tensor_count = mesh.devices.shape
    mesh = jax.sharding.Mesh(
        mesh.devices.reshape(dp_count // 2, 2, tensor_count // 2, 2), ("z", "y", "x", "c")
    )
    dp = ("z", "y")
    tensor = ("x", "c")
    both = dp + tensor
    return jax.shard_map(
        per_device,
        mesh=mesh,
        in_specs=(
            P(dp, None),
            P(dp),
            P(),
            P(None, tensor),
            P(None, tensor),
            P(None, tensor),
            P(tensor, None),
            P(),
            P(),
            P(both, None),
            P(both, None),
            P(dp, None, tensor),
            P(dp, None, tensor),
            P(dp, tensor, None),
            P(both, None),
        ),
        out_specs=(
            P(both, None),
            P(dp, None),
            P(),
            P(None, tensor),
            P(None, tensor),
            P(None, tensor),
            P(tensor, None),
            P(),
            P(),
            P(dp, None, tensor),
            P(dp, None, tensor),
            P(dp, tensor, None),
        ),
        check_vma=False,
    )
```

```python
import functools

import jax
import jax.numpy as jnp
import numpy as np
from jax import lax
from jax.experimental import pallas as pl
from jax.experimental.pallas import tpu as pltpu
from jax.sharding import PartitionSpec as P

HD = 64
EXPERTS = 32
TOPK = 8


EPSILON = 1e-06
THETA_BASE = 10000.0
HIGHEST = lax.Precision.HIGHEST


def rope_tables(length, width_in):
    half_width = width_in // 2
    frequency = THETA_BASE ** (-(jnp.arange(half_width, dtype=jnp.float32) / half_width))
    angles = jnp.arange(length, dtype=jnp.float32)[:, None] * frequency[None, :]
    return (jnp.cos(angles), jnp.sin(angles))


def rotate(vectors, cosine, sine, direction):
    half_width = vectors.shape[-1] // 2
    front_half = vectors[..., :half_width]
    back_half = vectors[..., half_width:]
    cos_part = cosine[:, None, :]
    sin_part = sine[:, None, :] * direction
    return jnp.concatenate(
        [
            front_half * cos_part - back_half * sin_part,
            back_half * cos_part + front_half * sin_part,
        ],
        -1,
    )


NT = (((1,), (1,)), ((), ()))
TN = (((0,), (0,)), ((), ()))
f32 = jnp.float32
bf16 = jnp.bfloat16
BQ = 512
BK = 1024
BK_BACK = 512

def busy(us):
    return pl.CostEstimate(flops=int(us * 1e8), bytes_accessed=0, transcendentals=0)


def lanes(shape):
    return lax.broadcasted_iota(jnp.int32, shape, len(shape) - 1)

def rope_wide(v, cos, sin):
    low = lanes(v.shape) % HD < HD // 2
    swapped = jnp.where(low, pltpu.roll(v, 128 - HD // 2, 1), pltpu.roll(v, HD // 2, 1))
    return v * cos + swapped * sin

def project_kernel(x_ref, gain_ref, wq_ref, wk_ref, wv_ref, cos_ref, sin_ref, a_ref, q_ref, k_ref, v_ref):
    x = x_ref[...].astype(f32)
    r = lax.rsqrt(jnp.mean(x * x, -1, keepdims=True) + EPSILON)
    a = (x * r * gain_ref[...].astype(f32)).astype(bf16)
    a_ref[...] = a
    cos, sin = cos_ref[...], sin_ref[...]
    k = jnp.dot(a, wk_ref[...], preferred_element_type=f32)
    k_ref[...] = rope_wide(k, cos, sin).astype(bf16)
    v = jnp.dot(a, wv_ref[...], preferred_element_type=f32).astype(bf16)
    v_ref[:, :128] = v
    v_ref[:, 128:] = jnp.ones_like(v)
    low = lanes(k.shape) < HD
    for pair in range(2):
        q = jnp.dot(a, wq_ref[:, pair * 128 : pair * 128 + 128], preferred_element_type=f32)
        q = rope_wide(q, cos, sin) * HD ** (-0.5)
        other = pltpu.roll(q, HD, 1)
        mine = low if pair == 0 else ~low
        first, second = (q, other) if pair == 0 else (other, q)
        q_ref[2 * pair] = jnp.where(mine, first, 0.0).astype(bf16)
        q_ref[2 * pair + 1] = jnp.where(mine, second, 0.0).astype(bf16)

def project(tokens, gain, wq, wk, wv, cos, sin):
    L, D = tokens.shape
    B = 256
    full = lambda a: pl.BlockSpec(a.shape, lambda i: (0,) * a.ndim)
    rows = lambda w: pl.BlockSpec((B, w), lambda i: (i, 0))
    return pl.pallas_call(
        project_kernel, grid=(L // B,),
        in_specs=[rows(D), full(gain), full(wq), full(wk), full(wv), rows(128), rows(128)],
        out_specs=[rows(D), pl.BlockSpec((4, B, 128), lambda i: (0, i, 0)), rows(128), rows(256)],
        out_shape=[jax.ShapeDtypeStruct((L, D), bf16), jax.ShapeDtypeStruct((4, L, 128), bf16),
                   jax.ShapeDtypeStruct((L, 128), bf16), jax.ShapeDtypeStruct((L, 256), bf16)],
        compiler_params=pltpu.CompilerParams(vmem_limit_bytes=40 << 20),
        cost_estimate=busy(9),
        name="project",
    )(tokens, gain, wq, wk, wv, cos, sin)

def attend_kernel(bq, bk, kv, prefix_ref, q_ref, k_ref, v_ref, *refs):
    o_ref, lse_ref, s_ref = refs[-3:]
    i = pl.program_id(0)
    start = i * bq
    prefix = prefix_ref[0]
    full_blocks = jnp.maximum(start + 1, prefix) // bk
    all_blocks = (jnp.maximum(start + bq, prefix) + bk - 1) // bk
    rows = 2 * bq
    pos = start + lax.broadcasted_iota(jnp.int32, (rows, 1), 0) % bq
    limit = jnp.maximum(pos, prefix - 1)
    low = lanes((bq, 128)) < HD
    q = jnp.concatenate([q_ref[0], q_ref[1]], 0)

    def tile_max(s, peak):
        for c in range(bk // 128):
            peak = jnp.maximum(peak, s[:, c * 128 : c * 128 + 128])
        return peak

    def plain(j, peak):
        off = pl.multiple_of(j * bk, bk)
        s = lax.dot_general(q, k_ref[pl.ds(off, bk), :], NT, preferred_element_type=f32)
        s_ref[:, pl.ds(off, bk)] = s
        return tile_max(s, peak)

    def masked(j, peak):
        off = pl.multiple_of(j * bk, bk)
        s = lax.dot_general(q, k_ref[pl.ds(off, bk), :], NT, preferred_element_type=f32)
        s = jnp.where(lanes((rows, bk)) <= limit - off, s, -1e30)
        s_ref[:, pl.ds(off, bk)] = s
        return tile_max(s, peak)

    peak = jnp.full((rows, 128), -1e30, f32)
    peak = lax.fori_loop(0, full_blocks, plain, peak)
    peak = lax.fori_loop(full_blocks, all_blocks, masked, peak)
    peak = jnp.max(peak, -1, keepdims=True)

    def weigh(j, acc):
        off = pl.multiple_of(j * bk, bk)
        p = jnp.exp(s_ref[:, pl.ds(off, bk)] - peak).astype(bf16)
        return acc + jnp.dot(p, v_ref[pl.ds(off, bk), :], preferred_element_type=f32)

    acc = lax.fori_loop(0, all_blocks, weigh, jnp.zeros((rows, 256), f32))
    total = acc[:, 128:]
    out = acc[:, :128] / total
    one, two = out[:bq], out[bq:]
    if kv == 0:
        merged = jnp.where(low, one, pltpu.roll(two, HD, 1))
    else:
        merged = jnp.where(low, pltpu.roll(one, HD, 1), two)
    o_ref[...] = merged.astype(bf16)
    lse = (peak + jnp.log(total)).T
    lse_ref[0] = lse[:8]


def attend(prefix, q, k, v, kv, bq, bk, before=()):
    L = k.shape[0]
    return pl.pallas_call(
        functools.partial(attend_kernel, bq, bk, kv),
        grid_spec=pltpu.PrefetchScalarGridSpec(
            num_scalar_prefetch=1, grid=(L // bq,),
            in_specs=[pl.BlockSpec((2, bq, 128), lambda i, p: (kv, i, 0)),
                      pl.BlockSpec((L, 128), lambda i, p: (0, 0)),
                      pl.BlockSpec((L, 256), lambda i, p: (0, 0))]
            + [pl.BlockSpec(memory_space=pl.ANY)] * len(before),
            out_specs=[pl.BlockSpec((bq, 128), lambda i, p: (i, kv)),
                       pl.BlockSpec((1, 8, 2 * bq), lambda i, p: (kv, 0, i))],
            scratch_shapes=[pltpu.VMEM((2 * bq, L), f32)]),
        out_shape=[jax.ShapeDtypeStruct((L, 256), bf16), jax.ShapeDtypeStruct((2, 8, 2 * L), f32)],
        input_output_aliases={4 + i: i for i in range(len(before))},
        compiler_params=pltpu.CompilerParams(vmem_limit_bytes=48 << 20),
        cost_estimate=busy(14),
        name="attend",
    )(prefix, q, k, v, *before)


def attend_back_kernel(bq, bk, prefix_ref, q_ref, k_ref, v_ref, o_ref, do_ref, lse_ref, cos_ref, sin_ref, cosa_ref, sina_ref,
                       out_ref, dk_acc, dv_acc):
    i = pl.program_id(0)
    start = i * bq
    prefix = prefix_ref[0]
    full_blocks = jnp.maximum(start + 1, prefix) // bk
    all_blocks = (jnp.maximum(start + bq, prefix) + bk - 1) // bk
    rows = 2 * bq
    pos = start + lax.broadcasted_iota(jnp.int32, (1, rows), 1) % bq
    limit = jnp.maximum(pos, prefix - 1)
    low = lanes((bq, 128)) < HD

    @pl.when(i == 0)
    def _():
        dk_acc[...] = jnp.zeros_like(dk_acc)
        dv_acc[...] = jnp.zeros_like(dv_acc)

    for kv in range(2):
        q = jnp.concatenate([q_ref[2 * kv], q_ref[2 * kv + 1]], 0)
        mine = low if kv == 0 else ~low
        pair = do_ref[:, kv * 128 : kv * 128 + 128].astype(f32)
        swap = pltpu.roll(pair, HD, 1)
        first, second = (pair, swap) if kv == 0 else (swap, pair)
        do = jnp.concatenate([jnp.where(mine, first, 0.0), jnp.where(mine, second, 0.0)], 0).astype(bf16)
        prod = pair * o_ref[:, kv * 128 : kv * 128 + 128].astype(f32)
        one = jnp.sum(jnp.where(low, prod, 0.0), -1, keepdims=True)
        two = jnp.sum(jnp.where(low, 0.0, prod), -1, keepdims=True)
        center = jnp.broadcast_to(jnp.concatenate([one, two], 0), (rows, 128)).T[:1]
        lse = lse_ref[kv, :1, :]

        def step(j, dq, mask):
            off = pl.multiple_of(j * bk, bk)
            kb = k_ref[pl.ds(off, bk), :]
            s = lax.dot_general(kb, q, NT, preferred_element_type=f32)
            if mask:
                s = jnp.where(off + lax.broadcasted_iota(jnp.int32, (bk, rows), 0) <= limit, s, -1e30)
            p = jnp.exp(s - lse)
            dp = lax.dot_general(v_ref[pl.ds(off, bk), :128], do, NT, preferred_element_type=f32)
            ds = (p * (dp - center)).astype(bf16)
            dv_acc[pl.ds(off, bk), :] += jnp.dot(p.astype(bf16), do, preferred_element_type=f32)
            dk_acc[pl.ds(off, bk), :] += jnp.dot(ds, q, preferred_element_type=f32)
            return dq + lax.dot_general(ds, kb, TN, preferred_element_type=f32)

        dq = jnp.zeros((rows, 128), f32)
        dq = lax.fori_loop(0, full_blocks, functools.partial(step, mask=False), dq)
        dq = lax.fori_loop(full_blocks, all_blocks, functools.partial(step, mask=True), dq)
        dq = dq * HD ** (-0.5)
        one, two = dq[:bq], dq[bq:]
        if kv == 0:
            merged = jnp.where(low, one, pltpu.roll(two, HD, 1))
        else:
            merged = jnp.where(low, pltpu.roll(one, HD, 1), two)
        out_ref[pl.ds(pl.multiple_of(start, bq), bq), kv * 128 : kv * 128 + 128] = rope_wide(merged, cos_ref[...], -sin_ref[...]).astype(bf16)

    @pl.when(i == pl.num_programs(0) - 1)
    def _():
        for b in range(dk_acc.shape[0] // bq):
            r = pl.ds(b * bq, bq)
            out_ref[r, 256:384] = rope_wide(dk_acc[r, :], cosa_ref[r, :], -sina_ref[r, :]).astype(bf16)
            out_ref[r, 384:] = dv_acc[r, :].astype(bf16)

def attend_back(prefix, q, k, v, o, do, lse, cos, sin, bq=256, bk=256):
    L = k.shape[0]
    fullL = pl.BlockSpec((L, 128), lambda i, p: (0, 0))
    return pl.pallas_call(
        functools.partial(attend_back_kernel, bq, bk),
        grid_spec=pltpu.PrefetchScalarGridSpec(
            num_scalar_prefetch=1, grid=(L // bq,),
            in_specs=[pl.BlockSpec((4, bq, 128), lambda i, p: (0, i, 0)), fullL,
                      pl.BlockSpec((L, 256), lambda i, p: (0, 0)),
                      pl.BlockSpec((bq, 256), lambda i, p: (i, 0)),
                      pl.BlockSpec((bq, 256), lambda i, p: (i, 0)),
                      pl.BlockSpec((2, 8, 2 * bq), lambda i, p: (0, 0, i)),
                      pl.BlockSpec((bq, 128), lambda i, p: (i, 0)),
                      pl.BlockSpec((bq, 128), lambda i, p: (i, 0)), fullL, fullL],
            out_specs=pl.BlockSpec((L, 512), lambda i, p: (0, 0)),
            scratch_shapes=[pltpu.VMEM((L, 128), f32), pltpu.VMEM((L, 128), f32)]),
        out_shape=jax.ShapeDtypeStruct((L, 512), bf16),
        compiler_params=pltpu.CompilerParams(vmem_limit_bytes=48 << 20),
        cost_estimate=busy(46),
        name="attend_back",
    )(prefix, q, k, v, o, do, lse, cos, sin, cos, sin)


def pick_kernel(experts, per, cap, pairs, shift_ref, *refs):
    in_ref, dyo_ref, gs_ref, gate_ref, code_ref, code_t, gate_t, rows_s, dy_s = refs[-9:]
    tokens, width = rows_s.shape

    @pl.when(pl.program_id(0) == 0)
    def _():
        if pairs:
            rows_ref, rows_other, side_ref, side_other, router_ref = refs[:5]
            first = shift_ref[experts] != 0
            rows = jnp.where(first, rows_ref[...], rows_other[...])
            side = jnp.where(first, side_ref[...], side_other[...])
        else:
            rows_ref, side_ref, router_ref = refs[:3]
            rows, side = rows_ref[...], side_ref[...]
        rows_s[...] = rows
        dy_s[...] = side[:, :width]
        code = side[:, width:].astype(f32)
        code_ref[...] = code
        logits = jnp.dot(rows, router_ref[...], preferred_element_type=f32)
        chosen = jnp.where(code >= 0, logits, -1e30)
        raised = jnp.where(code >= 0, jnp.exp(chosen - jnp.max(chosen, -1, keepdims=True)), 0.0)
        gate = raised / jnp.sum(raised, -1, keepdims=True)
        gate_ref[...] = gate
        gate_t[...] = gate.T
        code_t[...] = code.T

    hots = []
    for e in range(per):
        row = pl.ds(shift_ref[pl.program_id(0) * per + e], 1)
        hot = code_t[row, :] == lax.broadcasted_iota(jnp.int32, (cap, tokens), 0).astype(f32)
        gs = jnp.sum(jnp.where(hot, gate_t[row, :], 0.0), -1, keepdims=True)
        gs_ref[e] = jnp.broadcast_to(gs, (cap, 128))
        hots.append(hot.astype(bf16))
    hot = jnp.concatenate(hots, 0)
    in_ref[...] = jnp.dot(hot, rows_s[...], preferred_element_type=f32).astype(bf16).reshape(in_ref.shape)
    dyo_ref[...] = jnp.dot(hot, dy_s[...], preferred_element_type=f32).astype(bf16).reshape(dyo_ref.shape)


def pick(shift, rows, sides, router, cap):
    R, D = rows[0].shape
    E = shift.shape[0] - 1
    W = router.shape[1]
    per = 2
    operands = [*rows, *sides, router]
    whole = lambda a: pl.BlockSpec(a.shape, lambda e: (0, 0))
    some = lambda w: pl.BlockSpec((per, cap, w), lambda e: (e, 0, 0))
    wide = pl.BlockSpec((R, W), lambda e: (0, 0))
    return pl.pallas_call(
        functools.partial(pick_kernel, E, per, cap, len(rows) == 2),
        grid=(E // per,),
        in_specs=[pl.BlockSpec(memory_space=pltpu.SMEM)] + [whole(a) for a in operands],
        out_specs=[some(D), some(D), some(128), wide, wide],
        out_shape=[pltpu.HBM((E, cap, D), bf16), pltpu.HBM((E, cap, D), bf16),
                   pltpu.HBM((E, cap, 128), f32), jax.ShapeDtypeStruct((R, W), f32), jax.ShapeDtypeStruct((R, W), f32)],
        scratch_shapes=[pltpu.VMEM((W, R), f32), pltpu.VMEM((W, R), f32), pltpu.VMEM((R, D), bf16), pltpu.VMEM((R, D), bf16)],
        compiler_params=pltpu.CompilerParams(vmem_limit_bytes=40 << 20),
        cost_estimate=busy(4),
        name="pick",
    )(shift, *operands)


def ffn_kernel(n, blocks, *refs):
    rows_refs, dy_refs, gs_refs = refs[:n], refs[n : 2 * n], refs[2 * n : 3 * n]
    w_ref, eout_ref, drows_ref, dgs_ref, act_ref, dgu_ref = refs[3 * n :]
    cap, D = rows_refs[0].shape[1:]
    M = n * cap
    rows = jnp.concatenate([r[0] for r in rows_refs], 0)
    dy = jnp.concatenate([r[0] for r in dy_refs], 0)
    gs = jnp.concatenate([r[0] for r in gs_refs], 0)
    dout = (dy.astype(f32) * gs[:, :1]).astype(bf16)
    F = w_ref.shape[-1]
    eout = jnp.zeros((M, D), f32)
    drows = jnp.zeros((M, D), f32)
    for pair in range(0, blocks, 2):
        acts = []
        wd2 = jnp.concatenate([w_ref[0, pair, 2, 0], w_ref[0, pair + 1, 2, 0]], 1)
        dact2 = jnp.dot(dout, wd2, preferred_element_type=f32)
        for b in (pair, pair + 1):
            w = jnp.concatenate([w_ref[0, b, 0, 0], w_ref[0, b, 1, 0]], 1)
            gu = jnp.dot(rows, w, preferred_element_type=f32)
            g, u = gu[:, :F], gu[:, F:]
            sg = 1.0 / (1.0 + jnp.exp(-g))
            gsg = g * sg
            acts.append((gsg * u).astype(bf16))
            dact = dact2[:, (b - pair) * F : (b - pair + 1) * F]
            dg = dact * u * (sg + gsg * (1.0 - sg))
            du = dact * gsg
            dgu = jnp.concatenate([dg, du], 1).astype(bf16)
            dgu_ref[0, :, b * 2 * F : (b + 1) * 2 * F] = dgu
            drows = drows + lax.dot_general(dgu, w, NT, preferred_element_type=f32)
        act = jnp.concatenate(acts, 1)
        act_ref[0, :, pair * F : (pair + 2) * F] = act
        eout = eout + lax.dot_general(act, wd2, NT, preferred_element_type=f32)
    eout = eout.astype(bf16)
    eout_ref[0] = eout
    drows_ref[0] = drows.astype(bf16)
    dgs = jnp.sum(dy.astype(f32) * eout.astype(f32), -1, keepdims=True)
    dgs_ref[0] = jnp.broadcast_to(dgs, (M, 128))


def ffn(picked, weights):
    n = len(picked)
    total, cap, D = picked[0][0].shape
    groups, blocks, _, E, _, F = weights.shape
    H = blocks * F
    M = n * cap
    spec = lambda w: pl.BlockSpec((1, cap, w), lambda e: (e, 0, 0))
    outs = lambda w: pl.BlockSpec((1, M, w), lambda e: (e, 0, 0))
    wsp = pl.BlockSpec((1, blocks, 3, 1, D, F), lambda e: (e // E, 0, 0, e % E, 0, 0))
    sh = lambda w, t: jax.ShapeDtypeStruct((total, M, w), t)
    return pl.pallas_call(
        functools.partial(ffn_kernel, n, blocks), grid=(total,),
        in_specs=[spec(D)] * (2 * n) + [spec(128)] * n + [wsp],
        out_specs=[outs(D), outs(D), outs(128), outs(H), outs(2 * H)],
        out_shape=[sh(D, bf16), sh(D, bf16), sh(128, f32), sh(H, bf16), sh(2 * H, bf16)],
        compiler_params=pltpu.CompilerParams(vmem_limit_bytes=56 << 20),
        cost_estimate=busy(40),
        name="ffn",
    )(*[p[i] for i in range(3) for p in picked], weights)


def wgrad_kernel(n, blocks, *refs):
    rows_refs, dy_refs, gs_refs = refs[:n], refs[n : 2 * n], refs[2 * n : 3 * n]
    act_ref, dgu_ref, out_ref = refs[3 * n :]
    rows = jnp.concatenate([r[0] for r in rows_refs], 0)
    dy = jnp.concatenate([r[0] for r in dy_refs], 0)
    gs = jnp.concatenate([r[0] for r in gs_refs], 0)
    dout = (dy.astype(f32) * gs[:, :1]).astype(bf16)
    F = act_ref.shape[2] // blocks
    for b in range(blocks):
        dgu = dgu_ref[0, :, b * 2 * F : (b + 1) * 2 * F]
        g = lax.dot_general(rows, dgu, TN, preferred_element_type=f32).astype(bf16)
        out_ref[0, b, 0, 0] = g[:, :F]
        out_ref[0, b, 1, 0] = g[:, F:]
    for pair in range(0, blocks, 2):
        gd = lax.dot_general(dout, act_ref[0, :, pair * F : (pair + 2) * F], TN, preferred_element_type=f32).astype(bf16)
        out_ref[0, pair, 2, 0] = gd[:, :F]
        out_ref[0, pair + 1, 2, 0] = gd[:, F:]


def wgrad(picked, act, dgu, blocks, groups):
    n = len(picked)
    total, cap, D = picked[0][0].shape
    M, H = act.shape[1:]
    F = H // blocks
    E = total // groups
    spec = lambda w: pl.BlockSpec((1, cap, w), lambda e: (e, 0, 0))
    wide = lambda w: pl.BlockSpec((1, M, w), lambda e: (e, 0, 0))
    return pl.pallas_call(
        functools.partial(wgrad_kernel, n, blocks),
        grid=(total,),
        in_specs=[spec(D)] * (2 * n) + [spec(128)] * n + [wide(H), wide(2 * H)],
        out_specs=pl.BlockSpec((1, blocks, 3, 1, D, F), lambda e: (e // E, 0, 0, e % E, 0, 0)),
        out_shape=jax.ShapeDtypeStruct((groups, blocks, 3, E, D, F), bf16),
        compiler_params=pltpu.CompilerParams(vmem_limit_bytes=56 << 20),
        cost_estimate=busy(26),
        name="wgrad",
    )(*[p[i] for i in range(3) for p in picked], act, dgu)


def hot_columns(code, shift, cap):
    col = jnp.sum(jnp.where(lanes(code.shape) == shift, code, 0.0), -1, keepdims=True)
    return col == lanes((code.shape[0], cap)).astype(f32)


def merge_back_kernel(n, E, cap, shift_ref, *refs):
    sides, (d_ref, g_ref), outs = refs[:n], refs[n : n + 2], refs[n + 2 :]
    D = d_ref.shape[2]
    lane = lanes((cap, 128))
    for source in range(n):

        @pl.when(pl.program_id(0) == source)
        def _():
            code = sides[source][...]
            total = jnp.zeros((code.shape[0], D), f32)
            gates = jnp.zeros((code.shape[0], 128), f32)
            for e0 in range(0, E, 4):
                some = range(e0, min(e0 + 4, E))
                hot = jnp.concatenate([hot_columns(code, shift_ref[e], cap).astype(bf16) for e in some], 1)
                rows = jnp.concatenate([d_ref[e] for e in some], 0)
                side = jnp.concatenate([jnp.where(lane == shift_ref[e], g_ref[e], 0.0).astype(bf16) for e in some], 0)
                total = total + jnp.dot(hot, rows, preferred_element_type=f32)
                gates = gates + jnp.dot(hot, side, preferred_element_type=f32)
            outs[source][:, :D] = total.astype(bf16)
            outs[source][:, D:] = gates.astype(bf16)


def merge_back(shift, codes, first, drows, dgs, cap):
    n = len(codes)
    R, W = codes[0].shape
    E, _, D = drows.shape
    part = lambda w: pl.BlockSpec((E, cap, w), lambda i: (0, i + first, 0))
    whole = lambda w: pl.BlockSpec((R, w), lambda i: (0, 0))
    return pl.pallas_call(
        functools.partial(merge_back_kernel, n, E, cap),
        grid=(n,),
        in_specs=[pl.BlockSpec(memory_space=pltpu.SMEM)] + [whole(W)] * n + [part(D), part(128)],
        out_specs=[whole(D + 128)] * n,
        out_shape=[jax.ShapeDtypeStruct((R, D + 128), bf16)] * n,
        compiler_params=pltpu.CompilerParams(vmem_limit_bytes=48 << 20),
        cost_estimate=busy(3 * n),
        name="merge_back",
    )(shift, *codes, drows, dgs)


def merge_out_kernel(n, E, cap, shift_ref, *refs):
    sides, gates, e_ref, outs = refs[:n], refs[n : 2 * n], refs[2 * n], refs[2 * n + 1 :]
    D = e_ref.shape[2]
    for source in range(n):

        @pl.when(pl.program_id(0) == source)
        def _():
            code = sides[source][...]
            gate = gates[source][...]
            total = jnp.zeros((code.shape[0], D), f32)
            for e0 in range(0, E, 4):
                some = range(e0, min(e0 + 4, E))
                parts = []
                for e in some:
                    g = jnp.sum(jnp.where(lanes(gate.shape) == shift_ref[e], gate, 0.0), -1, keepdims=True)
                    parts.append(jnp.where(hot_columns(code, shift_ref[e], cap), g, 0.0).astype(bf16))
                rows = jnp.concatenate([e_ref[e] for e in some], 0)
                total = total + jnp.dot(jnp.concatenate(parts, 1), rows, preferred_element_type=f32)
            outs[source][...] = total.astype(bf16)


def merge_out(shift, codes, gates, eout, cap):
    n = len(codes)
    R, W = codes[0].shape
    E, _, D = eout.shape
    whole = lambda w: pl.BlockSpec((R, w), lambda i: (0, 0))
    return pl.pallas_call(
        functools.partial(merge_out_kernel, n, E, cap),
        grid=(n,),
        in_specs=[pl.BlockSpec(memory_space=pltpu.SMEM)] + [whole(W)] * (2 * n)
        + [pl.BlockSpec((E, cap, D), lambda i: (0, i, 0))],
        out_specs=[whole(D)] * n,
        out_shape=[jax.ShapeDtypeStruct((R, D), bf16)] * n,
        compiler_params=pltpu.CompilerParams(vmem_limit_bytes=48 << 20),
        cost_estimate=busy(11),
        name="merge_out",
    )(shift, *codes, *gates, eout)


def finish_kernel(core_ref, sum_ref, x_ref, dh_ref, gain_ref, *refs):
    out_ref = refs[-1]
    x = x_ref[...].astype(f32)
    r = lax.rsqrt(jnp.mean(x * x, -1, keepdims=True) + EPSILON)
    scaled = sum_ref[...].astype(f32) * gain_ref[...].astype(f32)
    out_ref[...] = dh_ref[...].astype(f32) + r * scaled - x * (r * r * r * jnp.mean(scaled * x, -1, keepdims=True))


def finish(core, summed, tokens, hidden, gain, rows, before=()):
    L, D = tokens.shape
    half = rows // 2
    place = lambda i, p: ((i // 2) * 4 + p[0] * 2 + i % 2, 0)
    return pl.pallas_call(
        finish_kernel,
        grid_spec=pltpu.PrefetchScalarGridSpec(
            num_scalar_prefetch=1, grid=(L // rows,),
            in_specs=[pl.BlockSpec((half, D), lambda i, p: (i, 0)), pl.BlockSpec((half, D), place), pl.BlockSpec((half, D), place),
                      pl.BlockSpec((1, D), lambda i, p: (0, 0))] + [pl.BlockSpec(memory_space=pl.ANY)] * len(before),
            out_specs=pl.BlockSpec((half, D), place)),
        out_shape=jax.ShapeDtypeStruct((L, D), f32),
        input_output_aliases={5 + i: i for i in range(len(before))},
        compiler_params=pltpu.CompilerParams(vmem_limit_bytes=48 << 20),
        cost_estimate=busy(4),
        name="finish",
    )(core, summed, tokens, hidden, gain, *before)


def spread_kernel(n, more, rank_ref, att_ref, w_ref, *refs):
    blocks = refs[:n]
    hidden_ref, do_ref, og_ref = refs[-3:]
    i = pl.program_id(0)

    @pl.when(i == 0)
    def _():
        og_ref[...] = refs[n][...] if more else jnp.zeros_like(og_ref)

    for b in range(n):

        @pl.when(i == b)
        def _():
            block = blocks[b][...]
            hidden_ref[...] = block
            do_ref[...] = lax.dot_general(block, w_ref[...], NT, preferred_element_type=f32).astype(bf16)
            og_ref[...] += lax.dot_general(att_ref[...], block, TN, preferred_element_type=f32)


def spread(rank, first, blocks, attended, w_out, before=None):
    n = len(blocks)
    R, D = blocks[0].shape
    L, H = attended.shape
    place = lambda i, p: (p[0] ^ (i + first), 0)
    whole = lambda a: pl.BlockSpec(a.shape, lambda i, p: (0, 0))
    total = jax.ShapeDtypeStruct((H, D), f32)
    operands = [attended, w_out, *blocks]
    specs = [pl.BlockSpec((R, H), place), whole(w_out)] + [whole(b) for b in blocks]
    aliases = {}
    if before is not None:
        hidden, do, og = before
        operands += [og, hidden, do]
        specs += [whole(og)] + [pl.BlockSpec(memory_space=pl.ANY)] * 2
        aliases = {len(operands) - 1: 0, len(operands): 1}
    return pl.pallas_call(
        functools.partial(spread_kernel, n, before is not None),
        grid_spec=pltpu.PrefetchScalarGridSpec(
            num_scalar_prefetch=1, grid=(n,), in_specs=specs,
            out_specs=[pl.BlockSpec((R, D), place), pl.BlockSpec((R, H), place), whole(total)]),
        out_shape=[pltpu.HBM((L, D), bf16), pltpu.HBM((L, H), bf16), total],
        input_output_aliases=aliases,
        compiler_params=pltpu.CompilerParams(vmem_limit_bytes=32 << 20),
        cost_estimate=busy(3),
        name="spread",
    )(rank, *operands)


def swap(x, axis, bit=1):
    count = lax.axis_size(axis)
    return lax.ppermute(x, axis, [(i, i ^ bit) for i in range(count)])


def total_over(x, axes):
    for axis in axes:
        bit = 1
        while bit < lax.axis_size(axis):
            x = x + swap(x, axis, bit)
            bit *= 2
    return x


def wide_tables(length):
    half = HD // 2
    angles = np.arange(length)[:, None] * THETA_BASE ** (-(np.arange(half) / half))[None, :]
    cos, sin = np.cos(angles), np.sin(angles)
    return (
        jnp.asarray(np.concatenate([cos, cos, cos, cos], 1), f32),
        jnp.asarray(np.concatenate([-sin, sin, -sin, sin], 1), f32),
    )


NEAR = [(0, 1), (1, 0), (2, 3), (3, 2)]
MIDDLE = [(1, 2), (2, 1)]
TO_ENDS = [(1, 0), (2, 3)]
FROM_ENDS = [(0, 1), (3, 2)]


def line_first(x):
    return lax.ppermute(x, "z", NEAR), lax.ppermute(x, "z", MIDDLE)


def line_second(near, across):
    return lax.ppermute(near, "z", MIDDLE), lax.ppermute(across, "z", TO_ENDS)


def line_third(across_far):
    return lax.ppermute(across_far, "z", TO_ENDS)


def hold(*arrays):
    return lax.optimization_barrier(arrays)


def line_out(parts):
    return lax.ppermute(parts[3], "z", FROM_ENDS), lax.ppermute(parts[2], "z", FROM_ENDS)


def add_low(a, b):
    return (a.astype(f32) + b.astype(f32)).astype(a.dtype)


def line_over(part, from_end):
    return lax.ppermute(add_low(part, from_end), "z", MIDDLE)


def line_in(part, across_far):
    return lax.ppermute(add_low(part, across_far), "z", NEAR)


def line_sum(parts, from_end_far, from_end):
    own, near, two, three = parts
    across_far = line_over(two, from_end_far)
    across = line_over(three, from_end)
    got = line_in(near, across_far)
    return own.astype(f32) + across.astype(f32) + got.astype(f32)


def per_device_fast(
    tokens,
    prefix,
    gain_attn,
    w_query,
    w_key,
    w_value,
    w_out,
    gain_moe,
    w_router,
    routes,
    fill_order,
    w_gate,
    w_up,
    w_down,
    cotangent,
):
    z, y, x, c = (lax.axis_index(a) for a in ("z", "y", "x", "c"))
    shards = lax.axis_size("x") * lax.axis_size("c")
    groups = lax.axis_size("y")
    rank = x * lax.axis_size("c") + c
    at_end = (z == 0) | (z == lax.axis_size("z") - 1)
    length, width = tokens.shape
    own_rows = routes.shape[0]
    local = w_gate.shape[0]
    cap = own_rows * TOPK // EXPERTS

    expert_ids = jnp.arange(EXPERTS, dtype=jnp.int32)
    member = jnp.sum((routes[:, :, None] == expert_ids[None, None, :]).astype(f32), 1)
    priority = fill_order[0]
    earlier = (priority[None, :] < priority[:, None]).astype(bf16)
    slot_full = jnp.dot(earlier, member.astype(bf16), preferred_element_type=f32)
    code = jnp.where(member > 0, jnp.minimum(slot_full, float(cap)), -1.0).astype(bf16)
    code = jnp.pad(code, ((0, 0), (0, 128 - EXPERTS)), constant_values=-1)
    side_own = jnp.concatenate([cotangent, code], 1)
    side_near, side_across = line_first(side_own)
    router_wide = jnp.pad(w_router, ((0, 0), (0, 128 - EXPERTS)))
    shift = z * groups * local + jnp.arange(groups * local, dtype=jnp.int32)
    shift_end = jnp.concatenate([shift, at_end.astype(jnp.int32)[None]])

    own_weights = jnp.stack([w_gate, w_up, w_down.transpose(0, 2, 1)])
    weights = lax.all_gather(own_weights, ("y", "x", "c"), axis=0, tiled=False)
    weights = weights.reshape((groups, shards) + own_weights.shape)

    cos, sin = wide_tables(length)
    normed_one, query, key, value = project(tokens, gain_attn[None], w_query, w_key, w_value, cos, sin)
    first_half = attend(prefix, query, key, value, 0, BQ, BK)
    *first_half, side_near, side_across = hold(*first_half, side_near, side_across)
    side_far, side_relay = line_second(side_near, side_across)
    attended, log_total = attend(prefix, query, key, value, 1, BQ, BK, first_half)
    attended, side_far = hold(attended, side_far)
    side_last = line_third(side_far)


    def out_block(place):
        rows = lax.dynamic_slice_in_dim(attended, place * own_rows, own_rows, 0)
        return jnp.dot(rows, w_out, preferred_element_type=f32)

    far_sum = out_block(rank ^ 2) + swap(out_block(rank ^ 3).astype(bf16), "c").astype(f32)
    far_got = swap(far_sum.astype(bf16), "x").astype(f32)
    near_got = swap(out_block(rank ^ 1).astype(bf16), "c").astype(f32)
    x_rows = lax.dynamic_slice_in_dim(tokens, rank * own_rows, own_rows, 0).astype(f32)
    hidden_in = x_rows + out_block(rank) + near_got + far_got
    rms_two = lax.rsqrt(jnp.mean(hidden_in * hidden_in, -1, keepdims=True) + EPSILON)
    gain_two = gain_moe.astype(f32)
    normed_two = (hidden_in * rms_two * gain_two).astype(bf16)

    near, across = line_first(normed_two)
    near, across, side_last = hold(near, across, side_last)
    far, relay = line_second(near, across)
    last = line_third(far)
    picked = [
        pick(shift_end, rows, sides, router_wide, cap)
        for rows, sides in (
            ((normed_two,), (side_own,)),
            ((near,), (side_near,)),
            ((relay, far), (side_relay, side_far)),
            ((last, across), (side_last, side_across)),
        )
    ]
    gates = [p[3] for p in picked]
    codes = [p[4] for p in picked]
    expert_out, rows_grad, gate_slots, act, hidden_grads = ffn(picked, weights)
    far_back = merge_back(shift, codes[2:], 2, rows_grad, gate_slots, cap)
    late_grad, *far_back = hold(rows_grad, *far_back)
    back = [*merge_back(shift, codes[:2], 0, late_grad, gate_slots, cap), *far_back]
    back_out = line_out(back)
    late_act, *_ = hold(act, *back)
    parts = wgrad(picked, late_act, hidden_grads, shards, groups)
    back_far_out, parts = hold(back_out[0], parts)
    back_out = (back_far_out, back_out[1])
    back_own = line_sum(back, *back_out)
    part_sum = lax.psum_scatter(
        parts.reshape((groups * shards,) + parts.shape[2:]), ("y", "x", "c"), scatter_dimension=0, tiled=False
    )

    gate_own = gates[0]
    gate_grad = back_own[:, width:]
    logit_grad = gate_own * (gate_grad - jnp.sum(gate_own * gate_grad, -1, keepdims=True))
    logit_low = logit_grad.astype(bf16)
    normed_two_grad = back_own[:, :width] + lax.dot_general(
        logit_low, router_wide, (((1,), (1,)), ((), ())), preferred_element_type=f32
    )
    router_part = lax.dot_general(
        logit_low, normed_two, (((0,), (0,)), ((), ())), preferred_element_type=f32
    )[:EXPERTS]
    gain_two_part = jnp.sum(normed_two_grad * hidden_in * rms_two, 0)
    scaled_two = normed_two_grad * gain_two
    hidden_grad = (
        cotangent.astype(f32)
        + rms_two * scaled_two
        - hidden_in * rms_two**3 * jnp.mean(scaled_two * hidden_in, -1, keepdims=True)
    ).astype(bf16)
    small = jnp.concatenate([router_part, gain_two_part[None], jnp.zeros((7, width), f32)], 0)
    small = total_over(small.reshape(-1, width // 2).astype(bf16), ("c", "x"))
    hidden_over_x = swap(hidden_grad, "x")
    late_out, *_ = hold(expert_out, hidden_grad)
    out_parts = merge_out(shift, codes, gates, late_out, cap)
    hidden_over_x, *out_parts = hold(hidden_over_x, *out_parts)
    out_end_far, out_end = line_out(out_parts)
    rank_row = rank.astype(jnp.int32)[None]
    near_done = spread(rank_row, 0, [hidden_grad, swap(hidden_grad, "c")], attended, w_out)
    hidden_over_x, *near_done = hold(hidden_over_x, *near_done)
    hidden_all, attended_grad, out_grad = spread(
        rank_row, 2, [hidden_over_x, swap(hidden_over_x, "c")], attended, w_out, near_done
    )
    attended_grad, small, out_low, out_end_far = hold(attended_grad, small, out_grad.astype(bf16), out_end_far)
    out_far = line_over(out_parts[2], out_end_far)
    heads_back = attend_back(
        prefix, query, key, value, attended, attended_grad, log_total, cos, sin, BQ, BK_BACK
    )
    heads_in = jnp.concatenate([w_query, w_key, w_value], 1)
    heads_grad = jnp.einsum("id,ih->dh", normed_one, heads_back, preferred_element_type=f32)
    low = jnp.concatenate([heads_grad.astype(bf16), out_low.reshape(-1, heads_grad.shape[1]), small], 0)
    heads_back, low, part_sum, out_far, out_end = hold(heads_back, low, part_sum, out_far, out_end)

    low_all = lax.psum(low, ("z", "y"))

    out_across = line_over(out_parts[3], out_end)
    out_got = line_in(out_parts[1], out_far)
    moe_own = out_parts[0].astype(f32) + out_across.astype(f32) + out_got.astype(f32)
    block_output = (hidden_in + moe_own).astype(bf16)

    by_core = heads_back.reshape(shards // 2, 2, own_rows, -1)

    def rows_of(which):
        rows = lax.dynamic_index_in_dim(by_core, which, 1, keepdims=False)
        return lax.dot_general(rows, heads_in, (((2,), (1,)), ((), ())), preferred_element_type=f32)

    from_core = swap(rows_of(1 - c).astype(bf16), "c")
    core_sum = (rows_of(c) + from_core.astype(f32)).astype(bf16)
    chip_sum = (core_sum.astype(f32) + swap(core_sum, "x").astype(f32)).astype(bf16)
    chip_sum, low_all = hold(chip_sum, low_all)
    other_sum = swap(chip_sum, "c")
    core = c.astype(jnp.int32)[None]
    gain_row = gain_attn[None]
    input_grad = finish(core, chip_sum.reshape(-1, width), tokens, hidden_all, gain_row, own_rows)
    other_sum, input_grad = hold(other_sum, input_grad)
    input_grad = finish(
        1 - core, other_sum.reshape(-1, width), tokens, hidden_all, gain_row, own_rows, (input_grad,)
    )
    low_all = low_all.astype(f32)
    split = width + out_grad.size // low.shape[1]
    heads_total = low_all[:width]
    out_total = low_all[width:split].reshape(out_grad.shape)
    small_total = low_all[split:].reshape(-1, width)
    gain_one_part = jnp.sum(heads_total * heads_in.astype(f32), 1) / gain_attn.astype(f32)
    gain_one_total = total_over(gain_one_part.reshape(8, -1), ("c", "x")).reshape(-1)
    cut = w_query.shape[1]
    return (
        block_output,
        input_grad,
        gain_one_total,
        heads_total[:, :cut],
        heads_total[:, cut : cut + w_key.shape[1]],
        heads_total[:, cut + w_key.shape[1] :],
        out_total,
        small_total[EXPERTS],
        small_total[:EXPERTS].T,
        part_sum[0].astype(f32),
        part_sum[1].astype(f32),
        part_sum[2].astype(f32).transpose(0, 2, 1),
    )


def group_gather(x, axes):
    return lax.all_gather(x, axes, axis=0, tiled=False)


def per_device_general(
    tokens,
    prefix,
    gain_attn,
    w_query,
    w_key,
    w_value,
    w_out,
    gain_moe,
    w_router,
    routes,
    fill_order,
    w_gate,
    w_up,
    w_down,
    cotangent,
):
    f32 = jnp.float32
    bf16 = jnp.bfloat16
    z_count = lax.axis_size("z")
    y_count = lax.axis_size("y")
    shards = lax.axis_size("x") * lax.axis_size("c")
    z_rank = lax.axis_index("z")
    tensor_rank = lax.axis_index("x") * lax.axis_size("c") + lax.axis_index("c")
    length = tokens.shape[0]
    model_width = tokens.shape[1]
    own_rows = routes.shape[0]
    local_experts = w_gate.shape[0]
    group_experts = local_experts * y_count
    capacity = own_rows * TOPK // EXPERTS
    heads_local = w_query.shape[1] // HD
    kv_local = w_key.shape[1] // HD
    group_size = heads_local // kv_local
    block_rows = min(512, length)
    block_count = length // block_rows
    score_scale = HD ** (-0.5)
    hidden = w_gate.shape[2] * shards

    expert_ids = jnp.arange(EXPERTS, dtype=jnp.int32)
    member = jnp.sum((routes[:, :, None] == expert_ids[None, None, :]).astype(f32), 1)
    priority = fill_order[0]
    earlier = (priority[None, :] < priority[:, None]).astype(bf16)
    slot_full = jnp.dot(earlier, member.astype(bf16), preferred_element_type=f32)
    slot_code = jnp.where(member > 0, jnp.minimum(slot_full, float(capacity)), -1.0).astype(bf16)

    weights_gate = group_gather(w_gate, ("y", "x", "c")).reshape(
        y_count, shards, local_experts, model_width, -1
    )
    weights_up = group_gather(w_up, ("y", "x", "c")).reshape(
        y_count, shards, local_experts, model_width, -1
    )
    weights_down = group_gather(w_down, ("y", "x", "c")).reshape(
        y_count, shards, local_experts, -1, model_width
    )
    weights_gate = weights_gate.transpose(0, 2, 3, 1, 4).reshape(group_experts, model_width, hidden)
    weights_up = weights_up.transpose(0, 2, 3, 1, 4).reshape(group_experts, model_width, hidden)
    weights_down = weights_down.transpose(0, 2, 1, 3, 4).reshape(group_experts, hidden, model_width)
    cot_all = lax.all_gather(cotangent, "z", axis=0, tiled=False)
    code_all = lax.all_gather(slot_code, "z", axis=0, tiled=False)

    x_full = tokens.astype(f32)
    rms_one = lax.rsqrt(jnp.mean(x_full * x_full, -1, keepdims=True) + EPSILON)
    gain_one = gain_attn.astype(f32)
    normed_one = (x_full * rms_one * gain_one).astype(bf16)
    query_raw = jnp.dot(normed_one, w_query, preferred_element_type=f32)
    key_raw = jnp.dot(normed_one, w_key, preferred_element_type=f32)
    values = (
        jnp.dot(normed_one, w_value, preferred_element_type=f32)
        .astype(bf16)
        .reshape(length, kv_local, HD)
    )
    cosine, sine = rope_tables(length, HD)
    query_rot = rotate(query_raw.reshape(length, heads_local, HD), cosine, sine, 1.0).astype(bf16)
    key_rot = rotate(key_raw.reshape(length, kv_local, HD), cosine, sine, 1.0).astype(bf16)
    query_blocks = query_rot.reshape(block_count, block_rows, kv_local, group_size, HD)
    block_starts = jnp.arange(block_count, dtype=jnp.int32) * block_rows
    positions = jnp.arange(length, dtype=jnp.int32)
    prefix_len = prefix[0]

    def block_scores(query_block, offset):
        query_pos = offset + jnp.arange(block_rows, dtype=jnp.int32)
        raw_scores = (
            jnp.einsum("igjd,kgd->gjik", query_block, key_rot, preferred_element_type=jnp.float32)
            * score_scale
        )
        visible = (positions[None, :] <= query_pos[:, None]) | (positions[None, :] < prefix_len)
        return jnp.where(visible[None, None], raw_scores, -1e30)

    def attend_block(inputs):
        query_block, offset = inputs
        scores = block_scores(query_block, offset)
        row_peak = jnp.max(scores, -1, keepdims=True)
        weights = jnp.exp(scores - row_peak)
        row_total = jnp.sum(weights, -1, keepdims=True)
        probabilities = (weights / row_total).astype(jnp.bfloat16)
        attended = jnp.einsum(
            "gjik,kgd->igjd", probabilities, values, preferred_element_type=jnp.float32
        )
        return (attended.astype(jnp.bfloat16), (row_peak + jnp.log(row_total))[..., 0])

    attended_blocks, log_totals = lax.map(attend_block, (query_blocks, block_starts))
    attended_all = attended_blocks.reshape(length, heads_local * HD)
    attention_rows = lax.psum_scatter(
        jnp.dot(attended_all, w_out, preferred_element_type=f32).astype(bf16),
        ("x", "c"),
        scatter_dimension=0,
        tiled=True,
    ).astype(f32)
    x_rows = lax.dynamic_slice_in_dim(tokens, tensor_rank * own_rows, own_rows, 0).astype(f32)
    hidden_in = x_rows + attention_rows
    rms_two = lax.rsqrt(jnp.mean(hidden_in * hidden_in, -1, keepdims=True) + EPSILON)
    gain_two = gain_moe.astype(f32)
    normed_two = (hidden_in * rms_two * gain_two).astype(bf16)
    normed_all = lax.all_gather(normed_two, "z", axis=0, tiled=False)

    def gates(rows, code):
        logits = jnp.dot(rows, w_router, preferred_element_type=f32)
        chosen = jnp.where(code >= 0, logits, -jnp.inf)
        raised = jnp.exp(chosen - jnp.max(chosen, -1, keepdims=True))
        return raised / jnp.sum(raised, -1, keepdims=True)

    gate_own = gates(normed_two, slot_code)
    first = z_rank * group_experts
    gate_all = jax.vmap(gates)(normed_all, code_all)
    gate_group = lax.dynamic_slice_in_dim(gate_all, first, group_experts, 2)
    code_group = lax.dynamic_slice_in_dim(code_all, first, group_experts, 2).astype(jnp.int32)
    slot_ids = jnp.arange(capacity, dtype=jnp.int32)
    hot = code_group.transpose(2, 0, 1)[:, :, None, :] == slot_ids[None, None, :, None]
    pick = hot.astype(bf16)
    pick_gate = jnp.where(hot, gate_group.transpose(2, 0, 1)[:, :, None, :], 0.0)
    gate_slot = jnp.sum(pick_gate, -1)
    rows_in = jnp.einsum("esci,sid->escd", pick, normed_all, preferred_element_type=f32).astype(bf16)
    rows_dy = jnp.einsum("esci,sid->escd", pick, cot_all, preferred_element_type=f32)
    gate_pre = jnp.einsum("escd,edf->escf", rows_in, weights_gate, preferred_element_type=f32)
    up_pre = jnp.einsum("escd,edf->escf", rows_in, weights_up, preferred_element_type=f32)
    activated = (gate_pre / (1.0 + jnp.exp(-gate_pre)) * up_pre).astype(bf16)
    expert_out = jnp.einsum(
        "escf,efd->escd", activated, weights_down, preferred_element_type=f32
    ).astype(bf16)
    out_grad_rows = (rows_dy * gate_slot[..., None]).astype(bf16)
    gate_grad_slot = jnp.sum(rows_dy * expert_out.astype(f32), -1)
    gate_grad = jnp.einsum("esci,esc->sie", pick.astype(f32), gate_grad_slot, precision=HIGHEST)
    moe_part = jnp.einsum(
        "esci,escd->sid", pick_gate.astype(bf16), expert_out, preferred_element_type=f32
    ).astype(bf16)
    hid_grad = jnp.einsum("escd,efd->escf", out_grad_rows, weights_down, preferred_element_type=f32)
    sigmoid_g = 1.0 / (1.0 + jnp.exp(-gate_pre))
    back_gate = (hid_grad * up_pre * sigmoid_g * (1.0 + gate_pre * (1.0 - sigmoid_g))).astype(bf16)
    back_up = (hid_grad * gate_pre * sigmoid_g).astype(bf16)
    rows_grad = (
        jnp.einsum("escf,edf->escd", back_gate, weights_gate, preferred_element_type=f32)
        + jnp.einsum("escf,edf->escd", back_up, weights_up, preferred_element_type=f32)
    ).astype(bf16)
    rows_part = jnp.einsum("esci,escd->sid", pick, rows_grad, preferred_element_type=f32).astype(bf16)
    down_part = jnp.einsum("escf,escd->efd", activated, out_grad_rows, preferred_element_type=f32)
    gate_part = jnp.einsum("escd,escf->edf", rows_in, back_gate, preferred_element_type=f32)
    up_part = jnp.einsum("escd,escf->edf", rows_in, back_up, preferred_element_type=f32)

    gate_grad_wide = lax.dynamic_update_slice_in_dim(
        jnp.zeros((z_count, own_rows, EXPERTS), f32), gate_grad, first, 2
    )
    back_pack = jnp.concatenate([rows_part, gate_grad_wide.astype(bf16)], -1)
    back_own = lax.psum_scatter(back_pack, "z", scatter_dimension=0, tiled=False).astype(f32)
    moe_own = lax.psum_scatter(moe_part, "z", scatter_dimension=0, tiled=False).astype(f32)
    block_output = (hidden_in + moe_own).astype(bf16)

    def shard_sum(part, dim):
        width = part.shape[dim] // shards
        split = part.reshape((y_count, local_experts) + part.shape[1:dim] + (shards, width) + part.shape[dim + 1 :])
        split = jnp.moveaxis(split, dim + 1, 1).astype(bf16)
        split = split.reshape((y_count * shards,) + split.shape[2:])
        return lax.psum_scatter(split, ("y", "x", "c"), scatter_dimension=0, tiled=False).astype(f32)

    grad_gate = shard_sum(gate_part, 2)
    grad_up = shard_sum(up_part, 2)
    grad_down = shard_sum(down_part, 1)

    normed_two_grad = back_own[:, :model_width]
    gate_grad_own = back_own[:, model_width:]
    logit_grad = gate_own * (
        gate_grad_own - jnp.sum(gate_own * gate_grad_own, -1, keepdims=True)
    )
    router_part = jnp.dot(normed_two.astype(f32).T, logit_grad, precision=HIGHEST)
    normed_two_grad = normed_two_grad + jnp.dot(
        logit_grad, w_router.astype(f32).T, precision=HIGHEST
    )
    gain_two_part = jnp.sum(normed_two_grad * hidden_in * rms_two, 0)
    scaled_two = normed_two_grad * gain_two
    grad_rows = cotangent.astype(f32)
    hidden_grad = (
        grad_rows
        + rms_two * scaled_two
        - hidden_in * rms_two**3 * jnp.mean(scaled_two * hidden_in, -1, keepdims=True)
    )
    shard_part = lax.all_gather(
        hidden_grad.astype(bf16), ("x", "c"), axis=0, tiled=True
    ).astype(f32)
    attended_part = jnp.einsum(
        "id,hd->ih", shard_part.astype(jnp.bfloat16), w_out, preferred_element_type=jnp.float32
    )
    attended_grad = attended_part.astype(jnp.bfloat16)
    out_grad = jnp.einsum(
        "ih,id->hd",
        attended_all,
        shard_part.astype(jnp.bfloat16),
        preferred_element_type=jnp.float32,
    )
    grad_blocks = attended_grad.reshape(block_count, block_rows, kv_local, group_size, HD)

    def back_block(running, inputs):
        key_acc, value_acc = running
        query_block, grad_block, log_block, offset = inputs
        scores = block_scores(query_block, offset)
        probabilities = jnp.exp(scores - log_block[..., None])
        prob_grad = jnp.einsum(
            "igjd,kgd->gjik", grad_block, values, preferred_element_type=jnp.float32
        )
        center = jnp.sum(prob_grad * probabilities, -1, keepdims=True)
        score_grad = (probabilities * (prob_grad - center)).astype(jnp.bfloat16)
        query_grad = (
            jnp.einsum("gjik,kgd->igjd", score_grad, key_rot, preferred_element_type=jnp.float32)
            * score_scale
        )
        key_acc = (
            key_acc
            + jnp.einsum(
                "gjik,igjd->kgd", score_grad, query_block, preferred_element_type=jnp.float32
            )
            * score_scale
        )
        value_acc = value_acc + jnp.einsum(
            "gjik,igjd->kgd",
            probabilities.astype(jnp.bfloat16),
            grad_block,
            preferred_element_type=jnp.float32,
        )
        return ((key_acc, value_acc), query_grad)

    zero_kv = jnp.zeros((length, kv_local, HD), jnp.float32)
    (key_grad, value_grad), query_grads = lax.scan(
        back_block, (zero_kv, zero_kv), (query_blocks, grad_blocks, log_totals, block_starts)
    )
    query_back = (
        rotate(query_grads.reshape(length, heads_local, HD), cosine, sine, -1.0)
        .reshape(length, heads_local * HD)
        .astype(jnp.bfloat16)
    )
    key_back = (
        rotate(key_grad, cosine, sine, -1.0).reshape(length, kv_local * HD).astype(jnp.bfloat16)
    )
    value_back = value_grad.reshape(length, kv_local * HD).astype(jnp.bfloat16)
    query_weight = jnp.einsum(
        "id,ih->dh", normed_one, query_back, preferred_element_type=jnp.float32
    )
    key_weight = jnp.einsum("id,ih->dh", normed_one, key_back, preferred_element_type=jnp.float32)
    value_weight = jnp.einsum(
        "id,ih->dh", normed_one, value_back, preferred_element_type=jnp.float32
    )
    normed_one_grad = jnp.einsum(
        "ih,dh->id", query_back, w_query, preferred_element_type=jnp.float32
    )
    normed_one_grad = normed_one_grad + jnp.einsum(
        "ih,dh->id", key_back, w_key, preferred_element_type=jnp.float32
    )
    normed_one_grad = normed_one_grad + jnp.einsum(
        "ih,dh->id", value_back, w_value, preferred_element_type=jnp.float32
    )
    total_one = lax.psum(normed_one_grad.astype(bf16), ("x", "c")).astype(f32)
    gain_one_part = jnp.sum(normed_one_grad * x_full * rms_one, 0)
    scaled_one = total_one * gain_one
    input_grad = (
        shard_part
        + rms_one * scaled_one
        - x_full * rms_one**3 * jnp.mean(scaled_one * x_full, -1, keepdims=True)
    )
    dp = ("z", "y")
    everyone = ("z", "y", "x", "c")
    summed = [
        lax.psum(part.astype(bf16), dp).astype(f32)
        for part in (query_weight, key_weight, value_weight, out_grad)
    ]
    router_total, gain_one_total, gain_two_total = (
        lax.psum(part.astype(bf16), everyone).astype(f32)
        for part in (router_part, gain_one_part, gain_two_part)
    )
    return (
        block_output,
        input_grad,
        gain_one_total,
        summed[0],
        summed[1],
        summed[2],
        summed[3],
        gain_two_total,
        router_total,
        grad_gate,
        grad_up,
        grad_down,
    )


def solution(mesh):
    dp_count, tensor_count = mesh.devices.shape
    mesh = jax.sharding.Mesh(
        mesh.devices.reshape(dp_count // 2, 2, tensor_count // 2, 2), ("z", "y", "x", "c")
    )
    fast = mesh.devices.shape == (4, 2, 2, 2)
    dp = ("z", "y")
    tensor = ("x", "c")
    both = dp + tensor
    return jax.shard_map(
        per_device_fast if fast else per_device_general,
        mesh=mesh,
        in_specs=(
            P(dp, None),
            P(dp),
            P(),
            P(None, tensor),
            P(None, tensor),
            P(None, tensor),
            P(tensor, None),
            P(),
            P(),
            P(both, None),
            P(both, None),
            P(dp, None, tensor),
            P(dp, None, tensor),
            P(dp, tensor, None),
            P(both, None),
        ),
        out_specs=(
            P(both, None),
            P(dp, None),
            P(),
            P(None, tensor),
            P(None, tensor),
            P(None, tensor),
            P(tensor, None),
            P(),
            P(),
            P(dp, None, tensor),
            P(dp, None, tensor),
            P(dp, tensor, None),
        ),
        check_vma=False,
    )
```

```python
import functools

import jax
import jax.numpy as jnp
import numpy as np
from jax import lax
from jax.experimental import pallas as pl
from jax.experimental.pallas import tpu as pltpu
from jax.sharding import PartitionSpec as P

HD = 64
EXPERTS = 32
TOPK = 8


EPSILON = 1e-06
THETA_BASE = 10000.0
HIGHEST = lax.Precision.HIGHEST


def rope_tables(length, width_in):
    half_width = width_in // 2
    frequency = THETA_BASE ** (-(jnp.arange(half_width, dtype=jnp.float32) / half_width))
    angles = jnp.arange(length, dtype=jnp.float32)[:, None] * frequency[None, :]
    return (jnp.cos(angles), jnp.sin(angles))


def rotate(vectors, cosine, sine, direction):
    half_width = vectors.shape[-1] // 2
    front_half = vectors[..., :half_width]
    back_half = vectors[..., half_width:]
    cos_part = cosine[:, None, :]
    sin_part = sine[:, None, :] * direction
    return jnp.concatenate(
        [
            front_half * cos_part - back_half * sin_part,
            back_half * cos_part + front_half * sin_part,
        ],
        -1,
    )


NT = (((1,), (1,)), ((), ()))
TN = (((0,), (0,)), ((), ()))
f32 = jnp.float32
bf16 = jnp.bfloat16
BQ = 512
BK = 1024
BK_BACK = 512

def busy(us):
    return pl.CostEstimate(flops=int(us * 1e8), bytes_accessed=0, transcendentals=0)


def lanes(shape):
    return lax.broadcasted_iota(jnp.int32, shape, len(shape) - 1)

def rope_wide(v, cos, sin):
    low = lanes(v.shape) % HD < HD // 2
    swapped = jnp.where(low, pltpu.roll(v, 128 - HD // 2, 1), pltpu.roll(v, HD // 2, 1))
    return v * cos + swapped * sin

def project_kernel(x_ref, gain_ref, wq_ref, wk_ref, wv_ref, cos_ref, sin_ref, a_ref, q_ref, k_ref, v_ref):
    x = x_ref[...].astype(f32)
    r = lax.rsqrt(jnp.mean(x * x, -1, keepdims=True) + EPSILON)
    a = (x * r * gain_ref[...].astype(f32)).astype(bf16)
    a_ref[...] = a
    cos, sin = cos_ref[...], sin_ref[...]
    k = jnp.dot(a, wk_ref[...], preferred_element_type=f32)
    k_ref[...] = rope_wide(k, cos, sin).astype(bf16)
    v = jnp.dot(a, wv_ref[...], preferred_element_type=f32).astype(bf16)
    v_ref[:, :128] = v
    v_ref[:, 128:] = jnp.ones_like(v)
    low = lanes(k.shape) < HD
    for pair in range(2):
        q = jnp.dot(a, wq_ref[:, pair * 128 : pair * 128 + 128], preferred_element_type=f32)
        q = rope_wide(q, cos, sin) * HD ** (-0.5)
        other = pltpu.roll(q, HD, 1)
        mine = low if pair == 0 else ~low
        first, second = (q, other) if pair == 0 else (other, q)
        q_ref[2 * pair] = jnp.where(mine, first, 0.0).astype(bf16)
        q_ref[2 * pair + 1] = jnp.where(mine, second, 0.0).astype(bf16)

def project(tokens, gain, wq, wk, wv, cos, sin):
    L, D = tokens.shape
    B = 256
    full = lambda a: pl.BlockSpec(a.shape, lambda i: (0,) * a.ndim)
    rows = lambda w: pl.BlockSpec((B, w), lambda i: (i, 0))
    return pl.pallas_call(
        project_kernel, grid=(L // B,),
        in_specs=[rows(D), full(gain), full(wq), full(wk), full(wv), rows(128), rows(128)],
        out_specs=[rows(D), pl.BlockSpec((4, B, 128), lambda i: (0, i, 0)), rows(128), rows(256)],
        out_shape=[pltpu.HBM((L, D), bf16), pltpu.HBM((4, L, 128), bf16), pltpu.HBM((L, 128), bf16), pltpu.HBM((L, 256), bf16)],
        compiler_params=pltpu.CompilerParams(vmem_limit_bytes=40 << 20),
        cost_estimate=busy(9),
        name="project",
    )(tokens, gain, wq, wk, wv, cos, sin)

def attend_kernel(bq, bk, kv, prefix_ref, q_ref, k_ref, v_ref, *refs):
    o_ref, lse_ref, s_ref = refs[-3:]
    i = pl.program_id(0)
    start = i * bq
    prefix = prefix_ref[0]
    full_blocks = jnp.maximum(start + 1, prefix) // bk
    all_blocks = (jnp.maximum(start + bq, prefix) + bk - 1) // bk
    rows = 2 * bq
    pos = start + lax.broadcasted_iota(jnp.int32, (rows, 1), 0) % bq
    limit = jnp.maximum(pos, prefix - 1)
    low = lanes((bq, 128)) < HD
    q = jnp.concatenate([q_ref[0], q_ref[1]], 0)

    def tile_max(s, peak):
        for c in range(bk // 128):
            peak = jnp.maximum(peak, s[:, c * 128 : c * 128 + 128])
        return peak

    def plain(j, peak):
        off = pl.multiple_of(j * bk, bk)
        s = lax.dot_general(q, k_ref[pl.ds(off, bk), :], NT, preferred_element_type=f32)
        s_ref[:, pl.ds(off, bk)] = s
        return tile_max(s, peak)

    def masked(j, peak):
        off = pl.multiple_of(j * bk, bk)
        s = lax.dot_general(q, k_ref[pl.ds(off, bk), :], NT, preferred_element_type=f32)
        s = jnp.where(lanes((rows, bk)) <= limit - off, s, -1e30)
        s_ref[:, pl.ds(off, bk)] = s
        return tile_max(s, peak)

    peak = jnp.full((rows, 128), -1e30, f32)
    peak = lax.fori_loop(0, full_blocks, plain, peak)
    peak = lax.fori_loop(full_blocks, all_blocks, masked, peak)
    peak = jnp.max(peak, -1, keepdims=True)

    def weigh(j, acc):
        off = pl.multiple_of(j * bk, bk)
        p = jnp.exp(s_ref[:, pl.ds(off, bk)] - peak).astype(bf16)
        return acc + jnp.dot(p, v_ref[pl.ds(off, bk), :], preferred_element_type=f32)

    acc = lax.fori_loop(0, all_blocks, weigh, jnp.zeros((rows, 256), f32))
    total = acc[:, 128:]
    out = acc[:, :128] / total
    one, two = out[:bq], out[bq:]
    if kv == 0:
        merged = jnp.where(low, one, pltpu.roll(two, HD, 1))
    else:
        merged = jnp.where(low, pltpu.roll(one, HD, 1), two)
    o_ref[...] = merged.astype(bf16)
    lse = (peak + jnp.log(total)).T
    lse_ref[0] = lse[:8]


def attend(prefix, q, k, v, kv, bq, bk, before=()):
    L = k.shape[0]
    return pl.pallas_call(
        functools.partial(attend_kernel, bq, bk, kv),
        grid_spec=pltpu.PrefetchScalarGridSpec(
            num_scalar_prefetch=1, grid=(L // bq,),
            in_specs=[pl.BlockSpec((2, bq, 128), lambda i, p: (kv, i, 0)),
                      pl.BlockSpec((L, 128), lambda i, p: (0, 0)),
                      pl.BlockSpec((L, 256), lambda i, p: (0, 0))]
            + [pl.BlockSpec(memory_space=pl.ANY)] * len(before),
            out_specs=[pl.BlockSpec((bq, 128), lambda i, p: (i, kv)),
                       pl.BlockSpec((1, 8, 2 * bq), lambda i, p: (kv, 0, i))],
            scratch_shapes=[pltpu.VMEM((2 * bq, L), f32)]),
        out_shape=[pltpu.HBM((L, 256), bf16), pltpu.HBM((2, 8, 2 * L), f32)],
        input_output_aliases={4 + i: i for i in range(len(before))},
        compiler_params=pltpu.CompilerParams(vmem_limit_bytes=48 << 20),
        cost_estimate=busy(14),
        name="attend",
    )(prefix, q, k, v, *before)


def attend_back_kernel(bq, bk, prefix_ref, q_ref, k_ref, v_ref, o_ref, do_ref, lse_ref, cos_ref, sin_ref, cosa_ref, sina_ref,
                       out_ref, dk_acc, dv_acc, dq_acc):
    i = pl.program_id(0)
    start = i * bq
    prefix = prefix_ref[0]
    full_blocks = jnp.maximum(start + 1, prefix) // bk
    all_blocks = (jnp.maximum(start + bq, prefix) + bk - 1) // bk
    rows = 2 * bq
    pos = start + lax.broadcasted_iota(jnp.int32, (1, rows), 1) % bq
    limit = jnp.maximum(pos, prefix - 1)
    low = lanes((bq, 128)) < HD

    @pl.when(i == 0)
    def _():
        dk_acc[...] = jnp.zeros_like(dk_acc)
        dv_acc[...] = jnp.zeros_like(dv_acc)

    heads = []
    for kv in range(2):
        q = jnp.concatenate([q_ref[2 * kv], q_ref[2 * kv + 1]], 0)
        mine = low if kv == 0 else ~low
        pair = do_ref[:, kv * 128 : kv * 128 + 128].astype(f32)
        swap = pltpu.roll(pair, HD, 1)
        first, second = (pair, swap) if kv == 0 else (swap, pair)
        do = jnp.concatenate([jnp.where(mine, first, 0.0), jnp.where(mine, second, 0.0)], 0).astype(bf16)
        prod = pair * o_ref[:, kv * 128 : kv * 128 + 128].astype(f32)
        one = jnp.sum(jnp.where(low, prod, 0.0), -1, keepdims=True)
        two = jnp.sum(jnp.where(low, 0.0, prod), -1, keepdims=True)
        center = jnp.broadcast_to(jnp.concatenate([one, two], 0), (rows, 128)).T[:1]
        heads.append((q, do, center, lse_ref[kv, :1, :]))
    dq_acc[...] = jnp.zeros_like(dq_acc)

    def step(j, _, mask):
        off = pl.multiple_of(j * bk, bk)
        kb = k_ref[pl.ds(off, bk), :]
        vb = v_ref[pl.ds(off, bk), :128]
        dvs, dks = [], []
        for kv, (q, do, center, lse) in enumerate(heads):
            s = lax.dot_general(kb, q, NT, preferred_element_type=f32)
            dp = lax.dot_general(vb, do, NT, preferred_element_type=f32)
            if mask:
                s = jnp.where(off + lax.broadcasted_iota(jnp.int32, (bk, rows), 0) <= limit, s, -1e30)
            p = jnp.exp(s - lse)
            ds = (p * (dp - center)).astype(bf16)
            dvs.append(jnp.dot(p.astype(bf16), do, preferred_element_type=f32))
            dks.append(jnp.dot(ds, q, preferred_element_type=f32))
            dq_acc[kv] += lax.dot_general(ds, kb, TN, preferred_element_type=f32)
        dv_acc[pl.ds(off, bk), :] += dvs[0] + dvs[1]
        dk_acc[pl.ds(off, bk), :] += dks[0] + dks[1]
        return 0

    lax.fori_loop(0, full_blocks, functools.partial(step, mask=False), 0)
    lax.fori_loop(full_blocks, all_blocks, functools.partial(step, mask=True), 0)
    for kv in range(2):
        dq = dq_acc[kv] * HD ** (-0.5)
        one, two = dq[:bq], dq[bq:]
        if kv == 0:
            merged = jnp.where(low, one, pltpu.roll(two, HD, 1))
        else:
            merged = jnp.where(low, pltpu.roll(one, HD, 1), two)
        out_ref[pl.ds(pl.multiple_of(start, bq), bq), kv * 128 : kv * 128 + 128] = rope_wide(merged, cos_ref[...], -sin_ref[...]).astype(bf16)

    @pl.when(i == pl.num_programs(0) - 1)
    def _():
        for b in range(dk_acc.shape[0] // bq):
            r = pl.ds(b * bq, bq)
            out_ref[r, 256:384] = rope_wide(dk_acc[r, :], cosa_ref[r, :], -sina_ref[r, :]).astype(bf16)
            out_ref[r, 384:] = dv_acc[r, :].astype(bf16)

def attend_back(prefix, q, k, v, o, do, lse, cos, sin, bq=256, bk=256):
    L = k.shape[0]
    fullL = pl.BlockSpec((L, 128), lambda i, p: (0, 0))
    return pl.pallas_call(
        functools.partial(attend_back_kernel, bq, bk),
        grid_spec=pltpu.PrefetchScalarGridSpec(
            num_scalar_prefetch=1, grid=(L // bq,),
            in_specs=[pl.BlockSpec((4, bq, 128), lambda i, p: (0, i, 0)), fullL,
                      pl.BlockSpec((L, 256), lambda i, p: (0, 0)),
                      pl.BlockSpec((bq, 256), lambda i, p: (i, 0)),
                      pl.BlockSpec((bq, 256), lambda i, p: (i, 0)),
                      pl.BlockSpec((2, 8, 2 * bq), lambda i, p: (0, 0, i)),
                      pl.BlockSpec((bq, 128), lambda i, p: (i, 0)),
                      pl.BlockSpec((bq, 128), lambda i, p: (i, 0)), fullL, fullL],
            out_specs=pl.BlockSpec((L, 512), lambda i, p: (0, 0)),
            scratch_shapes=[pltpu.VMEM((L, 128), f32), pltpu.VMEM((L, 128), f32), pltpu.VMEM((2, 2 * bq, 128), f32)]),
        out_shape=jax.ShapeDtypeStruct((L, 512), bf16),
        compiler_params=pltpu.CompilerParams(vmem_limit_bytes=48 << 20),
        cost_estimate=busy(46),
        name="attend_back",
    )(prefix, q, k, v, o, do, lse, cos, sin, cos, sin)


def pick_kernel(experts, per, cap, pairs, shift_ref, *refs):
    in_ref, dyo_ref, gs_ref, gate_ref, code_ref, code_t, gate_t, rows_s, dy_s = refs[-9:]
    tokens, width = rows_s.shape

    @pl.when(pl.program_id(0) == 0)
    def _():
        if pairs:
            rows_ref, rows_other, side_ref, side_other, router_ref = refs[:5]
            first = shift_ref[experts] != 0
            rows = jnp.where(first, rows_ref[...], rows_other[...])
            side = jnp.where(first, side_ref[...], side_other[...])
        else:
            rows_ref, side_ref, router_ref = refs[:3]
            rows, side = rows_ref[...], side_ref[...]
        rows_s[...] = rows
        dy_s[...] = side[:, :width]
        code = side[:, width:].astype(f32)
        code_ref[...] = code
        logits = jnp.dot(rows, router_ref[...], preferred_element_type=f32)
        chosen = jnp.where(code >= 0, logits, -1e30)
        raised = jnp.where(code >= 0, jnp.exp(chosen - jnp.max(chosen, -1, keepdims=True)), 0.0)
        gate = raised / jnp.sum(raised, -1, keepdims=True)
        gate_ref[...] = gate
        gate_t[...] = gate.T
        code_t[...] = code.T

    hots = []
    for e in range(per):
        row = pl.ds(shift_ref[pl.program_id(0) * per + e], 1)
        hot = code_t[row, :] == lax.broadcasted_iota(jnp.int32, (cap, tokens), 0).astype(f32)
        gs = jnp.sum(jnp.where(hot, gate_t[row, :], 0.0), -1, keepdims=True)
        gs_ref[e] = jnp.broadcast_to(gs, (cap, 128))
        hots.append(hot.astype(bf16))
    hot = jnp.concatenate(hots, 0)
    in_ref[...] = jnp.dot(hot, rows_s[...], preferred_element_type=f32).astype(bf16).reshape(in_ref.shape)
    dyo_ref[...] = jnp.dot(hot, dy_s[...], preferred_element_type=f32).astype(bf16).reshape(dyo_ref.shape)


def pick(shift, rows, sides, router, cap):
    R, D = rows[0].shape
    E = shift.shape[0] - 1
    W = router.shape[1]
    per = 2
    operands = [*rows, *sides, router]
    whole = lambda a: pl.BlockSpec(a.shape, lambda e: (0, 0))
    some = lambda w: pl.BlockSpec((per, cap, w), lambda e: (e, 0, 0))
    wide = pl.BlockSpec((R, W), lambda e: (0, 0))
    return pl.pallas_call(
        functools.partial(pick_kernel, E, per, cap, len(rows) == 2),
        grid=(E // per,),
        in_specs=[pl.BlockSpec(memory_space=pltpu.SMEM)] + [whole(a) for a in operands],
        out_specs=[some(D), some(D), some(128), wide, wide],
        out_shape=[pltpu.HBM((E, cap, D), bf16), pltpu.HBM((E, cap, D), bf16),
                   pltpu.HBM((E, cap, 128), f32), jax.ShapeDtypeStruct((R, W), f32), jax.ShapeDtypeStruct((R, W), f32)],
        scratch_shapes=[pltpu.VMEM((W, R), f32), pltpu.VMEM((W, R), f32), pltpu.VMEM((R, D), bf16), pltpu.VMEM((R, D), bf16)],
        compiler_params=pltpu.CompilerParams(vmem_limit_bytes=40 << 20),
        cost_estimate=busy(4),
        name="pick",
    )(shift, *operands)


def ffn_kernel(n, blocks, *refs):
    rows_refs, dy_refs, gs_refs = refs[:n], refs[n : 2 * n], refs[2 * n : 3 * n]
    w_ref = refs[3 * n]
    eout_ref, drows_ref, dgs_ref, act_ref, dgu_ref = refs[-5:]
    cap, D = rows_refs[0].shape[1:]
    M = n * cap
    rows = jnp.concatenate([r[0] for r in rows_refs], 0)
    dy = jnp.concatenate([r[0] for r in dy_refs], 0)
    gs = jnp.concatenate([r[0] for r in gs_refs], 0)
    dout = (dy.astype(f32) * gs[:, :1]).astype(bf16)
    F = w_ref.shape[-1]
    eout = jnp.zeros((M, D), f32)
    drows = jnp.zeros((M, D), f32)
    for pair in range(0, blocks, 2):
        acts = []
        wd2 = jnp.concatenate([w_ref[0, pair, 2, 0], w_ref[0, pair + 1, 2, 0]], 1)
        dact2 = jnp.dot(dout, wd2, preferred_element_type=f32)
        for b in (pair, pair + 1):
            w = jnp.concatenate([w_ref[0, b, 0, 0], w_ref[0, b, 1, 0]], 1)
            gu = jnp.dot(rows, w, preferred_element_type=f32)
            g, u = gu[:, :F], gu[:, F:]
            sg = 1.0 / (1.0 + jnp.exp(-g))
            gsg = g * sg
            acts.append((gsg * u).astype(bf16))
            dact = dact2[:, (b - pair) * F : (b - pair + 1) * F]
            dg = dact * u * (sg + gsg * (1.0 - sg))
            du = dact * gsg
            dgu = jnp.concatenate([dg, du], 1).astype(bf16)
            dgu_ref[0, :, b * 2 * F : (b + 1) * 2 * F] = dgu
            drows = drows + lax.dot_general(dgu, w, NT, preferred_element_type=f32)
        act = jnp.concatenate(acts, 1)
        act_ref[0, :, pair * F : (pair + 2) * F] = act
        eout = eout + lax.dot_general(act, wd2, NT, preferred_element_type=f32)
    eout = eout.astype(bf16)
    eout_ref[0] = eout
    drows_ref[0] = drows.astype(bf16)
    dgs = jnp.sum(dy.astype(f32) * eout.astype(f32), -1, keepdims=True)
    dgs_ref[0] = jnp.broadcast_to(dgs, (M, 128))


def ffn(picked, weights, groups, before=()):
    n = len(picked)
    total, cap, D = picked[0][0].shape
    _, blocks, _, E, _, F = weights.shape
    H = blocks * F
    M = n * cap
    first = groups[0] * E
    spec = lambda w: pl.BlockSpec((1, cap, w), lambda e: (e + first, 0, 0))
    outs = lambda w: pl.BlockSpec((1, M, w), lambda e: (e + first, 0, 0))
    wsp = pl.BlockSpec((1, blocks, 3, 1, D, F), lambda e: ((e + first) // E, 0, 0, (e + first) % E, 0, 0))
    sh = lambda w, t: pltpu.HBM((total, M, w), t)
    operands = [p[i] for i in range(3) for p in picked] + [weights]
    return pl.pallas_call(
        functools.partial(ffn_kernel, n, blocks), grid=(len(groups) * E,),
        in_specs=[spec(D)] * (2 * n) + [spec(128)] * n + [wsp] + [pl.BlockSpec(memory_space=pl.ANY)] * len(before),
        out_specs=[outs(D), outs(D), outs(128), outs(H), outs(2 * H)],
        out_shape=[sh(D, bf16), sh(D, bf16), sh(128, f32), sh(H, bf16), sh(2 * H, bf16)],
        input_output_aliases={len(operands) + i: i for i in range(len(before))},
        compiler_params=pltpu.CompilerParams(vmem_limit_bytes=56 << 20),
        cost_estimate=busy(12 * len(groups)),
        name="ffn",
    )(*operands, *before)


def wgrad_kernel(n, halves, blocks, *refs):
    rows_refs, dy_refs, gs_refs = refs[:n], refs[n : 2 * n], refs[2 * n : 3 * n]
    act_refs, dgu_refs, out_ref = refs[3 * n : 3 * n + halves], refs[3 * n + halves : 3 * n + 2 * halves], refs[-1]
    rows = jnp.concatenate([r[0] for r in rows_refs], 0)
    dy = jnp.concatenate([r[0] for r in dy_refs], 0)
    gs = jnp.concatenate([r[0] for r in gs_refs], 0)
    dout = (dy.astype(f32) * gs[:, :1]).astype(bf16)
    F = act_refs[0].shape[2] // blocks
    for b in range(blocks):
        dgu = jnp.concatenate([r[0, :, b * 2 * F : (b + 1) * 2 * F] for r in dgu_refs], 0)
        g = lax.dot_general(rows, dgu, TN, preferred_element_type=f32).astype(bf16)
        out_ref[0, b, 0, 0] = g[:, :F]
        out_ref[0, b, 1, 0] = g[:, F:]
    for pair in range(0, blocks, 2):
        act = jnp.concatenate([r[0, :, pair * F : (pair + 2) * F] for r in act_refs], 0)
        gd = lax.dot_general(dout, act, TN, preferred_element_type=f32).astype(bf16)
        out_ref[0, pair, 2, 0] = gd[:, :F]
        out_ref[0, pair + 1, 2, 0] = gd[:, F:]


def wgrad(picked, acts, dgus, blocks, groups, group, before=()):
    n = len(picked)
    total, cap, D = picked[0][0].shape
    H = acts[0].shape[2]
    F = H // blocks
    E = total // groups
    spec = lambda w: pl.BlockSpec((1, cap, w), lambda e: (e + group * E, 0, 0))
    wide = lambda a: pl.BlockSpec((1,) + a.shape[1:], lambda e: (e + group * E, 0, 0))
    operands = [*[p[i] for i in range(3) for p in picked], *acts, *dgus]
    return pl.pallas_call(
        functools.partial(wgrad_kernel, n, len(acts), blocks),
        grid=(E,),
        in_specs=[spec(D)] * (2 * n) + [spec(128)] * n + [wide(a) for a in (*acts, *dgus)]
        + [pl.BlockSpec(memory_space=pl.ANY)] * len(before),
        out_specs=pl.BlockSpec((1, blocks, 3, 1, D, F), lambda e: (group, 0, 0, e, 0, 0)),
        out_shape=pltpu.HBM((groups, blocks, 3, E, D, F), bf16),
        input_output_aliases={len(operands) + i: i for i in range(len(before))},
        compiler_params=pltpu.CompilerParams(vmem_limit_bytes=56 << 20),
        cost_estimate=busy(13),
        name="wgrad",
    )(*operands, *before)


def hot_columns(code, shift, cap):
    col = jnp.sum(jnp.where(lanes(code.shape) == shift, code, 0.0), -1, keepdims=True)
    return col == lanes((code.shape[0], cap)).astype(f32)


def merge_back_kernel(n, E, cap, shift_ref, *refs):
    sides, (d_ref, g_ref), outs = refs[:n], refs[n : n + 2], refs[n + 2 :]
    D = d_ref.shape[2]
    lane = lanes((cap, 128))
    for source in range(n):

        @pl.when(pl.program_id(0) == source)
        def _():
            code = sides[source][...]
            total = jnp.zeros((code.shape[0], D), f32)
            gates = jnp.zeros((code.shape[0], 128), f32)
            for e0 in range(0, E, 4):
                some = range(e0, min(e0 + 4, E))
                hot = jnp.concatenate([hot_columns(code, shift_ref[e], cap).astype(bf16) for e in some], 1)
                rows = jnp.concatenate([d_ref[e] for e in some], 0)
                side = jnp.concatenate([jnp.where(lane == shift_ref[e], g_ref[e], 0.0).astype(bf16) for e in some], 0)
                total = total + jnp.dot(hot, rows, preferred_element_type=f32)
                gates = gates + jnp.dot(hot, side, preferred_element_type=f32)
            outs[source][:, :D] = total.astype(bf16)
            outs[source][:, D:] = gates.astype(bf16)


def merge_back(shift, codes, drows, dgs, cap):
    n = len(codes)
    R, W = codes[0].shape
    E, _, D = drows.shape
    part = lambda w: pl.BlockSpec((E, cap, w), lambda i: (0, i, 0))
    whole = lambda w: pl.BlockSpec((R, w), lambda i: (0, 0))
    return pl.pallas_call(
        functools.partial(merge_back_kernel, n, E, cap),
        grid=(n,),
        in_specs=[pl.BlockSpec(memory_space=pltpu.SMEM)] + [whole(W)] * n + [part(D), part(128)],
        out_specs=[whole(D + 128)] * n,
        out_shape=[jax.ShapeDtypeStruct((R, D + 128), bf16)] * n,
        compiler_params=pltpu.CompilerParams(vmem_limit_bytes=48 << 20),
        cost_estimate=busy(3 * n),
        name="merge_back",
    )(shift, *codes, drows, dgs)


def merge_out_kernel(n, E, cap, shift_ref, *refs):
    sides, gates, e_ref, outs = refs[:n], refs[n : 2 * n], refs[2 * n], refs[2 * n + 1 :]
    D = e_ref.shape[2]
    for source in range(n):

        @pl.when(pl.program_id(0) == source)
        def _():
            code = sides[source][...]
            gate = gates[source][...]
            total = jnp.zeros((code.shape[0], D), f32)
            for e0 in range(0, E, 4):
                some = range(e0, min(e0 + 4, E))
                parts = []
                for e in some:
                    g = jnp.sum(jnp.where(lanes(gate.shape) == shift_ref[e], gate, 0.0), -1, keepdims=True)
                    parts.append(jnp.where(hot_columns(code, shift_ref[e], cap), g, 0.0).astype(bf16))
                rows = jnp.concatenate([e_ref[e] for e in some], 0)
                total = total + jnp.dot(jnp.concatenate(parts, 1), rows, preferred_element_type=f32)
            outs[source][...] = total.astype(bf16)


def merge_out(shift, codes, gates, eout, cap):
    n = len(codes)
    R, W = codes[0].shape
    E, _, D = eout.shape
    whole = lambda w: pl.BlockSpec((R, w), lambda i: (0, 0))
    return pl.pallas_call(
        functools.partial(merge_out_kernel, n, E, cap),
        grid=(n,),
        in_specs=[pl.BlockSpec(memory_space=pltpu.SMEM)] + [whole(W)] * (2 * n)
        + [pl.BlockSpec((E, cap, D), lambda i: (0, i, 0))],
        out_specs=[whole(D)] * n,
        out_shape=[jax.ShapeDtypeStruct((R, D), bf16)] * n,
        compiler_params=pltpu.CompilerParams(vmem_limit_bytes=48 << 20),
        cost_estimate=busy(11),
        name="merge_out",
    )(shift, *codes, *gates, eout)


def finish_kernel(core_ref, sum_ref, x_ref, dh_ref, gain_ref, *refs):
    out_ref = refs[-1]
    x = x_ref[...].astype(f32)
    r = lax.rsqrt(jnp.mean(x * x, -1, keepdims=True) + EPSILON)
    scaled = sum_ref[...].astype(f32) * gain_ref[...].astype(f32)
    out_ref[...] = dh_ref[...].astype(f32) + r * scaled - x * (r * r * r * jnp.mean(scaled * x, -1, keepdims=True))


def finish(core, summed, tokens, hidden, gain, rows, before=()):
    L, D = tokens.shape
    half = rows // 2
    place = lambda i, p: ((i // 2) * 4 + p[0] * 2 + i % 2, 0)
    return pl.pallas_call(
        finish_kernel,
        grid_spec=pltpu.PrefetchScalarGridSpec(
            num_scalar_prefetch=1, grid=(L // rows,),
            in_specs=[pl.BlockSpec((half, D), lambda i, p: (i, 0)), pl.BlockSpec((half, D), place), pl.BlockSpec((half, D), place),
                      pl.BlockSpec((1, D), lambda i, p: (0, 0))] + [pl.BlockSpec(memory_space=pl.ANY)] * len(before),
            out_specs=pl.BlockSpec((half, D), place)),
        out_shape=jax.ShapeDtypeStruct((L, D), f32),
        input_output_aliases={5 + i: i for i in range(len(before))},
        compiler_params=pltpu.CompilerParams(vmem_limit_bytes=48 << 20),
        cost_estimate=busy(4),
        name="finish",
    )(core, summed, tokens, hidden, gain, *before)


def spread_kernel(n, more, rank_ref, att_ref, w_ref, *refs):
    blocks = refs[:n]
    hidden_ref, do_ref, og_ref = refs[-3:]
    i = pl.program_id(0)

    @pl.when(i == 0)
    def _():
        og_ref[...] = refs[n][...] if more else jnp.zeros_like(og_ref)

    for b in range(n):

        @pl.when(i == b)
        def _():
            block = blocks[b][...]
            hidden_ref[...] = block
            do_ref[...] = lax.dot_general(block, w_ref[...], NT, preferred_element_type=f32).astype(bf16)
            og_ref[...] += lax.dot_general(att_ref[...], block, TN, preferred_element_type=f32)


def spread(rank, first, blocks, attended, w_out, before=None):
    n = len(blocks)
    R, D = blocks[0].shape
    L, H = attended.shape
    place = lambda i, p: (p[0] ^ (i + first), 0)
    whole = lambda a: pl.BlockSpec(a.shape, lambda i, p: (0, 0))
    total = jax.ShapeDtypeStruct((H, D), f32)
    operands = [attended, w_out, *blocks]
    specs = [pl.BlockSpec((R, H), place), whole(w_out)] + [whole(b) for b in blocks]
    aliases = {}
    if before is not None:
        hidden, do, og = before
        operands += [og, hidden, do]
        specs += [whole(og)] + [pl.BlockSpec(memory_space=pl.ANY)] * 2
        aliases = {len(operands) - 1: 0, len(operands): 1}
    return pl.pallas_call(
        functools.partial(spread_kernel, n, before is not None),
        grid_spec=pltpu.PrefetchScalarGridSpec(
            num_scalar_prefetch=1, grid=(n,), in_specs=specs,
            out_specs=[pl.BlockSpec((R, D), place), pl.BlockSpec((R, H), place), whole(total)]),
        out_shape=[pltpu.HBM((L, D), bf16), pltpu.HBM((L, H), bf16), total],
        input_output_aliases=aliases,
        compiler_params=pltpu.CompilerParams(vmem_limit_bytes=32 << 20),
        cost_estimate=busy(3),
        name="spread",
    )(rank, *operands)


def swap(x, axis, bit=1):
    count = lax.axis_size(axis)
    return lax.ppermute(x, axis, [(i, i ^ bit) for i in range(count)])


def total_over(x, axes):
    for axis in axes:
        bit = 1
        while bit < lax.axis_size(axis):
            x = x + swap(x, axis, bit)
            bit *= 2
    return x


def wide_tables(length):
    half = HD // 2
    angles = np.arange(length)[:, None] * THETA_BASE ** (-(np.arange(half) / half))[None, :]
    cos, sin = np.cos(angles), np.sin(angles)
    return (
        jnp.asarray(np.concatenate([cos, cos, cos, cos], 1), f32),
        jnp.asarray(np.concatenate([-sin, sin, -sin, sin], 1), f32),
    )


NEAR = [(0, 1), (1, 0), (2, 3), (3, 2)]
MIDDLE = [(1, 2), (2, 1)]
TO_ENDS = [(1, 0), (2, 3)]
FROM_ENDS = [(0, 1), (3, 2)]


def line_first(x):
    return lax.ppermute(x, "z", NEAR), lax.ppermute(x, "z", MIDDLE)


def line_second(near, across):
    return lax.ppermute(near, "z", MIDDLE), lax.ppermute(across, "z", TO_ENDS)


def line_third(across_far):
    return lax.ppermute(across_far, "z", TO_ENDS)


def hold(*arrays):
    return lax.optimization_barrier(arrays)


def line_out(parts):
    return lax.ppermute(parts[3], "z", FROM_ENDS), lax.ppermute(parts[2], "z", FROM_ENDS)


def add_low(a, b):
    return (a.astype(f32) + b.astype(f32)).astype(a.dtype)


def line_over(part, from_end):
    return lax.ppermute(add_low(part, from_end), "z", MIDDLE)


def line_in(part, across_far):
    return lax.ppermute(add_low(part, across_far), "z", NEAR)


def line_sum(parts, from_end_far, from_end):
    own, near, two, three = parts
    across_far = line_over(two, from_end_far)
    across = line_over(three, from_end)
    got = line_in(near, across_far)
    return own.astype(f32) + across.astype(f32) + got.astype(f32)


def per_device_fast(
    tokens,
    prefix,
    gain_attn,
    w_query,
    w_key,
    w_value,
    w_out,
    gain_moe,
    w_router,
    routes,
    fill_order,
    w_gate,
    w_up,
    w_down,
    cotangent,
):
    z, y, x, c = (lax.axis_index(a) for a in ("z", "y", "x", "c"))
    shards = lax.axis_size("x") * lax.axis_size("c")
    groups = lax.axis_size("y")
    rank = x * lax.axis_size("c") + c
    at_end = (z == 0) | (z == lax.axis_size("z") - 1)
    length, width = tokens.shape
    own_rows = routes.shape[0]
    local = w_gate.shape[0]
    cap = own_rows * TOPK // EXPERTS

    own_weights = jnp.stack([w_gate, w_up, w_down.transpose(0, 2, 1)])
    weights = lax.all_gather(own_weights, ("y", "x", "c"), axis=0, tiled=False)
    weights = weights.reshape((groups, shards) + own_weights.shape)

    expert_ids = jnp.arange(EXPERTS, dtype=jnp.int32)
    member = jnp.sum((routes[:, :, None] == expert_ids[None, None, :]).astype(f32), 1)
    priority = fill_order[0]
    earlier = (priority[None, :] < priority[:, None]).astype(bf16)
    slot_full = jnp.dot(earlier, member.astype(bf16), preferred_element_type=f32)
    code = jnp.where(member > 0, jnp.minimum(slot_full, float(cap)), -1.0).astype(bf16)
    code = jnp.pad(code, ((0, 0), (0, 128 - EXPERTS)), constant_values=-1)
    side_own = jnp.concatenate([cotangent, code], 1)
    side_near, side_across = line_first(side_own)
    router_wide = jnp.pad(w_router, ((0, 0), (0, 128 - EXPERTS)))
    shift = z * groups * local + jnp.arange(groups * local, dtype=jnp.int32)
    shift_end = jnp.concatenate([shift, at_end.astype(jnp.int32)[None]])


    cos, sin = wide_tables(length)
    normed_one, query, key, value = project(tokens, gain_attn[None], w_query, w_key, w_value, cos, sin)
    first_half = attend(prefix, query, key, value, 0, BQ, BK)
    *first_half, side_near, side_across = hold(*first_half, side_near, side_across)
    side_far, side_relay = line_second(side_near, side_across)
    attended, log_total = attend(prefix, query, key, value, 1, BQ, BK, first_half)
    attended, side_far = hold(attended, side_far)
    side_last = line_third(side_far)

    def out_block(place):
        rows = lax.dynamic_slice_in_dim(attended, place * own_rows, own_rows, 0)
        return jnp.dot(rows, w_out, preferred_element_type=f32)

    far_sum = out_block(rank ^ 2) + swap(out_block(rank ^ 3).astype(bf16), "c").astype(f32)
    far_got = swap(far_sum.astype(bf16), "x")
    near_sum = out_block(rank) + swap(out_block(rank ^ 1).astype(bf16), "c").astype(f32)
    near_sum, far_got, side_relay, side_last = hold(near_sum, far_got, side_relay, side_last)
    x_rows = lax.dynamic_slice_in_dim(tokens, rank * own_rows, own_rows, 0).astype(f32)
    hidden_in = x_rows + near_sum + far_got.astype(f32)
    rms_two = lax.rsqrt(jnp.mean(hidden_in * hidden_in, -1, keepdims=True) + EPSILON)
    gain_two = gain_moe.astype(f32)
    normed_two = (hidden_in * rms_two * gain_two).astype(bf16)

    near, across = line_first(normed_two)

    def pick_of(rows, sides):
        return pick(shift_end, rows, sides, router_wide, cap)

    pick_own = pick_of((normed_two,), (side_own,))
    near, across, *pick_own = hold(near, across, *pick_own)
    far, relay = line_second(near, across)
    close = [pick_own, pick_of((near,), (side_near,))]
    half_close = ffn(close, weights, (0,))
    far, relay, *half_close = hold(far, relay, *half_close)
    last = line_third(far)
    done_close = ffn(close, weights, (1,), half_close)
    apart = [pick_of((relay, far), (side_relay, side_far))]
    last, *done_close = hold(last, *done_close)
    apart.append(pick_of((last, across), (side_last, side_across)))
    done_apart = ffn(apart, weights, (0, 1))
    picked = close + apart
    gates = [p[3] for p in picked]
    codes = [p[4] for p in picked]
    far_back = merge_back(shift, codes[2:], done_apart[1], done_apart[2], cap)
    back = [*merge_back(shift, codes[:2], done_close[1], done_close[2], cap), *far_back]
    back_end_far, back_end = line_out(back)
    late_act, *_ = hold(done_apart[3], *back)
    used = (done_close[3], late_act), (done_close[4], done_apart[4]), shards, groups
    parts = wgrad(picked, *used, 0)
    parts = wgrad(picked, *used, 1, (parts,))
    back_end_far, parts = hold(back_end_far, parts)
    across_far = line_over(back[2], back_end_far)
    across = line_over(back[3], back_end)
    late_close, late_apart, _ = hold(done_close[0], done_apart[0], across_far)
    out_parts = [
        *merge_out(shift, codes[:2], gates[:2], late_close, cap),
        *merge_out(shift, codes[2:], gates[2:], late_apart, cap),
    ]
    got = line_in(back[1], across_far)
    got, across, *out_parts = hold(got, across, *out_parts)
    back_own = back[0].astype(f32) + across.astype(f32) + got.astype(f32)
    out_end_far, out_end = line_out(out_parts)
    part_sum = lax.psum_scatter(
        parts.reshape((groups * shards,) + parts.shape[2:]), ("y", "x", "c"), scatter_dimension=0, tiled=False
    )

    gate_own = gates[0]
    gate_grad = back_own[:, width:]
    logit_grad = gate_own * (gate_grad - jnp.sum(gate_own * gate_grad, -1, keepdims=True))
    logit_low = logit_grad.astype(bf16)
    normed_two_grad = back_own[:, :width] + lax.dot_general(
        logit_low, router_wide, (((1,), (1,)), ((), ())), preferred_element_type=f32
    )
    router_part = lax.dot_general(
        logit_low, normed_two, (((0,), (0,)), ((), ())), preferred_element_type=f32
    )[:EXPERTS]
    gain_two_part = jnp.sum(normed_two_grad * hidden_in * rms_two, 0)
    scaled_two = normed_two_grad * gain_two
    hidden_grad = (
        cotangent.astype(f32)
        + rms_two * scaled_two
        - hidden_in * rms_two**3 * jnp.mean(scaled_two * hidden_in, -1, keepdims=True)
    ).astype(bf16)
    small = jnp.concatenate([router_part, gain_two_part[None], jnp.zeros((7, width), f32)], 0)
    small = small.reshape(-1, width // 2).astype(bf16)
    hidden_over_x = swap(hidden_grad, "x")
    rank_row = rank.astype(jnp.int32)[None]
    near_done = spread(rank_row, 0, [hidden_grad, swap(hidden_grad, "c")], attended, w_out)
    *near_done, out_end_far, out_end = hold(*near_done, out_end_far, out_end)
    out_two, out_three = add_low(out_parts[2], out_end_far), add_low(out_parts[3], out_end)
    hidden_over_x, out_two, out_three, *near_done = hold(hidden_over_x, out_two, out_three, *near_done)
    hidden_all, attended_grad, out_grad = spread(
        rank_row, 2, [hidden_over_x, swap(hidden_over_x, "c")], attended, w_out, near_done
    )
    attended_grad, small, out_low = hold(attended_grad, small, out_grad.astype(bf16))
    out_far, out_across = (lax.ppermute(part, "z", MIDDLE) for part in (out_two, out_three))
    heads_back = attend_back(
        prefix, query, key, value, attended, attended_grad, log_total, cos, sin, BQ, BK_BACK
    )
    heads_in = jnp.concatenate([w_query, w_key, w_value], 1)
    heads_grad = jnp.einsum("id,ih->dh", normed_one, heads_back, preferred_element_type=f32)
    low = jnp.concatenate([heads_grad.astype(bf16), out_low.reshape(-1, heads_grad.shape[1]), small], 0)
    low = jnp.pad(low, ((0, -low.shape[0] % 1024), (0, 0)))
    heads_back, low, part_sum, out_far, out_across = hold(heads_back, low, part_sum, out_far, out_across)
    out_got = line_in(out_parts[1], out_far)

    low_part = lax.psum_scatter(low, ("z", "y"), scatter_dimension=0, tiled=True)

    by_core = heads_back.reshape(shards // 2, 2, own_rows, -1)

    def rows_of(which):
        rows = lax.dynamic_index_in_dim(by_core, which, 1, keepdims=False)
        return lax.dot_general(rows, heads_in, (((2,), (1,)), ((), ())), preferred_element_type=f32)

    from_core = swap(rows_of(1 - c).astype(bf16), "c")
    core_sum = (rows_of(c) + from_core.astype(f32)).astype(bf16)
    core_got, low_part, out_got = hold(swap(core_sum, "x"), low_part, out_got)
    moe_own = out_parts[0].astype(f32) + out_across.astype(f32) + out_got.astype(f32)
    block_output = (hidden_in + moe_own).astype(bf16)
    low_all = lax.all_gather(low_part, ("z", "y"), axis=0, tiled=True)
    chip_sum = (core_sum.astype(f32) + core_got.astype(f32)).astype(bf16)
    other_sum = swap(chip_sum, "c")
    core = c.astype(jnp.int32)[None]
    gain_row = gain_attn[None]
    input_grad = finish(core, chip_sum.reshape(-1, width), tokens, hidden_all, gain_row, own_rows)
    other_sum, input_grad = hold(other_sum, input_grad)
    input_grad = finish(
        1 - core, other_sum.reshape(-1, width), tokens, hidden_all, gain_row, own_rows, (input_grad,)
    )
    expert_grads = part_sum[0].astype(f32), part_sum[1].astype(f32), part_sum[2].astype(f32).transpose(0, 2, 1)
    low_all, input_grad, block_output, *expert_grads = hold(low_all, input_grad, block_output, *expert_grads)
    low_all = low_all.astype(f32)
    split = width + out_grad.size // low.shape[1]
    heads_total = low_all[:width]
    out_total = low_all[width:split].reshape(out_grad.shape)
    gain_one_part = jnp.sum(heads_total * heads_in.astype(f32), 1) / gain_attn.astype(f32)
    rest = jnp.concatenate([low_all[split : split + 2 * (EXPERTS + 8)].reshape(-1, width), gain_one_part[None], jnp.zeros((7, width), f32)], 0)
    rest = total_over(rest.astype(bf16), ("c", "x")).astype(f32)
    cut = w_query.shape[1]
    return (
        block_output,
        input_grad,
        rest[EXPERTS + 8],
        heads_total[:, :cut],
        heads_total[:, cut : cut + w_key.shape[1]],
        heads_total[:, cut + w_key.shape[1] :],
        out_total,
        rest[EXPERTS],
        rest[:EXPERTS].T,
        *expert_grads,
    )


def group_gather(x, axes):
    return lax.all_gather(x, axes, axis=0, tiled=False)


def per_device_general(
    tokens,
    prefix,
    gain_attn,
    w_query,
    w_key,
    w_value,
    w_out,
    gain_moe,
    w_router,
    routes,
    fill_order,
    w_gate,
    w_up,
    w_down,
    cotangent,
):
    f32 = jnp.float32
    bf16 = jnp.bfloat16
    z_count = lax.axis_size("z")
    y_count = lax.axis_size("y")
    shards = lax.axis_size("x") * lax.axis_size("c")
    z_rank = lax.axis_index("z")
    tensor_rank = lax.axis_index("x") * lax.axis_size("c") + lax.axis_index("c")
    length = tokens.shape[0]
    model_width = tokens.shape[1]
    own_rows = routes.shape[0]
    local_experts = w_gate.shape[0]
    group_experts = local_experts * y_count
    capacity = own_rows * TOPK // EXPERTS
    heads_local = w_query.shape[1] // HD
    kv_local = w_key.shape[1] // HD
    group_size = heads_local // kv_local
    block_rows = min(512, length)
    block_count = length // block_rows
    score_scale = HD ** (-0.5)
    hidden = w_gate.shape[2] * shards

    expert_ids = jnp.arange(EXPERTS, dtype=jnp.int32)
    member = jnp.sum((routes[:, :, None] == expert_ids[None, None, :]).astype(f32), 1)
    priority = fill_order[0]
    earlier = (priority[None, :] < priority[:, None]).astype(bf16)
    slot_full = jnp.dot(earlier, member.astype(bf16), preferred_element_type=f32)
    slot_code = jnp.where(member > 0, jnp.minimum(slot_full, float(capacity)), -1.0).astype(bf16)

    weights_gate = group_gather(w_gate, ("y", "x", "c")).reshape(
        y_count, shards, local_experts, model_width, -1
    )
    weights_up = group_gather(w_up, ("y", "x", "c")).reshape(
        y_count, shards, local_experts, model_width, -1
    )
    weights_down = group_gather(w_down, ("y", "x", "c")).reshape(
        y_count, shards, local_experts, -1, model_width
    )
    weights_gate = weights_gate.transpose(0, 2, 3, 1, 4).reshape(group_experts, model_width, hidden)
    weights_up = weights_up.transpose(0, 2, 3, 1, 4).reshape(group_experts, model_width, hidden)
    weights_down = weights_down.transpose(0, 2, 1, 3, 4).reshape(group_experts, hidden, model_width)
    cot_all = lax.all_gather(cotangent, "z", axis=0, tiled=False)
    code_all = lax.all_gather(slot_code, "z", axis=0, tiled=False)

    x_full = tokens.astype(f32)
    rms_one = lax.rsqrt(jnp.mean(x_full * x_full, -1, keepdims=True) + EPSILON)
    gain_one = gain_attn.astype(f32)
    normed_one = (x_full * rms_one * gain_one).astype(bf16)
    query_raw = jnp.dot(normed_one, w_query, preferred_element_type=f32)
    key_raw = jnp.dot(normed_one, w_key, preferred_element_type=f32)
    values = (
        jnp.dot(normed_one, w_value, preferred_element_type=f32)
        .astype(bf16)
        .reshape(length, kv_local, HD)
    )
    cosine, sine = rope_tables(length, HD)
    query_rot = rotate(query_raw.reshape(length, heads_local, HD), cosine, sine, 1.0).astype(bf16)
    key_rot = rotate(key_raw.reshape(length, kv_local, HD), cosine, sine, 1.0).astype(bf16)
    query_blocks = query_rot.reshape(block_count, block_rows, kv_local, group_size, HD)
    block_starts = jnp.arange(block_count, dtype=jnp.int32) * block_rows
    positions = jnp.arange(length, dtype=jnp.int32)
    prefix_len = prefix[0]

    def block_scores(query_block, offset):
        query_pos = offset + jnp.arange(block_rows, dtype=jnp.int32)
        raw_scores = (
            jnp.einsum("igjd,kgd->gjik", query_block, key_rot, preferred_element_type=jnp.float32)
            * score_scale
        )
        visible = (positions[None, :] <= query_pos[:, None]) | (positions[None, :] < prefix_len)
        return jnp.where(visible[None, None], raw_scores, -1e30)

    def attend_block(inputs):
        query_block, offset = inputs
        scores = block_scores(query_block, offset)
        row_peak = jnp.max(scores, -1, keepdims=True)
        weights = jnp.exp(scores - row_peak)
        row_total = jnp.sum(weights, -1, keepdims=True)
        probabilities = (weights / row_total).astype(jnp.bfloat16)
        attended = jnp.einsum(
            "gjik,kgd->igjd", probabilities, values, preferred_element_type=jnp.float32
        )
        return (attended.astype(jnp.bfloat16), (row_peak + jnp.log(row_total))[..., 0])

    attended_blocks, log_totals = lax.map(attend_block, (query_blocks, block_starts))
    attended_all = attended_blocks.reshape(length, heads_local * HD)
    attention_rows = lax.psum_scatter(
        jnp.dot(attended_all, w_out, preferred_element_type=f32).astype(bf16),
        ("x", "c"),
        scatter_dimension=0,
        tiled=True,
    ).astype(f32)
    x_rows = lax.dynamic_slice_in_dim(tokens, tensor_rank * own_rows, own_rows, 0).astype(f32)
    hidden_in = x_rows + attention_rows
    rms_two = lax.rsqrt(jnp.mean(hidden_in * hidden_in, -1, keepdims=True) + EPSILON)
    gain_two = gain_moe.astype(f32)
    normed_two = (hidden_in * rms_two * gain_two).astype(bf16)
    normed_all = lax.all_gather(normed_two, "z", axis=0, tiled=False)

    def gates(rows, code):
        logits = jnp.dot(rows, w_router, preferred_element_type=f32)
        chosen = jnp.where(code >= 0, logits, -jnp.inf)
        raised = jnp.exp(chosen - jnp.max(chosen, -1, keepdims=True))
        return raised / jnp.sum(raised, -1, keepdims=True)

    gate_own = gates(normed_two, slot_code)
    first = z_rank * group_experts
    gate_all = jax.vmap(gates)(normed_all, code_all)
    gate_group = lax.dynamic_slice_in_dim(gate_all, first, group_experts, 2)
    code_group = lax.dynamic_slice_in_dim(code_all, first, group_experts, 2).astype(jnp.int32)
    slot_ids = jnp.arange(capacity, dtype=jnp.int32)
    hot = code_group.transpose(2, 0, 1)[:, :, None, :] == slot_ids[None, None, :, None]
    pick = hot.astype(bf16)
    pick_gate = jnp.where(hot, gate_group.transpose(2, 0, 1)[:, :, None, :], 0.0)
    gate_slot = jnp.sum(pick_gate, -1)
    rows_in = jnp.einsum("esci,sid->escd", pick, normed_all, preferred_element_type=f32).astype(bf16)
    rows_dy = jnp.einsum("esci,sid->escd", pick, cot_all, preferred_element_type=f32)
    gate_pre = jnp.einsum("escd,edf->escf", rows_in, weights_gate, preferred_element_type=f32)
    up_pre = jnp.einsum("escd,edf->escf", rows_in, weights_up, preferred_element_type=f32)
    activated = (gate_pre / (1.0 + jnp.exp(-gate_pre)) * up_pre).astype(bf16)
    expert_out = jnp.einsum(
        "escf,efd->escd", activated, weights_down, preferred_element_type=f32
    ).astype(bf16)
    out_grad_rows = (rows_dy * gate_slot[..., None]).astype(bf16)
    gate_grad_slot = jnp.sum(rows_dy * expert_out.astype(f32), -1)
    gate_grad = jnp.einsum("esci,esc->sie", pick.astype(f32), gate_grad_slot, precision=HIGHEST)
    moe_part = jnp.einsum(
        "esci,escd->sid", pick_gate.astype(bf16), expert_out, preferred_element_type=f32
    ).astype(bf16)
    hid_grad = jnp.einsum("escd,efd->escf", out_grad_rows, weights_down, preferred_element_type=f32)
    sigmoid_g = 1.0 / (1.0 + jnp.exp(-gate_pre))
    back_gate = (hid_grad * up_pre * sigmoid_g * (1.0 + gate_pre * (1.0 - sigmoid_g))).astype(bf16)
    back_up = (hid_grad * gate_pre * sigmoid_g).astype(bf16)
    rows_grad = (
        jnp.einsum("escf,edf->escd", back_gate, weights_gate, preferred_element_type=f32)
        + jnp.einsum("escf,edf->escd", back_up, weights_up, preferred_element_type=f32)
    ).astype(bf16)
    rows_part = jnp.einsum("esci,escd->sid", pick, rows_grad, preferred_element_type=f32).astype(bf16)
    down_part = jnp.einsum("escf,escd->efd", activated, out_grad_rows, preferred_element_type=f32)
    gate_part = jnp.einsum("escd,escf->edf", rows_in, back_gate, preferred_element_type=f32)
    up_part = jnp.einsum("escd,escf->edf", rows_in, back_up, preferred_element_type=f32)

    gate_grad_wide = lax.dynamic_update_slice_in_dim(
        jnp.zeros((z_count, own_rows, EXPERTS), f32), gate_grad, first, 2
    )
    back_pack = jnp.concatenate([rows_part, gate_grad_wide.astype(bf16)], -1)
    back_own = lax.psum_scatter(back_pack, "z", scatter_dimension=0, tiled=False).astype(f32)
    moe_own = lax.psum_scatter(moe_part, "z", scatter_dimension=0, tiled=False).astype(f32)
    block_output = (hidden_in + moe_own).astype(bf16)

    def shard_sum(part, dim):
        width = part.shape[dim] // shards
        split = part.reshape((y_count, local_experts) + part.shape[1:dim] + (shards, width) + part.shape[dim + 1 :])
        split = jnp.moveaxis(split, dim + 1, 1).astype(bf16)
        split = split.reshape((y_count * shards,) + split.shape[2:])
        return lax.psum_scatter(split, ("y", "x", "c"), scatter_dimension=0, tiled=False).astype(f32)

    grad_gate = shard_sum(gate_part, 2)
    grad_up = shard_sum(up_part, 2)
    grad_down = shard_sum(down_part, 1)

    normed_two_grad = back_own[:, :model_width]
    gate_grad_own = back_own[:, model_width:]
    logit_grad = gate_own * (
        gate_grad_own - jnp.sum(gate_own * gate_grad_own, -1, keepdims=True)
    )
    router_part = jnp.dot(normed_two.astype(f32).T, logit_grad, precision=HIGHEST)
    normed_two_grad = normed_two_grad + jnp.dot(
        logit_grad, w_router.astype(f32).T, precision=HIGHEST
    )
    gain_two_part = jnp.sum(normed_two_grad * hidden_in * rms_two, 0)
    scaled_two = normed_two_grad * gain_two
    grad_rows = cotangent.astype(f32)
    hidden_grad = (
        grad_rows
        + rms_two * scaled_two
        - hidden_in * rms_two**3 * jnp.mean(scaled_two * hidden_in, -1, keepdims=True)
    )
    shard_part = lax.all_gather(
        hidden_grad.astype(bf16), ("x", "c"), axis=0, tiled=True
    ).astype(f32)
    attended_part = jnp.einsum(
        "id,hd->ih", shard_part.astype(jnp.bfloat16), w_out, preferred_element_type=jnp.float32
    )
    attended_grad = attended_part.astype(jnp.bfloat16)
    out_grad = jnp.einsum(
        "ih,id->hd",
        attended_all,
        shard_part.astype(jnp.bfloat16),
        preferred_element_type=jnp.float32,
    )
    grad_blocks = attended_grad.reshape(block_count, block_rows, kv_local, group_size, HD)

    def back_block(running, inputs):
        key_acc, value_acc = running
        query_block, grad_block, log_block, offset = inputs
        scores = block_scores(query_block, offset)
        probabilities = jnp.exp(scores - log_block[..., None])
        prob_grad = jnp.einsum(
            "igjd,kgd->gjik", grad_block, values, preferred_element_type=jnp.float32
        )
        center = jnp.sum(prob_grad * probabilities, -1, keepdims=True)
        score_grad = (probabilities * (prob_grad - center)).astype(jnp.bfloat16)
        query_grad = (
            jnp.einsum("gjik,kgd->igjd", score_grad, key_rot, preferred_element_type=jnp.float32)
            * score_scale
        )
        key_acc = (
            key_acc
            + jnp.einsum(
                "gjik,igjd->kgd", score_grad, query_block, preferred_element_type=jnp.float32
            )
            * score_scale
        )
        value_acc = value_acc + jnp.einsum(
            "gjik,igjd->kgd",
            probabilities.astype(jnp.bfloat16),
            grad_block,
            preferred_element_type=jnp.float32,
        )
        return ((key_acc, value_acc), query_grad)

    zero_kv = jnp.zeros((length, kv_local, HD), jnp.float32)
    (key_grad, value_grad), query_grads = lax.scan(
        back_block, (zero_kv, zero_kv), (query_blocks, grad_blocks, log_totals, block_starts)
    )
    query_back = (
        rotate(query_grads.reshape(length, heads_local, HD), cosine, sine, -1.0)
        .reshape(length, heads_local * HD)
        .astype(jnp.bfloat16)
    )
    key_back = (
        rotate(key_grad, cosine, sine, -1.0).reshape(length, kv_local * HD).astype(jnp.bfloat16)
    )
    value_back = value_grad.reshape(length, kv_local * HD).astype(jnp.bfloat16)
    query_weight = jnp.einsum(
        "id,ih->dh", normed_one, query_back, preferred_element_type=jnp.float32
    )
    key_weight = jnp.einsum("id,ih->dh", normed_one, key_back, preferred_element_type=jnp.float32)
    value_weight = jnp.einsum(
        "id,ih->dh", normed_one, value_back, preferred_element_type=jnp.float32
    )
    normed_one_grad = jnp.einsum(
        "ih,dh->id", query_back, w_query, preferred_element_type=jnp.float32
    )
    normed_one_grad = normed_one_grad + jnp.einsum(
        "ih,dh->id", key_back, w_key, preferred_element_type=jnp.float32
    )
    normed_one_grad = normed_one_grad + jnp.einsum(
        "ih,dh->id", value_back, w_value, preferred_element_type=jnp.float32
    )
    total_one = lax.psum(normed_one_grad.astype(bf16), ("x", "c")).astype(f32)
    gain_one_part = jnp.sum(normed_one_grad * x_full * rms_one, 0)
    scaled_one = total_one * gain_one
    input_grad = (
        shard_part
        + rms_one * scaled_one
        - x_full * rms_one**3 * jnp.mean(scaled_one * x_full, -1, keepdims=True)
    )
    dp = ("z", "y")
    everyone = ("z", "y", "x", "c")
    summed = [
        lax.psum(part.astype(bf16), dp).astype(f32)
        for part in (query_weight, key_weight, value_weight, out_grad)
    ]
    router_total, gain_one_total, gain_two_total = (
        lax.psum(part.astype(bf16), everyone).astype(f32)
        for part in (router_part, gain_one_part, gain_two_part)
    )
    return (
        block_output,
        input_grad,
        gain_one_total,
        summed[0],
        summed[1],
        summed[2],
        summed[3],
        gain_two_total,
        router_total,
        grad_gate,
        grad_up,
        grad_down,
    )


def solution(mesh):
    dp_count, tensor_count = mesh.devices.shape
    mesh = jax.sharding.Mesh(
        mesh.devices.reshape(dp_count // 2, 2, tensor_count // 2, 2), ("z", "y", "x", "c")
    )
    fast = mesh.devices.shape == (4, 2, 2, 2)
    dp = ("z", "y")
    tensor = ("x", "c")
    both = dp + tensor
    return jax.shard_map(
        per_device_fast if fast else per_device_general,
        mesh=mesh,
        in_specs=(
            P(dp, None),
            P(dp),
            P(),
            P(None, tensor),
            P(None, tensor),
            P(None, tensor),
            P(tensor, None),
            P(),
            P(),
            P(both, None),
            P(both, None),
            P(dp, None, tensor),
            P(dp, None, tensor),
            P(dp, tensor, None),
            P(both, None),
        ),
        out_specs=(
            P(both, None),
            P(dp, None),
            P(),
            P(None, tensor),
            P(None, tensor),
            P(None, tensor),
            P(tensor, None),
            P(),
            P(),
            P(dp, None, tensor),
            P(dp, None, tensor),
            P(dp, tensor, None),
        ),
        check_vma=False,
    )
```

```python
import functools

import jax
import jax.numpy as jnp
import numpy as np
from jax import lax
from jax.experimental import pallas as pl
from jax.experimental.pallas import tpu as pltpu
from jax.sharding import PartitionSpec as P

HD = 64
EXPERTS = 32
TOPK = 8


EPSILON = 1e-06
THETA_BASE = 10000.0
HIGHEST = lax.Precision.HIGHEST


def rope_tables(length, width_in):
    half_width = width_in // 2
    frequency = THETA_BASE ** (-(jnp.arange(half_width, dtype=jnp.float32) / half_width))
    angles = jnp.arange(length, dtype=jnp.float32)[:, None] * frequency[None, :]
    return (jnp.cos(angles), jnp.sin(angles))


def rotate(vectors, cosine, sine, direction):
    half_width = vectors.shape[-1] // 2
    front_half = vectors[..., :half_width]
    back_half = vectors[..., half_width:]
    cos_part = cosine[:, None, :]
    sin_part = sine[:, None, :] * direction
    return jnp.concatenate(
        [
            front_half * cos_part - back_half * sin_part,
            back_half * cos_part + front_half * sin_part,
        ],
        -1,
    )


NT = (((1,), (1,)), ((), ()))
TN = (((0,), (0,)), ((), ()))
f32 = jnp.float32
bf16 = jnp.bfloat16
BQ = 512
BK = 1024
BK_BACK = 512

def busy(us):
    return pl.CostEstimate(flops=int(us * 1e8), bytes_accessed=0, transcendentals=0)


def lanes(shape):
    return lax.broadcasted_iota(jnp.int32, shape, len(shape) - 1)

def rope_wide(v, cos, sin):
    low = lanes(v.shape) % HD < HD // 2
    swapped = jnp.where(low, pltpu.roll(v, 128 - HD // 2, 1), pltpu.roll(v, HD // 2, 1))
    return v * cos + swapped * sin

def project_kernel(x_ref, gain_ref, wq_ref, wk_ref, wv_ref, cos_ref, sin_ref, a_ref, q_ref, k_ref, v_ref):
    x = x_ref[...].astype(f32)
    r = lax.rsqrt(jnp.mean(x * x, -1, keepdims=True) + EPSILON)
    a = (x * r * gain_ref[...].astype(f32)).astype(bf16)
    a_ref[...] = a
    cos, sin = cos_ref[...], sin_ref[...]
    k = jnp.dot(a, wk_ref[...], preferred_element_type=f32)
    k_ref[...] = rope_wide(k, cos, sin).astype(bf16)
    v = jnp.dot(a, wv_ref[...], preferred_element_type=f32).astype(bf16)
    v_ref[:, :128] = v
    v_ref[:, 128:] = jnp.ones_like(v)
    low = lanes(k.shape) < HD
    for pair in range(2):
        q = jnp.dot(a, wq_ref[:, pair * 128 : pair * 128 + 128], preferred_element_type=f32)
        q = rope_wide(q, cos, sin) * HD ** (-0.5)
        other = pltpu.roll(q, HD, 1)
        mine = low if pair == 0 else ~low
        first, second = (q, other) if pair == 0 else (other, q)
        q_ref[2 * pair] = jnp.where(mine, first, 0.0).astype(bf16)
        q_ref[2 * pair + 1] = jnp.where(mine, second, 0.0).astype(bf16)

def project(tokens, gain, wq, wk, wv, cos, sin):
    L, D = tokens.shape
    B = 256
    full = lambda a: pl.BlockSpec(a.shape, lambda i: (0,) * a.ndim)
    rows = lambda w: pl.BlockSpec((B, w), lambda i: (i, 0))
    return pl.pallas_call(
        project_kernel, grid=(L // B,),
        in_specs=[rows(D), full(gain), full(wq), full(wk), full(wv), rows(128), rows(128)],
        out_specs=[rows(D), pl.BlockSpec((4, B, 128), lambda i: (0, i, 0)), rows(128), rows(256)],
        out_shape=[pltpu.HBM((L, D), bf16), pltpu.HBM((4, L, 128), bf16), pltpu.HBM((L, 128), bf16), pltpu.HBM((L, 256), bf16)],
        compiler_params=pltpu.CompilerParams(vmem_limit_bytes=40 << 20),
        cost_estimate=busy(9),
        name="project",
    )(tokens, gain, wq, wk, wv, cos, sin)

def attend_kernel(bq, bk, kv, prefix_ref, q_ref, k_ref, v_ref, *refs):
    o_ref, lse_ref, s_ref = refs[-3:]
    i = pl.program_id(0)
    start = i * bq
    prefix = prefix_ref[0]
    full_blocks = jnp.maximum(start + 1, prefix) // bk
    all_blocks = (jnp.maximum(start + bq, prefix) + bk - 1) // bk
    rows = 2 * bq
    pos = start + lax.broadcasted_iota(jnp.int32, (rows, 1), 0) % bq
    limit = jnp.maximum(pos, prefix - 1)
    low = lanes((bq, 128)) < HD
    q = jnp.concatenate([q_ref[0], q_ref[1]], 0)

    def tile_max(s, peak):
        for c in range(bk // 128):
            peak = jnp.maximum(peak, s[:, c * 128 : c * 128 + 128])
        return peak

    def plain(j, peak):
        off = pl.multiple_of(j * bk, bk)
        s = lax.dot_general(q, k_ref[pl.ds(off, bk), :], NT, preferred_element_type=f32)
        s_ref[:, pl.ds(off, bk)] = s
        return tile_max(s, peak)

    def masked(j, peak):
        off = pl.multiple_of(j * bk, bk)
        s = lax.dot_general(q, k_ref[pl.ds(off, bk), :], NT, preferred_element_type=f32)
        s = jnp.where(lanes((rows, bk)) <= limit - off, s, -1e30)
        s_ref[:, pl.ds(off, bk)] = s
        return tile_max(s, peak)

    peak = jnp.full((rows, 128), -1e30, f32)
    peak = lax.fori_loop(0, full_blocks, plain, peak)
    peak = lax.fori_loop(full_blocks, all_blocks, masked, peak)
    peak = jnp.max(peak, -1, keepdims=True)

    def weigh(j, acc):
        off = pl.multiple_of(j * bk, bk)
        p = jnp.exp(s_ref[:, pl.ds(off, bk)] - peak).astype(bf16)
        return acc + jnp.dot(p, v_ref[pl.ds(off, bk), :], preferred_element_type=f32)

    acc = lax.fori_loop(0, all_blocks, weigh, jnp.zeros((rows, 256), f32))
    total = acc[:, 128:]
    out = acc[:, :128] / total
    one, two = out[:bq], out[bq:]
    if kv == 0:
        merged = jnp.where(low, one, pltpu.roll(two, HD, 1))
    else:
        merged = jnp.where(low, pltpu.roll(one, HD, 1), two)
    o_ref[...] = merged.astype(bf16)
    lse = (peak + jnp.log(total)).T
    lse_ref[0] = lse[:8]


def attend(prefix, q, k, v, kv, bq, bk, before=()):
    L = k.shape[0]
    return pl.pallas_call(
        functools.partial(attend_kernel, bq, bk, kv),
        grid_spec=pltpu.PrefetchScalarGridSpec(
            num_scalar_prefetch=1, grid=(L // bq,),
            in_specs=[pl.BlockSpec((2, bq, 128), lambda i, p: (kv, i, 0)),
                      pl.BlockSpec((L, 128), lambda i, p: (0, 0)),
                      pl.BlockSpec((L, 256), lambda i, p: (0, 0))]
            + [pl.BlockSpec(memory_space=pl.ANY)] * len(before),
            out_specs=[pl.BlockSpec((bq, 128), lambda i, p: (i, kv)),
                       pl.BlockSpec((1, 8, 2 * bq), lambda i, p: (kv, 0, i))],
            scratch_shapes=[pltpu.VMEM((2 * bq, L), f32)]),
        out_shape=[pltpu.HBM((L, 256), bf16), pltpu.HBM((2, 8, 2 * L), f32)],
        input_output_aliases={4 + i: i for i in range(len(before))},
        compiler_params=pltpu.CompilerParams(vmem_limit_bytes=48 << 20),
        cost_estimate=busy(14),
        name="attend",
    )(prefix, q, k, v, *before)


def attend_back_kernel(bq, bk, prefix_ref, q_ref, k_ref, v_ref, o_ref, do_ref, lse_ref, cos_ref, sin_ref, cosa_ref, sina_ref,
                       out_ref, dk_acc, dv_acc, dq_acc):
    i = pl.program_id(0)
    start = i * bq
    prefix = prefix_ref[0]
    full_blocks = jnp.maximum(start + 1, prefix) // bk
    all_blocks = (jnp.maximum(start + bq, prefix) + bk - 1) // bk
    rows = 2 * bq
    pos = start + lax.broadcasted_iota(jnp.int32, (1, rows), 1) % bq
    limit = jnp.maximum(pos, prefix - 1)
    low = lanes((bq, 128)) < HD

    @pl.when(i == 0)
    def _():
        dk_acc[...] = jnp.zeros_like(dk_acc)
        dv_acc[...] = jnp.zeros_like(dv_acc)

    heads = []
    for kv in range(2):
        q = jnp.concatenate([q_ref[2 * kv], q_ref[2 * kv + 1]], 0)
        mine = low if kv == 0 else ~low
        pair = do_ref[:, kv * 128 : kv * 128 + 128].astype(f32)
        swap = pltpu.roll(pair, HD, 1)
        first, second = (pair, swap) if kv == 0 else (swap, pair)
        do = jnp.concatenate([jnp.where(mine, first, 0.0), jnp.where(mine, second, 0.0)], 0).astype(bf16)
        prod = pair * o_ref[:, kv * 128 : kv * 128 + 128].astype(f32)
        one = jnp.sum(jnp.where(low, prod, 0.0), -1, keepdims=True)
        two = jnp.sum(jnp.where(low, 0.0, prod), -1, keepdims=True)
        center = jnp.broadcast_to(jnp.concatenate([one, two], 0), (rows, 128)).T[:1]
        heads.append((q, do, center, lse_ref[kv, :1, :]))
    dq_acc[...] = jnp.zeros_like(dq_acc)

    def step(j, _, mask):
        off = pl.multiple_of(j * bk, bk)
        kb = k_ref[pl.ds(off, bk), :]
        vb = v_ref[pl.ds(off, bk), :128]
        dvs, dks = [], []
        for kv, (q, do, center, lse) in enumerate(heads):
            s = lax.dot_general(kb, q, NT, preferred_element_type=f32)
            dp = lax.dot_general(vb, do, NT, preferred_element_type=f32)
            if mask:
                s = jnp.where(off + lax.broadcasted_iota(jnp.int32, (bk, rows), 0) <= limit, s, -1e30)
            p = jnp.exp(s - lse)
            ds = (p * (dp - center)).astype(bf16)
            dvs.append(jnp.dot(p.astype(bf16), do, preferred_element_type=f32))
            dks.append(jnp.dot(ds, q, preferred_element_type=f32))
            dq_acc[kv] += lax.dot_general(ds, kb, TN, preferred_element_type=f32)
        dv_acc[pl.ds(off, bk), :] += dvs[0] + dvs[1]
        dk_acc[pl.ds(off, bk), :] += dks[0] + dks[1]
        return 0

    lax.fori_loop(0, full_blocks, functools.partial(step, mask=False), 0)
    lax.fori_loop(full_blocks, all_blocks, functools.partial(step, mask=True), 0)
    for kv in range(2):
        dq = dq_acc[kv] * HD ** (-0.5)
        one, two = dq[:bq], dq[bq:]
        if kv == 0:
            merged = jnp.where(low, one, pltpu.roll(two, HD, 1))
        else:
            merged = jnp.where(low, pltpu.roll(one, HD, 1), two)
        out_ref[pl.ds(pl.multiple_of(start, bq), bq), kv * 128 : kv * 128 + 128] = rope_wide(merged, cos_ref[...], -sin_ref[...]).astype(bf16)

    @pl.when(i == pl.num_programs(0) - 1)
    def _():
        for b in range(dk_acc.shape[0] // bq):
            r = pl.ds(b * bq, bq)
            out_ref[r, 256:384] = rope_wide(dk_acc[r, :], cosa_ref[r, :], -sina_ref[r, :]).astype(bf16)
            out_ref[r, 384:] = dv_acc[r, :].astype(bf16)

def attend_back(prefix, q, k, v, o, do, lse, cos, sin, bq=256, bk=256):
    L = k.shape[0]
    fullL = pl.BlockSpec((L, 128), lambda i, p: (0, 0))
    return pl.pallas_call(
        functools.partial(attend_back_kernel, bq, bk),
        grid_spec=pltpu.PrefetchScalarGridSpec(
            num_scalar_prefetch=1, grid=(L // bq,),
            in_specs=[pl.BlockSpec((4, bq, 128), lambda i, p: (0, i, 0)), fullL,
                      pl.BlockSpec((L, 256), lambda i, p: (0, 0)),
                      pl.BlockSpec((bq, 256), lambda i, p: (i, 0)),
                      pl.BlockSpec((bq, 256), lambda i, p: (i, 0)),
                      pl.BlockSpec((2, 8, 2 * bq), lambda i, p: (0, 0, i)),
                      pl.BlockSpec((bq, 128), lambda i, p: (i, 0)),
                      pl.BlockSpec((bq, 128), lambda i, p: (i, 0)), fullL, fullL],
            out_specs=pl.BlockSpec((L, 512), lambda i, p: (0, 0)),
            scratch_shapes=[pltpu.VMEM((L, 128), f32), pltpu.VMEM((L, 128), f32), pltpu.VMEM((2, 2 * bq, 128), f32)]),
        out_shape=jax.ShapeDtypeStruct((L, 512), bf16),
        compiler_params=pltpu.CompilerParams(vmem_limit_bytes=48 << 20),
        cost_estimate=busy(46),
        name="attend_back",
    )(prefix, q, k, v, o, do, lse, cos, sin, cos, sin)


def pick_kernel(experts, per, cap, pairs, shift_ref, *refs):
    in_ref, dyo_ref, gs_ref, gate_ref, code_ref, code_t, gate_t, rows_s, dy_s = refs[-9:]
    tokens, width = rows_s.shape

    @pl.when(pl.program_id(0) == 0)
    def _():
        if pairs:
            rows_ref, rows_other, side_ref, side_other, router_ref = refs[:5]
            first = shift_ref[experts] != 0
            rows = jnp.where(first, rows_ref[...], rows_other[...])
            side = jnp.where(first, side_ref[...], side_other[...])
        else:
            rows_ref, side_ref, router_ref = refs[:3]
            rows, side = rows_ref[...], side_ref[...]
        rows_s[...] = rows
        dy_s[...] = side[:, :width]
        code = side[:, width:].astype(f32)
        code_ref[...] = code
        logits = jnp.dot(rows, router_ref[...], preferred_element_type=f32)
        chosen = jnp.where(code >= 0, logits, -1e30)
        raised = jnp.where(code >= 0, jnp.exp(chosen - jnp.max(chosen, -1, keepdims=True)), 0.0)
        gate = raised / jnp.sum(raised, -1, keepdims=True)
        gate_ref[...] = gate
        gate_t[...] = gate.T
        code_t[...] = code.T

    hots = []
    for e in range(per):
        row = pl.ds(shift_ref[pl.program_id(0) * per + e], 1)
        hot = code_t[row, :] == lax.broadcasted_iota(jnp.int32, (cap, tokens), 0).astype(f32)
        gs = jnp.sum(jnp.where(hot, gate_t[row, :], 0.0), -1, keepdims=True)
        gs_ref[e] = jnp.broadcast_to(gs, (cap, 128))
        hots.append(hot.astype(bf16))
    hot = jnp.concatenate(hots, 0)
    in_ref[...] = jnp.dot(hot, rows_s[...], preferred_element_type=f32).astype(bf16).reshape(in_ref.shape)
    dyo_ref[...] = jnp.dot(hot, dy_s[...], preferred_element_type=f32).astype(bf16).reshape(dyo_ref.shape)


def pick(shift, rows, sides, router, cap):
    R, D = rows[0].shape
    E = shift.shape[0] - 1
    W = router.shape[1]
    per = 2
    operands = [*rows, *sides, router]
    whole = lambda a: pl.BlockSpec(a.shape, lambda e: (0, 0))
    some = lambda w: pl.BlockSpec((per, cap, w), lambda e: (e, 0, 0))
    wide = pl.BlockSpec((R, W), lambda e: (0, 0))
    return pl.pallas_call(
        functools.partial(pick_kernel, E, per, cap, len(rows) == 2),
        grid=(E // per,),
        in_specs=[pl.BlockSpec(memory_space=pltpu.SMEM)] + [whole(a) for a in operands],
        out_specs=[some(D), some(D), some(128), wide, wide],
        out_shape=[pltpu.HBM((E, cap, D), bf16), pltpu.HBM((E, cap, D), bf16),
                   pltpu.HBM((E, cap, 128), f32), jax.ShapeDtypeStruct((R, W), f32), jax.ShapeDtypeStruct((R, W), f32)],
        scratch_shapes=[pltpu.VMEM((W, R), f32), pltpu.VMEM((W, R), f32), pltpu.VMEM((R, D), bf16), pltpu.VMEM((R, D), bf16)],
        compiler_params=pltpu.CompilerParams(vmem_limit_bytes=40 << 20),
        cost_estimate=busy(4),
        name="pick",
    )(shift, *operands)


def ffn_kernel(n, blocks, *refs):
    rows_refs, dy_refs, gs_refs = refs[:n], refs[n : 2 * n], refs[2 * n : 3 * n]
    w_ref = refs[3 * n]
    eout_ref, drows_ref, dgs_ref, act_ref, dgu_ref = refs[-5:]
    cap, D = rows_refs[0].shape[1:]
    M = n * cap
    rows = jnp.concatenate([r[0] for r in rows_refs], 0)
    dy = jnp.concatenate([r[0] for r in dy_refs], 0)
    gs = jnp.concatenate([r[0] for r in gs_refs], 0)
    dout = (dy.astype(f32) * gs[:, :1]).astype(bf16)
    F = w_ref.shape[-1]
    eout = jnp.zeros((M, D), f32)
    drows = jnp.zeros((M, D), f32)
    for pair in range(0, blocks, 2):
        acts = []
        wd2 = jnp.concatenate([w_ref[0, pair, 2, 0], w_ref[0, pair + 1, 2, 0]], 1)
        dact2 = jnp.dot(dout, wd2, preferred_element_type=f32)
        for b in (pair, pair + 1):
            w = jnp.concatenate([w_ref[0, b, 0, 0], w_ref[0, b, 1, 0]], 1)
            gu = jnp.dot(rows, w, preferred_element_type=f32)
            g, u = gu[:, :F], gu[:, F:]
            sg = 1.0 / (1.0 + jnp.exp(-g))
            gsg = g * sg
            acts.append((gsg * u).astype(bf16))
            dact = dact2[:, (b - pair) * F : (b - pair + 1) * F]
            dg = dact * u * (sg + gsg * (1.0 - sg))
            du = dact * gsg
            dgu = jnp.concatenate([dg, du], 1).astype(bf16)
            dgu_ref[0, :, b * 2 * F : (b + 1) * 2 * F] = dgu
            drows = drows + lax.dot_general(dgu, w, NT, preferred_element_type=f32)
        act = jnp.concatenate(acts, 1)
        act_ref[0, :, pair * F : (pair + 2) * F] = act
        eout = eout + lax.dot_general(act, wd2, NT, preferred_element_type=f32)
    eout = eout.astype(bf16)
    eout_ref[0] = eout
    drows_ref[0] = drows.astype(bf16)
    dgs = jnp.sum(dy.astype(f32) * eout.astype(f32), -1, keepdims=True)
    dgs_ref[0] = jnp.broadcast_to(dgs, (M, 128))


def ffn(picked, weights, groups, before=()):
    n = len(picked)
    total, cap, D = picked[0][0].shape
    _, blocks, _, E, _, F = weights.shape
    H = blocks * F
    M = n * cap
    first = groups[0] * E
    spec = lambda w: pl.BlockSpec((1, cap, w), lambda e: (e + first, 0, 0))
    outs = lambda w: pl.BlockSpec((1, M, w), lambda e: (e + first, 0, 0))
    wsp = pl.BlockSpec((1, blocks, 3, 1, D, F), lambda e: ((e + first) // E, 0, 0, (e + first) % E, 0, 0))
    sh = lambda w, t: pltpu.HBM((total, M, w), t)
    operands = [p[i] for i in range(3) for p in picked] + [weights]
    return pl.pallas_call(
        functools.partial(ffn_kernel, n, blocks), grid=(len(groups) * E,),
        in_specs=[spec(D)] * (2 * n) + [spec(128)] * n + [wsp] + [pl.BlockSpec(memory_space=pl.ANY)] * len(before),
        out_specs=[outs(D), outs(D), outs(128), outs(H), outs(2 * H)],
        out_shape=[sh(D, bf16), sh(D, bf16), sh(128, f32), sh(H, bf16), sh(2 * H, bf16)],
        input_output_aliases={len(operands) + i: i for i in range(len(before))},
        compiler_params=pltpu.CompilerParams(vmem_limit_bytes=56 << 20),
        cost_estimate=busy(12 * len(groups)),
        name="ffn",
    )(*operands, *before)


def wgrad_kernel(n, halves, blocks, *refs):
    rows_refs, dy_refs, gs_refs = refs[:n], refs[n : 2 * n], refs[2 * n : 3 * n]
    act_refs, dgu_refs, out_ref = refs[3 * n : 3 * n + halves], refs[3 * n + halves : 3 * n + 2 * halves], refs[-1]
    rows = jnp.concatenate([r[0] for r in rows_refs], 0)
    dy = jnp.concatenate([r[0] for r in dy_refs], 0)
    gs = jnp.concatenate([r[0] for r in gs_refs], 0)
    dout = (dy.astype(f32) * gs[:, :1]).astype(bf16)
    F = act_refs[0].shape[2] // blocks
    for b in range(blocks):
        dgu = jnp.concatenate([r[0, :, b * 2 * F : (b + 1) * 2 * F] for r in dgu_refs], 0)
        g = lax.dot_general(rows, dgu, TN, preferred_element_type=f32).astype(bf16)
        out_ref[0, b, 0, 0] = g[:, :F]
        out_ref[0, b, 1, 0] = g[:, F:]
    for pair in range(0, blocks, 2):
        act = jnp.concatenate([r[0, :, pair * F : (pair + 2) * F] for r in act_refs], 0)
        gd = lax.dot_general(dout, act, TN, preferred_element_type=f32).astype(bf16)
        out_ref[0, pair, 2, 0] = gd[:, :F]
        out_ref[0, pair + 1, 2, 0] = gd[:, F:]


def wgrad(picked, acts, dgus, blocks, groups, group, before=()):
    n = len(picked)
    total, cap, D = picked[0][0].shape
    H = acts[0].shape[2]
    F = H // blocks
    E = total // groups
    spec = lambda w: pl.BlockSpec((1, cap, w), lambda e: (e + group * E, 0, 0))
    wide = lambda a: pl.BlockSpec((1,) + a.shape[1:], lambda e: (e + group * E, 0, 0))
    operands = [*[p[i] for i in range(3) for p in picked], *acts, *dgus]
    return pl.pallas_call(
        functools.partial(wgrad_kernel, n, len(acts), blocks),
        grid=(E,),
        in_specs=[spec(D)] * (2 * n) + [spec(128)] * n + [wide(a) for a in (*acts, *dgus)]
        + [pl.BlockSpec(memory_space=pl.ANY)] * len(before),
        out_specs=pl.BlockSpec((1, blocks, 3, 1, D, F), lambda e: (group, 0, 0, e, 0, 0)),
        out_shape=pltpu.HBM((groups, blocks, 3, E, D, F), bf16),
        input_output_aliases={len(operands) + i: i for i in range(len(before))},
        compiler_params=pltpu.CompilerParams(vmem_limit_bytes=56 << 20),
        cost_estimate=busy(13),
        name="wgrad",
    )(*operands, *before)


def hot_columns(code, shift, cap):
    col = jnp.sum(jnp.where(lanes(code.shape) == shift, code, 0.0), -1, keepdims=True)
    return col == lanes((code.shape[0], cap)).astype(f32)


def merge_back_kernel(n, E, cap, shift_ref, *refs):
    sides, (d_ref, g_ref), outs = refs[:n], refs[n : n + 2], refs[n + 2 :]
    D = d_ref.shape[2]
    lane = lanes((cap, 128))
    for source in range(n):

        @pl.when(pl.program_id(0) == source)
        def _():
            code = sides[source][...]
            total = jnp.zeros((code.shape[0], D), f32)
            gates = jnp.zeros((code.shape[0], 128), f32)
            for e0 in range(0, E, 4):
                some = range(e0, min(e0 + 4, E))
                hot = jnp.concatenate([hot_columns(code, shift_ref[e], cap).astype(bf16) for e in some], 1)
                rows = jnp.concatenate([d_ref[e] for e in some], 0)
                side = jnp.concatenate([jnp.where(lane == shift_ref[e], g_ref[e], 0.0).astype(bf16) for e in some], 0)
                total = total + jnp.dot(hot, rows, preferred_element_type=f32)
                gates = gates + jnp.dot(hot, side, preferred_element_type=f32)
            outs[source][:, :D] = total.astype(bf16)
            outs[source][:, D:] = gates.astype(bf16)


def merge_back(shift, codes, drows, dgs, cap):
    n = len(codes)
    R, W = codes[0].shape
    E, _, D = drows.shape
    part = lambda w: pl.BlockSpec((E, cap, w), lambda i: (0, i, 0))
    whole = lambda w: pl.BlockSpec((R, w), lambda i: (0, 0))
    return pl.pallas_call(
        functools.partial(merge_back_kernel, n, E, cap),
        grid=(n,),
        in_specs=[pl.BlockSpec(memory_space=pltpu.SMEM)] + [whole(W)] * n + [part(D), part(128)],
        out_specs=[whole(D + 128)] * n,
        out_shape=[jax.ShapeDtypeStruct((R, D + 128), bf16)] * n,
        compiler_params=pltpu.CompilerParams(vmem_limit_bytes=48 << 20),
        cost_estimate=busy(3 * n),
        name="merge_back",
    )(shift, *codes, drows, dgs)


def merge_out_kernel(n, E, cap, shift_ref, *refs):
    sides, gates, e_ref, outs = refs[:n], refs[n : 2 * n], refs[2 * n], refs[2 * n + 1 :]
    D = e_ref.shape[2]
    for source in range(n):

        @pl.when(pl.program_id(0) == source)
        def _():
            code = sides[source][...]
            gate = gates[source][...]
            total = jnp.zeros((code.shape[0], D), f32)
            for e0 in range(0, E, 4):
                some = range(e0, min(e0 + 4, E))
                parts = []
                for e in some:
                    g = jnp.sum(jnp.where(lanes(gate.shape) == shift_ref[e], gate, 0.0), -1, keepdims=True)
                    parts.append(jnp.where(hot_columns(code, shift_ref[e], cap), g, 0.0).astype(bf16))
                rows = jnp.concatenate([e_ref[e] for e in some], 0)
                total = total + jnp.dot(jnp.concatenate(parts, 1), rows, preferred_element_type=f32)
            outs[source][...] = total.astype(bf16)


def merge_out(shift, codes, gates, eout, cap):
    n = len(codes)
    R, W = codes[0].shape
    E, _, D = eout.shape
    whole = lambda w: pl.BlockSpec((R, w), lambda i: (0, 0))
    return pl.pallas_call(
        functools.partial(merge_out_kernel, n, E, cap),
        grid=(n,),
        in_specs=[pl.BlockSpec(memory_space=pltpu.SMEM)] + [whole(W)] * (2 * n)
        + [pl.BlockSpec((E, cap, D), lambda i: (0, i, 0))],
        out_specs=[whole(D)] * n,
        out_shape=[jax.ShapeDtypeStruct((R, D), bf16)] * n,
        compiler_params=pltpu.CompilerParams(vmem_limit_bytes=48 << 20),
        cost_estimate=busy(11),
        name="merge_out",
    )(shift, *codes, *gates, eout)


def finish_kernel(core_ref, sum_ref, x_ref, dh_ref, gain_ref, *refs):
    out_ref = refs[-1]
    x = x_ref[...].astype(f32)
    r = lax.rsqrt(jnp.mean(x * x, -1, keepdims=True) + EPSILON)
    scaled = sum_ref[...].astype(f32) * gain_ref[...].astype(f32)
    out_ref[...] = dh_ref[...].astype(f32) + r * scaled - x * (r * r * r * jnp.mean(scaled * x, -1, keepdims=True))


def finish(core, summed, tokens, hidden, gain, rows, before=()):
    L, D = tokens.shape
    half = rows // 2
    place = lambda i, p: ((i // 2) * 4 + p[0] * 2 + i % 2, 0)
    return pl.pallas_call(
        finish_kernel,
        grid_spec=pltpu.PrefetchScalarGridSpec(
            num_scalar_prefetch=1, grid=(L // rows,),
            in_specs=[pl.BlockSpec((half, D), lambda i, p: (i, 0)), pl.BlockSpec((half, D), place), pl.BlockSpec((half, D), place),
                      pl.BlockSpec((1, D), lambda i, p: (0, 0))] + [pl.BlockSpec(memory_space=pl.ANY)] * len(before),
            out_specs=pl.BlockSpec((half, D), place)),
        out_shape=jax.ShapeDtypeStruct((L, D), f32),
        input_output_aliases={5 + i: i for i in range(len(before))},
        compiler_params=pltpu.CompilerParams(vmem_limit_bytes=48 << 20),
        cost_estimate=busy(4),
        name="finish",
    )(core, summed, tokens, hidden, gain, *before)


def spread_kernel(n, more, rank_ref, att_ref, w_ref, *refs):
    blocks = refs[:n]
    hidden_ref, do_ref, og_ref = refs[-3:]
    i = pl.program_id(0)

    @pl.when(i == 0)
    def _():
        og_ref[...] = refs[n][...] if more else jnp.zeros_like(og_ref)

    for b in range(n):

        @pl.when(i == b)
        def _():
            block = blocks[b][...]
            hidden_ref[...] = block
            do_ref[...] = lax.dot_general(block, w_ref[...], NT, preferred_element_type=f32).astype(bf16)
            og_ref[...] += lax.dot_general(att_ref[...], block, TN, preferred_element_type=f32)


def spread(rank, first, blocks, attended, w_out, before=None):
    n = len(blocks)
    R, D = blocks[0].shape
    L, H = attended.shape
    place = lambda i, p: (p[0] ^ (i + first), 0)
    whole = lambda a: pl.BlockSpec(a.shape, lambda i, p: (0, 0))
    total = jax.ShapeDtypeStruct((H, D), f32)
    operands = [attended, w_out, *blocks]
    specs = [pl.BlockSpec((R, H), place), whole(w_out)] + [whole(b) for b in blocks]
    aliases = {}
    if before is not None:
        hidden, do, og = before
        operands += [og, hidden, do]
        specs += [whole(og)] + [pl.BlockSpec(memory_space=pl.ANY)] * 2
        aliases = {len(operands) - 1: 0, len(operands): 1}
    return pl.pallas_call(
        functools.partial(spread_kernel, n, before is not None),
        grid_spec=pltpu.PrefetchScalarGridSpec(
            num_scalar_prefetch=1, grid=(n,), in_specs=specs,
            out_specs=[pl.BlockSpec((R, D), place), pl.BlockSpec((R, H), place), whole(total)]),
        out_shape=[pltpu.HBM((L, D), bf16), pltpu.HBM((L, H), bf16), total],
        input_output_aliases=aliases,
        compiler_params=pltpu.CompilerParams(vmem_limit_bytes=32 << 20),
        cost_estimate=busy(3),
        name="spread",
    )(rank, *operands)


def grads_kernel(parts_ref, gate_ref, up_ref, down_ref):
    gate_ref[0] = parts_ref[0, 0].astype(f32)
    up_ref[0] = parts_ref[1, 0].astype(f32)
    down_ref[0] = parts_ref[2, 0].astype(f32).T


def expert_grads(parts):
    _, E, D, F = parts.shape
    one = lambda *s: pl.BlockSpec((1,) + s, lambda e: (e, 0, 0))
    return pl.pallas_call(
        grads_kernel,
        grid=(E,),
        in_specs=[pl.BlockSpec((3, 1, D, F), lambda e: (0, e, 0, 0))],
        out_specs=[one(D, F), one(D, F), one(F, D)],
        out_shape=[pltpu.HBM((E, D, F), f32), pltpu.HBM((E, D, F), f32), pltpu.HBM((E, F, D), f32)],
        compiler_params=pltpu.CompilerParams(vmem_limit_bytes=32 << 20),
        cost_estimate=busy(4),
        name="expert_grads",
    )(parts)


def swap(x, axis, bit=1):
    count = lax.axis_size(axis)
    return lax.ppermute(x, axis, [(i, i ^ bit) for i in range(count)])


def total_over(x, axes):
    for axis in axes:
        bit = 1
        while bit < lax.axis_size(axis):
            low = x.astype(bf16)
            x = low.astype(f32) + swap(low, axis, bit).astype(f32)
            bit *= 2
    return x


def wide_tables(length):
    half = HD // 2
    angles = np.arange(length)[:, None] * THETA_BASE ** (-(np.arange(half) / half))[None, :]
    cos, sin = np.cos(angles), np.sin(angles)
    return (
        jnp.asarray(np.concatenate([cos, cos, cos, cos], 1), f32),
        jnp.asarray(np.concatenate([-sin, sin, -sin, sin], 1), f32),
    )


NEAR = [(0, 1), (1, 0), (2, 3), (3, 2)]
MIDDLE = [(1, 2), (2, 1)]
TO_ENDS = [(1, 0), (2, 3)]
FROM_ENDS = [(0, 1), (3, 2)]


def line_first(x):
    return lax.ppermute(x, "z", NEAR), lax.ppermute(x, "z", MIDDLE)


def line_second(near, across):
    return lax.ppermute(near, "z", MIDDLE), lax.ppermute(across, "z", TO_ENDS)


def line_third(across_far):
    return lax.ppermute(across_far, "z", TO_ENDS)


def hold(*arrays):
    return lax.optimization_barrier(arrays)


def line_out(parts):
    return lax.ppermute(parts[3], "z", FROM_ENDS), lax.ppermute(parts[2], "z", FROM_ENDS)


def add_low(a, b):
    return (a.astype(f32) + b.astype(f32)).astype(a.dtype)


def line_over(part, from_end):
    return lax.ppermute(add_low(part, from_end), "z", MIDDLE)


def line_in(part, across_far):
    return lax.ppermute(add_low(part, across_far), "z", NEAR)


def line_sum(parts, from_end_far, from_end):
    own, near, two, three = parts
    across_far = line_over(two, from_end_far)
    across = line_over(three, from_end)
    got = line_in(near, across_far)
    return own.astype(f32) + across.astype(f32) + got.astype(f32)


def per_device_fast(
    tokens,
    prefix,
    gain_attn,
    w_query,
    w_key,
    w_value,
    w_out,
    gain_moe,
    w_router,
    routes,
    fill_order,
    w_gate,
    w_up,
    w_down,
    cotangent,
):
    z, y, x, c = (lax.axis_index(a) for a in ("z", "y", "x", "c"))
    shards = lax.axis_size("x") * lax.axis_size("c")
    groups = lax.axis_size("y")
    rank = x * lax.axis_size("c") + c
    at_end = (z == 0) | (z == lax.axis_size("z") - 1)
    length, width = tokens.shape
    own_rows = routes.shape[0]
    local = w_gate.shape[0]
    cap = own_rows * TOPK // EXPERTS

    own_weights = jnp.stack([w_gate, w_up, w_down.transpose(0, 2, 1)])
    weights = lax.all_gather(own_weights, ("y", "x", "c"), axis=0, tiled=False)
    weights = weights.reshape((groups, shards) + own_weights.shape)

    expert_ids = jnp.arange(EXPERTS, dtype=jnp.int32)
    member = jnp.sum((routes[:, :, None] == expert_ids[None, None, :]).astype(f32), 1)
    priority = fill_order[0]
    earlier = (priority[None, :] < priority[:, None]).astype(bf16)
    slot_full = jnp.dot(earlier, member.astype(bf16), preferred_element_type=f32)
    code = jnp.where(member > 0, jnp.minimum(slot_full, float(cap)), -1.0).astype(bf16)
    code = jnp.pad(code, ((0, 0), (0, 128 - EXPERTS)), constant_values=-1)
    side_own = jnp.concatenate([cotangent, code], 1)
    side_near, side_across = line_first(side_own)
    router_wide = jnp.pad(w_router, ((0, 0), (0, 128 - EXPERTS)))
    shift = z * groups * local + jnp.arange(groups * local, dtype=jnp.int32)
    shift_end = jnp.concatenate([shift, at_end.astype(jnp.int32)[None]])


    cos, sin = wide_tables(length)
    normed_one, query, key, value = project(tokens, gain_attn[None], w_query, w_key, w_value, cos, sin)
    first_half = attend(prefix, query, key, value, 0, BQ, BK)
    *first_half, side_near, side_across = hold(*first_half, side_near, side_across)
    side_far, side_relay = line_second(side_near, side_across)
    attended, log_total = attend(prefix, query, key, value, 1, BQ, BK, first_half)
    attended, side_far = hold(attended, side_far)
    side_last = line_third(side_far)

    def out_block(place):
        rows = lax.dynamic_slice_in_dim(attended, place * own_rows, own_rows, 0)
        return jnp.dot(rows, w_out, preferred_element_type=f32)

    far_sum = out_block(rank ^ 2) + swap(out_block(rank ^ 3).astype(bf16), "c").astype(f32)
    far_got = swap(far_sum.astype(bf16), "x")
    near_sum = out_block(rank) + swap(out_block(rank ^ 1).astype(bf16), "c").astype(f32)
    near_sum, far_got, side_relay, side_last = hold(near_sum, far_got, side_relay, side_last)
    x_rows = lax.dynamic_slice_in_dim(tokens, rank * own_rows, own_rows, 0).astype(f32)
    hidden_in = x_rows + near_sum + far_got.astype(f32)
    rms_two = lax.rsqrt(jnp.mean(hidden_in * hidden_in, -1, keepdims=True) + EPSILON)
    gain_two = gain_moe.astype(f32)
    normed_two = (hidden_in * rms_two * gain_two).astype(bf16)

    near, across = line_first(normed_two)

    def pick_of(rows, sides):
        return pick(shift_end, rows, sides, router_wide, cap)

    pick_own = pick_of((normed_two,), (side_own,))
    near, across, *pick_own = hold(near, across, *pick_own)
    far, relay = line_second(near, across)
    close = [pick_own, pick_of((near,), (side_near,))]
    half_close = ffn(close, weights, (0,))
    far, relay, *half_close = hold(far, relay, *half_close)
    last = line_third(far)
    done_close = ffn(close, weights, (1,), half_close)
    apart = [pick_of((relay, far), (side_relay, side_far))]
    last, *done_close = hold(last, *done_close)
    apart.append(pick_of((last, across), (side_last, side_across)))
    done_apart = ffn(apart, weights, (0, 1))
    picked = close + apart
    gates = [p[3] for p in picked]
    codes = [p[4] for p in picked]
    far_back = merge_back(shift, codes[2:], done_apart[1], done_apart[2], cap)
    back = [*merge_back(shift, codes[:2], done_close[1], done_close[2], cap), *far_back]
    back_end_far, back_end = line_out(back)
    late_act, *_ = hold(done_apart[3], *far_back)
    used = (done_close[3], late_act), (done_close[4], done_apart[4]), shards, groups
    parts = wgrad(picked, *used, 0)
    parts = wgrad(picked, *used, 1, (parts,))
    back_end_far, parts = hold(back_end_far, parts)
    across_far = line_over(back[2], back_end_far)
    across = line_over(back[3], back_end)
    late_close, late_apart, _ = hold(done_close[0], done_apart[0], across_far)
    out_parts = [
        *merge_out(shift, codes[:2], gates[:2], late_close, cap),
        *merge_out(shift, codes[2:], gates[2:], late_apart, cap),
    ]
    got = line_in(back[1], across_far)
    got, across, *out_parts = hold(got, across, *out_parts)
    back_own = back[0].astype(f32) + across.astype(f32) + got.astype(f32)
    out_end_far, out_end = line_out(out_parts)
    part_sum = lax.psum_scatter(
        parts.reshape((groups * shards,) + parts.shape[2:]), ("y", "x", "c"), scatter_dimension=0, tiled=False
    )

    gate_own = gates[0]
    gate_grad = back_own[:, width:]
    logit_grad = gate_own * (gate_grad - jnp.sum(gate_own * gate_grad, -1, keepdims=True))
    logit_low = logit_grad.astype(bf16)
    normed_two_grad = back_own[:, :width] + lax.dot_general(
        logit_low, router_wide, (((1,), (1,)), ((), ())), preferred_element_type=f32
    )
    router_part = lax.dot_general(
        logit_low, normed_two, (((0,), (0,)), ((), ())), preferred_element_type=f32
    )[:EXPERTS]
    gain_two_part = jnp.sum(normed_two_grad * hidden_in * rms_two, 0)
    scaled_two = normed_two_grad * gain_two
    hidden_grad = (
        cotangent.astype(f32)
        + rms_two * scaled_two
        - hidden_in * rms_two**3 * jnp.mean(scaled_two * hidden_in, -1, keepdims=True)
    ).astype(bf16)
    small = jnp.concatenate([router_part, gain_two_part[None], jnp.zeros((7, width), f32)], 0)
    hidden_over_x = swap(hidden_grad, "x")
    rank_row = rank.astype(jnp.int32)[None]
    near_done = spread(rank_row, 0, [hidden_grad, swap(hidden_grad, "c")], attended, w_out)
    *near_done, out_end_far, out_end = hold(*near_done, out_end_far, out_end)
    out_two, out_three = add_low(out_parts[2], out_end_far), add_low(out_parts[3], out_end)
    hidden_over_x, out_two, out_three, *near_done = hold(hidden_over_x, out_two, out_three, *near_done)
    hidden_all, attended_grad, out_grad = spread(
        rank_row, 2, [hidden_over_x, swap(hidden_over_x, "c")], attended, w_out, near_done
    )
    attended_grad, small, out_low = hold(attended_grad, small, out_grad.astype(bf16))
    out_far, out_across = (lax.ppermute(part, "z", MIDDLE) for part in (out_two, out_three))
    heads_back = attend_back(
        prefix, query, key, value, attended, attended_grad, log_total, cos, sin, BQ, BK_BACK
    )
    heads_in = jnp.concatenate([w_query, w_key, w_value], 1)
    heads_grad = jnp.einsum("id,ih->dh", normed_one, heads_back, preferred_element_type=f32)
    low = jnp.concatenate([heads_grad.astype(bf16), out_low.reshape(-1, heads_grad.shape[1])], 0)
    gain_one_part = jnp.sum(heads_grad * heads_in.astype(f32), 1) / gain_attn.astype(f32)
    small = jnp.concatenate([small[: EXPERTS + 1], gain_one_part[None], small[EXPERTS + 2 :]], 0)
    heads_back, low, part_sum, out_far, out_across = hold(heads_back, low, part_sum, out_far, out_across)
    out_got = line_in(out_parts[1], out_far)

    low_part = lax.psum_scatter(low, ("z", "y"), scatter_dimension=0, tiled=True)

    by_core = heads_back.reshape(shards // 2, 2, own_rows, -1)

    def rows_of(which):
        rows = lax.dynamic_index_in_dim(by_core, which, 1, keepdims=False)
        return lax.dot_general(rows, heads_in, (((2,), (1,)), ((), ())), preferred_element_type=f32)

    from_core = swap(rows_of(1 - c).astype(bf16), "c")
    core_sum = (rows_of(c) + from_core.astype(f32)).astype(bf16)
    core_got, low_part, out_got, small = hold(swap(core_sum, "x"), low_part, out_got, small)
    rest = total_over(small, ("c", "x", "y", "z"))
    moe_own = out_parts[0].astype(f32) + out_across.astype(f32) + out_got.astype(f32)
    block_output = (hidden_in + moe_own).astype(bf16)
    low_all = lax.all_gather(low_part, ("z", "y"), axis=0, tiled=True)
    summed_grads = expert_grads(part_sum)
    chip_sum = (core_sum.astype(f32) + core_got.astype(f32)).astype(bf16)
    other_sum = swap(chip_sum, "c")
    core = c.astype(jnp.int32)[None]
    gain_row = gain_attn[None]
    input_grad = finish(core, chip_sum.reshape(-1, width), tokens, hidden_all, gain_row, own_rows)
    other_sum, input_grad, *summed_grads = hold(other_sum, input_grad, *summed_grads)
    input_grad = finish(
        1 - core, other_sum.reshape(-1, width), tokens, hidden_all, gain_row, own_rows, (input_grad,)
    )
    low_all, input_grad, block_output, rest = hold(low_all, input_grad, block_output, rest)
    low_all = low_all.astype(f32)
    heads_total = low_all[:width]
    out_total = low_all[width:].reshape(out_grad.shape)
    cut = w_query.shape[1]
    return (
        block_output,
        input_grad,
        rest[EXPERTS + 1],
        heads_total[:, :cut],
        heads_total[:, cut : cut + w_key.shape[1]],
        heads_total[:, cut + w_key.shape[1] :],
        out_total,
        rest[EXPERTS],
        rest[:EXPERTS].T,
        *summed_grads,
    )


def group_gather(x, axes):
    return lax.all_gather(x, axes, axis=0, tiled=False)


def per_device_general(
    tokens,
    prefix,
    gain_attn,
    w_query,
    w_key,
    w_value,
    w_out,
    gain_moe,
    w_router,
    routes,
    fill_order,
    w_gate,
    w_up,
    w_down,
    cotangent,
):
    f32 = jnp.float32
    bf16 = jnp.bfloat16
    z_count = lax.axis_size("z")
    y_count = lax.axis_size("y")
    shards = lax.axis_size("x") * lax.axis_size("c")
    z_rank = lax.axis_index("z")
    tensor_rank = lax.axis_index("x") * lax.axis_size("c") + lax.axis_index("c")
    length = tokens.shape[0]
    model_width = tokens.shape[1]
    own_rows = routes.shape[0]
    local_experts = w_gate.shape[0]
    group_experts = local_experts * y_count
    capacity = own_rows * TOPK // EXPERTS
    heads_local = w_query.shape[1] // HD
    kv_local = w_key.shape[1] // HD
    group_size = heads_local // kv_local
    block_rows = min(512, length)
    block_count = length // block_rows
    score_scale = HD ** (-0.5)
    hidden = w_gate.shape[2] * shards

    expert_ids = jnp.arange(EXPERTS, dtype=jnp.int32)
    member = jnp.sum((routes[:, :, None] == expert_ids[None, None, :]).astype(f32), 1)
    priority = fill_order[0]
    earlier = (priority[None, :] < priority[:, None]).astype(bf16)
    slot_full = jnp.dot(earlier, member.astype(bf16), preferred_element_type=f32)
    slot_code = jnp.where(member > 0, jnp.minimum(slot_full, float(capacity)), -1.0).astype(bf16)

    weights_gate = group_gather(w_gate, ("y", "x", "c")).reshape(
        y_count, shards, local_experts, model_width, -1
    )
    weights_up = group_gather(w_up, ("y", "x", "c")).reshape(
        y_count, shards, local_experts, model_width, -1
    )
    weights_down = group_gather(w_down, ("y", "x", "c")).reshape(
        y_count, shards, local_experts, -1, model_width
    )
    weights_gate = weights_gate.transpose(0, 2, 3, 1, 4).reshape(group_experts, model_width, hidden)
    weights_up = weights_up.transpose(0, 2, 3, 1, 4).reshape(group_experts, model_width, hidden)
    weights_down = weights_down.transpose(0, 2, 1, 3, 4).reshape(group_experts, hidden, model_width)
    cot_all = lax.all_gather(cotangent, "z", axis=0, tiled=False)
    code_all = lax.all_gather(slot_code, "z", axis=0, tiled=False)

    x_full = tokens.astype(f32)
    rms_one = lax.rsqrt(jnp.mean(x_full * x_full, -1, keepdims=True) + EPSILON)
    gain_one = gain_attn.astype(f32)
    normed_one = (x_full * rms_one * gain_one).astype(bf16)
    query_raw = jnp.dot(normed_one, w_query, preferred_element_type=f32)
    key_raw = jnp.dot(normed_one, w_key, preferred_element_type=f32)
    values = (
        jnp.dot(normed_one, w_value, preferred_element_type=f32)
        .astype(bf16)
        .reshape(length, kv_local, HD)
    )
    cosine, sine = rope_tables(length, HD)
    query_rot = rotate(query_raw.reshape(length, heads_local, HD), cosine, sine, 1.0).astype(bf16)
    key_rot = rotate(key_raw.reshape(length, kv_local, HD), cosine, sine, 1.0).astype(bf16)
    query_blocks = query_rot.reshape(block_count, block_rows, kv_local, group_size, HD)
    block_starts = jnp.arange(block_count, dtype=jnp.int32) * block_rows
    positions = jnp.arange(length, dtype=jnp.int32)
    prefix_len = prefix[0]

    def block_scores(query_block, offset):
        query_pos = offset + jnp.arange(block_rows, dtype=jnp.int32)
        raw_scores = (
            jnp.einsum("igjd,kgd->gjik", query_block, key_rot, preferred_element_type=jnp.float32)
            * score_scale
        )
        visible = (positions[None, :] <= query_pos[:, None]) | (positions[None, :] < prefix_len)
        return jnp.where(visible[None, None], raw_scores, -1e30)

    def attend_block(inputs):
        query_block, offset = inputs
        scores = block_scores(query_block, offset)
        row_peak = jnp.max(scores, -1, keepdims=True)
        weights = jnp.exp(scores - row_peak)
        row_total = jnp.sum(weights, -1, keepdims=True)
        probabilities = (weights / row_total).astype(jnp.bfloat16)
        attended = jnp.einsum(
            "gjik,kgd->igjd", probabilities, values, preferred_element_type=jnp.float32
        )
        return (attended.astype(jnp.bfloat16), (row_peak + jnp.log(row_total))[..., 0])

    attended_blocks, log_totals = lax.map(attend_block, (query_blocks, block_starts))
    attended_all = attended_blocks.reshape(length, heads_local * HD)
    attention_rows = lax.psum_scatter(
        jnp.dot(attended_all, w_out, preferred_element_type=f32).astype(bf16),
        ("x", "c"),
        scatter_dimension=0,
        tiled=True,
    ).astype(f32)
    x_rows = lax.dynamic_slice_in_dim(tokens, tensor_rank * own_rows, own_rows, 0).astype(f32)
    hidden_in = x_rows + attention_rows
    rms_two = lax.rsqrt(jnp.mean(hidden_in * hidden_in, -1, keepdims=True) + EPSILON)
    gain_two = gain_moe.astype(f32)
    normed_two = (hidden_in * rms_two * gain_two).astype(bf16)
    normed_all = lax.all_gather(normed_two, "z", axis=0, tiled=False)

    def gates(rows, code):
        logits = jnp.dot(rows, w_router, preferred_element_type=f32)
        chosen = jnp.where(code >= 0, logits, -jnp.inf)
        raised = jnp.exp(chosen - jnp.max(chosen, -1, keepdims=True))
        return raised / jnp.sum(raised, -1, keepdims=True)

    gate_own = gates(normed_two, slot_code)
    first = z_rank * group_experts
    gate_all = jax.vmap(gates)(normed_all, code_all)
    gate_group = lax.dynamic_slice_in_dim(gate_all, first, group_experts, 2)
    code_group = lax.dynamic_slice_in_dim(code_all, first, group_experts, 2).astype(jnp.int32)
    slot_ids = jnp.arange(capacity, dtype=jnp.int32)
    hot = code_group.transpose(2, 0, 1)[:, :, None, :] == slot_ids[None, None, :, None]
    pick = hot.astype(bf16)
    pick_gate = jnp.where(hot, gate_group.transpose(2, 0, 1)[:, :, None, :], 0.0)
    gate_slot = jnp.sum(pick_gate, -1)
    rows_in = jnp.einsum("esci,sid->escd", pick, normed_all, preferred_element_type=f32).astype(bf16)
    rows_dy = jnp.einsum("esci,sid->escd", pick, cot_all, preferred_element_type=f32)
    gate_pre = jnp.einsum("escd,edf->escf", rows_in, weights_gate, preferred_element_type=f32)
    up_pre = jnp.einsum("escd,edf->escf", rows_in, weights_up, preferred_element_type=f32)
    activated = (gate_pre / (1.0 + jnp.exp(-gate_pre)) * up_pre).astype(bf16)
    expert_out = jnp.einsum(
        "escf,efd->escd", activated, weights_down, preferred_element_type=f32
    ).astype(bf16)
    out_grad_rows = (rows_dy * gate_slot[..., None]).astype(bf16)
    gate_grad_slot = jnp.sum(rows_dy * expert_out.astype(f32), -1)
    gate_grad = jnp.einsum("esci,esc->sie", pick.astype(f32), gate_grad_slot, precision=HIGHEST)
    moe_part = jnp.einsum(
        "esci,escd->sid", pick_gate.astype(bf16), expert_out, preferred_element_type=f32
    ).astype(bf16)
    hid_grad = jnp.einsum("escd,efd->escf", out_grad_rows, weights_down, preferred_element_type=f32)
    sigmoid_g = 1.0 / (1.0 + jnp.exp(-gate_pre))
    back_gate = (hid_grad * up_pre * sigmoid_g * (1.0 + gate_pre * (1.0 - sigmoid_g))).astype(bf16)
    back_up = (hid_grad * gate_pre * sigmoid_g).astype(bf16)
    rows_grad = (
        jnp.einsum("escf,edf->escd", back_gate, weights_gate, preferred_element_type=f32)
        + jnp.einsum("escf,edf->escd", back_up, weights_up, preferred_element_type=f32)
    ).astype(bf16)
    rows_part = jnp.einsum("esci,escd->sid", pick, rows_grad, preferred_element_type=f32).astype(bf16)
    down_part = jnp.einsum("escf,escd->efd", activated, out_grad_rows, preferred_element_type=f32)
    gate_part = jnp.einsum("escd,escf->edf", rows_in, back_gate, preferred_element_type=f32)
    up_part = jnp.einsum("escd,escf->edf", rows_in, back_up, preferred_element_type=f32)

    gate_grad_wide = lax.dynamic_update_slice_in_dim(
        jnp.zeros((z_count, own_rows, EXPERTS), f32), gate_grad, first, 2
    )
    back_pack = jnp.concatenate([rows_part, gate_grad_wide.astype(bf16)], -1)
    back_own = lax.psum_scatter(back_pack, "z", scatter_dimension=0, tiled=False).astype(f32)
    moe_own = lax.psum_scatter(moe_part, "z", scatter_dimension=0, tiled=False).astype(f32)
    block_output = (hidden_in + moe_own).astype(bf16)

    def shard_sum(part, dim):
        width = part.shape[dim] // shards
        split = part.reshape((y_count, local_experts) + part.shape[1:dim] + (shards, width) + part.shape[dim + 1 :])
        split = jnp.moveaxis(split, dim + 1, 1).astype(bf16)
        split = split.reshape((y_count * shards,) + split.shape[2:])
        return lax.psum_scatter(split, ("y", "x", "c"), scatter_dimension=0, tiled=False).astype(f32)

    grad_gate = shard_sum(gate_part, 2)
    grad_up = shard_sum(up_part, 2)
    grad_down = shard_sum(down_part, 1)

    normed_two_grad = back_own[:, :model_width]
    gate_grad_own = back_own[:, model_width:]
    logit_grad = gate_own * (
        gate_grad_own - jnp.sum(gate_own * gate_grad_own, -1, keepdims=True)
    )
    router_part = jnp.dot(normed_two.astype(f32).T, logit_grad, precision=HIGHEST)
    normed_two_grad = normed_two_grad + jnp.dot(
        logit_grad, w_router.astype(f32).T, precision=HIGHEST
    )
    gain_two_part = jnp.sum(normed_two_grad * hidden_in * rms_two, 0)
    scaled_two = normed_two_grad * gain_two
    grad_rows = cotangent.astype(f32)
    hidden_grad = (
        grad_rows
        + rms_two * scaled_two
        - hidden_in * rms_two**3 * jnp.mean(scaled_two * hidden_in, -1, keepdims=True)
    )
    shard_part = lax.all_gather(
        hidden_grad.astype(bf16), ("x", "c"), axis=0, tiled=True
    ).astype(f32)
    attended_part = jnp.einsum(
        "id,hd->ih", shard_part.astype(jnp.bfloat16), w_out, preferred_element_type=jnp.float32
    )
    attended_grad = attended_part.astype(jnp.bfloat16)
    out_grad = jnp.einsum(
        "ih,id->hd",
        attended_all,
        shard_part.astype(jnp.bfloat16),
        preferred_element_type=jnp.float32,
    )
    grad_blocks = attended_grad.reshape(block_count, block_rows, kv_local, group_size, HD)

    def back_block(running, inputs):
        key_acc, value_acc = running
        query_block, grad_block, log_block, offset = inputs
        scores = block_scores(query_block, offset)
        probabilities = jnp.exp(scores - log_block[..., None])
        prob_grad = jnp.einsum(
            "igjd,kgd->gjik", grad_block, values, preferred_element_type=jnp.float32
        )
        center = jnp.sum(prob_grad * probabilities, -1, keepdims=True)
        score_grad = (probabilities * (prob_grad - center)).astype(jnp.bfloat16)
        query_grad = (
            jnp.einsum("gjik,kgd->igjd", score_grad, key_rot, preferred_element_type=jnp.float32)
            * score_scale
        )
        key_acc = (
            key_acc
            + jnp.einsum(
                "gjik,igjd->kgd", score_grad, query_block, preferred_element_type=jnp.float32
            )
            * score_scale
        )
        value_acc = value_acc + jnp.einsum(
            "gjik,igjd->kgd",
            probabilities.astype(jnp.bfloat16),
            grad_block,
            preferred_element_type=jnp.float32,
        )
        return ((key_acc, value_acc), query_grad)

    zero_kv = jnp.zeros((length, kv_local, HD), jnp.float32)
    (key_grad, value_grad), query_grads = lax.scan(
        back_block, (zero_kv, zero_kv), (query_blocks, grad_blocks, log_totals, block_starts)
    )
    query_back = (
        rotate(query_grads.reshape(length, heads_local, HD), cosine, sine, -1.0)
        .reshape(length, heads_local * HD)
        .astype(jnp.bfloat16)
    )
    key_back = (
        rotate(key_grad, cosine, sine, -1.0).reshape(length, kv_local * HD).astype(jnp.bfloat16)
    )
    value_back = value_grad.reshape(length, kv_local * HD).astype(jnp.bfloat16)
    query_weight = jnp.einsum(
        "id,ih->dh", normed_one, query_back, preferred_element_type=jnp.float32
    )
    key_weight = jnp.einsum("id,ih->dh", normed_one, key_back, preferred_element_type=jnp.float32)
    value_weight = jnp.einsum(
        "id,ih->dh", normed_one, value_back, preferred_element_type=jnp.float32
    )
    normed_one_grad = jnp.einsum(
        "ih,dh->id", query_back, w_query, preferred_element_type=jnp.float32
    )
    normed_one_grad = normed_one_grad + jnp.einsum(
        "ih,dh->id", key_back, w_key, preferred_element_type=jnp.float32
    )
    normed_one_grad = normed_one_grad + jnp.einsum(
        "ih,dh->id", value_back, w_value, preferred_element_type=jnp.float32
    )
    total_one = lax.psum(normed_one_grad.astype(bf16), ("x", "c")).astype(f32)
    gain_one_part = jnp.sum(normed_one_grad * x_full * rms_one, 0)
    scaled_one = total_one * gain_one
    input_grad = (
        shard_part
        + rms_one * scaled_one
        - x_full * rms_one**3 * jnp.mean(scaled_one * x_full, -1, keepdims=True)
    )
    dp = ("z", "y")
    everyone = ("z", "y", "x", "c")
    summed = [
        lax.psum(part.astype(bf16), dp).astype(f32)
        for part in (query_weight, key_weight, value_weight, out_grad)
    ]
    router_total, gain_one_total, gain_two_total = (
        lax.psum(part.astype(bf16), everyone).astype(f32)
        for part in (router_part, gain_one_part, gain_two_part)
    )
    return (
        block_output,
        input_grad,
        gain_one_total,
        summed[0],
        summed[1],
        summed[2],
        summed[3],
        gain_two_total,
        router_total,
        grad_gate,
        grad_up,
        grad_down,
    )


def solution(mesh):
    dp_count, tensor_count = mesh.devices.shape
    mesh = jax.sharding.Mesh(
        mesh.devices.reshape(dp_count // 2, 2, tensor_count // 2, 2), ("z", "y", "x", "c")
    )
    fast = mesh.devices.shape == (4, 2, 2, 2)
    dp = ("z", "y")
    tensor = ("x", "c")
    both = dp + tensor
    return jax.shard_map(
        per_device_fast if fast else per_device_general,
        mesh=mesh,
        in_specs=(
            P(dp, None),
            P(dp),
            P(),
            P(None, tensor),
            P(None, tensor),
            P(None, tensor),
            P(tensor, None),
            P(),
            P(),
            P(both, None),
            P(both, None),
            P(dp, None, tensor),
            P(dp, None, tensor),
            P(dp, tensor, None),
            P(both, None),
        ),
        out_specs=(
            P(both, None),
            P(dp, None),
            P(),
            P(None, tensor),
            P(None, tensor),
            P(None, tensor),
            P(tensor, None),
            P(),
            P(),
            P(dp, None, tensor),
            P(dp, None, tensor),
            P(dp, tensor, None),
        ),
        check_vma=False,
    )
```

```python
import functools

import jax
import jax.numpy as jnp
import numpy as np
from jax import lax
from jax.experimental import pallas as pl
from jax.experimental.pallas import tpu as pltpu
from jax.sharding import PartitionSpec as P

HD = 64
EXPERTS = 32
TOPK = 8


EPSILON = 1e-06
THETA_BASE = 10000.0
HIGHEST = lax.Precision.HIGHEST


def rope_tables(length, width_in):
    half_width = width_in // 2
    frequency = THETA_BASE ** (-(jnp.arange(half_width, dtype=jnp.float32) / half_width))
    angles = jnp.arange(length, dtype=jnp.float32)[:, None] * frequency[None, :]
    return (jnp.cos(angles), jnp.sin(angles))


def rotate(vectors, cosine, sine, direction):
    half_width = vectors.shape[-1] // 2
    front_half = vectors[..., :half_width]
    back_half = vectors[..., half_width:]
    cos_part = cosine[:, None, :]
    sin_part = sine[:, None, :] * direction
    return jnp.concatenate(
        [
            front_half * cos_part - back_half * sin_part,
            back_half * cos_part + front_half * sin_part,
        ],
        -1,
    )


NT = (((1,), (1,)), ((), ()))
TN = (((0,), (0,)), ((), ()))
f32 = jnp.float32
bf16 = jnp.bfloat16
BQ = 512
BK = 1024
BK_BACK = 512

def from_hbm(*arrays):
    return [pltpu.with_memory_space_constraint(a, pltpu.HBM) for a in arrays]


def busy(us):
    return pl.CostEstimate(flops=int(us * 1e8), bytes_accessed=0, transcendentals=0)


def lanes(shape):
    return lax.broadcasted_iota(jnp.int32, shape, len(shape) - 1)

def rope_wide(v, cos, sin):
    low = lanes(v.shape) % HD < HD // 2
    swapped = jnp.where(low, pltpu.roll(v, 128 - HD // 2, 1), pltpu.roll(v, HD // 2, 1))
    return v * cos + swapped * sin

def project_kernel(x_ref, gain_ref, wq_ref, wk_ref, wv_ref, cos_ref, sin_ref, a_ref, q_ref, k_ref, v_ref):
    x = x_ref[...].astype(f32)
    r = lax.rsqrt(jnp.mean(x * x, -1, keepdims=True) + EPSILON)
    a = (x * r * gain_ref[...].astype(f32)).astype(bf16)
    a_ref[...] = a
    cos, sin = cos_ref[...], sin_ref[...]
    k = jnp.dot(a, wk_ref[...], preferred_element_type=f32)
    k_ref[...] = rope_wide(k, cos, sin).astype(bf16)
    v = jnp.dot(a, wv_ref[...], preferred_element_type=f32).astype(bf16)
    v_ref[:, :128] = v
    v_ref[:, 128:] = jnp.ones_like(v)
    low = lanes(k.shape) < HD
    for pair in range(2):
        q = jnp.dot(a, wq_ref[:, pair * 128 : pair * 128 + 128], preferred_element_type=f32)
        q = rope_wide(q, cos, sin) * HD ** (-0.5)
        other = pltpu.roll(q, HD, 1)
        mine = low if pair == 0 else ~low
        first, second = (q, other) if pair == 0 else (other, q)
        q_ref[2 * pair] = jnp.where(mine, first, 0.0).astype(bf16)
        q_ref[2 * pair + 1] = jnp.where(mine, second, 0.0).astype(bf16)

def project(tokens, gain, wq, wk, wv, cos, sin):
    L, D = tokens.shape
    B = 256
    full = lambda a: pl.BlockSpec(a.shape, lambda i: (0,) * a.ndim)
    rows = lambda w: pl.BlockSpec((B, w), lambda i: (i, 0))
    return pl.pallas_call(
        project_kernel, grid=(L // B,),
        in_specs=[rows(D), full(gain), full(wq), full(wk), full(wv), rows(128), rows(128)],
        out_specs=[rows(D), pl.BlockSpec((4, B, 128), lambda i: (0, i, 0)), rows(128), rows(256)],
        out_shape=[pltpu.HBM((L, D), bf16), pltpu.HBM((4, L, 128), bf16), pltpu.HBM((L, 128), bf16), pltpu.HBM((L, 256), bf16)],
        compiler_params=pltpu.CompilerParams(vmem_limit_bytes=40 << 20),
        cost_estimate=busy(9),
        name="project",
    )(*from_hbm(tokens), gain, wq, wk, wv, cos, sin)

def attend_kernel(bq, bk, kv, prefix_ref, q_ref, k_ref, v_ref, *refs):
    o_ref, lse_ref, s_ref = refs[-3:]
    i = pl.program_id(0)
    start = i * bq
    prefix = prefix_ref[0]
    full_blocks = jnp.maximum(start + 1, prefix) // bk
    all_blocks = (jnp.maximum(start + bq, prefix) + bk - 1) // bk
    rows = 2 * bq
    pos = start + lax.broadcasted_iota(jnp.int32, (rows, 1), 0) % bq
    limit = jnp.maximum(pos, prefix - 1)
    low = lanes((bq, 128)) < HD
    q = jnp.concatenate([q_ref[0], q_ref[1]], 0)

    def tile_max(s, peak):
        for c in range(bk // 128):
            peak = jnp.maximum(peak, s[:, c * 128 : c * 128 + 128])
        return peak

    def plain(j, peak):
        off = pl.multiple_of(j * bk, bk)
        s = lax.dot_general(q, k_ref[pl.ds(off, bk), :], NT, preferred_element_type=f32)
        s_ref[:, pl.ds(off, bk)] = s
        return tile_max(s, peak)

    def masked(j, peak):
        off = pl.multiple_of(j * bk, bk)
        s = lax.dot_general(q, k_ref[pl.ds(off, bk), :], NT, preferred_element_type=f32)
        s = jnp.where(lanes((rows, bk)) <= limit - off, s, -1e30)
        s_ref[:, pl.ds(off, bk)] = s
        return tile_max(s, peak)

    peak = jnp.full((rows, 128), -1e30, f32)
    peak = lax.fori_loop(0, full_blocks, plain, peak)
    peak = lax.fori_loop(full_blocks, all_blocks, masked, peak)
    peak = jnp.max(peak, -1, keepdims=True)

    def weigh(j, acc):
        off = pl.multiple_of(j * bk, bk)
        p = jnp.exp(s_ref[:, pl.ds(off, bk)] - peak).astype(bf16)
        return acc + jnp.dot(p, v_ref[pl.ds(off, bk), :], preferred_element_type=f32)

    acc = lax.fori_loop(0, all_blocks, weigh, jnp.zeros((rows, 256), f32))
    total = acc[:, 128:]
    out = acc[:, :128] / total
    one, two = out[:bq], out[bq:]
    if kv == 0:
        merged = jnp.where(low, one, pltpu.roll(two, HD, 1))
    else:
        merged = jnp.where(low, pltpu.roll(one, HD, 1), two)
    o_ref[...] = merged.astype(bf16)
    lse = (peak + jnp.log(total)).T
    lse_ref[0] = lse[:8]


def attend(prefix, q, k, v, kv, bq, bk, before=()):
    L = k.shape[0]
    return pl.pallas_call(
        functools.partial(attend_kernel, bq, bk, kv),
        grid_spec=pltpu.PrefetchScalarGridSpec(
            num_scalar_prefetch=1, grid=(L // bq,),
            in_specs=[pl.BlockSpec((2, bq, 128), lambda i, p: (kv, i, 0)),
                      pl.BlockSpec((L, 128), lambda i, p: (0, 0)),
                      pl.BlockSpec((L, 256), lambda i, p: (0, 0))]
            + [pl.BlockSpec(memory_space=pl.ANY)] * len(before),
            out_specs=[pl.BlockSpec((bq, 128), lambda i, p: (i, kv)),
                       pl.BlockSpec((1, 8, 2 * bq), lambda i, p: (kv, 0, i))],
            scratch_shapes=[pltpu.VMEM((2 * bq, L), f32)]),
        out_shape=[pltpu.HBM((L, 256), bf16), pltpu.HBM((2, 8, 2 * L), f32)],
        input_output_aliases={4 + i: i for i in range(len(before))},
        compiler_params=pltpu.CompilerParams(vmem_limit_bytes=48 << 20),
        cost_estimate=busy(14),
        name="attend",
    )(prefix, *from_hbm(q, k, v), *before)


def attend_back_kernel(bq, bk, prefix_ref, q_ref, k_ref, v_ref, o_ref, do_ref, lse_ref, cos_ref, sin_ref, cosa_ref, sina_ref,
                       out_ref, dk_acc, dv_acc, dq_acc):
    i = pl.program_id(0)
    start = i * bq
    prefix = prefix_ref[0]
    full_blocks = jnp.maximum(start + 1, prefix) // bk
    all_blocks = (jnp.maximum(start + bq, prefix) + bk - 1) // bk
    rows = 2 * bq
    pos = start + lax.broadcasted_iota(jnp.int32, (1, rows), 1) % bq
    limit = jnp.maximum(pos, prefix - 1)
    low = lanes((bq, 128)) < HD

    @pl.when(i == 0)
    def _():
        dk_acc[...] = jnp.zeros_like(dk_acc)
        dv_acc[...] = jnp.zeros_like(dv_acc)

    heads = []
    for kv in range(2):
        q = jnp.concatenate([q_ref[2 * kv], q_ref[2 * kv + 1]], 0)
        mine = low if kv == 0 else ~low
        pair = do_ref[:, kv * 128 : kv * 128 + 128].astype(f32)
        swap = pltpu.roll(pair, HD, 1)
        first, second = (pair, swap) if kv == 0 else (swap, pair)
        do = jnp.concatenate([jnp.where(mine, first, 0.0), jnp.where(mine, second, 0.0)], 0).astype(bf16)
        prod = pair * o_ref[:, kv * 128 : kv * 128 + 128].astype(f32)
        one = jnp.sum(jnp.where(low, prod, 0.0), -1, keepdims=True)
        two = jnp.sum(jnp.where(low, 0.0, prod), -1, keepdims=True)
        center = jnp.broadcast_to(jnp.concatenate([one, two], 0), (rows, 128)).T[:1]
        heads.append((q, do, center, lse_ref[kv, :1, :]))
    dq_acc[...] = jnp.zeros_like(dq_acc)

    def step(j, _, mask):
        off = pl.multiple_of(j * bk, bk)
        kb = k_ref[pl.ds(off, bk), :]
        vb = v_ref[pl.ds(off, bk), :128]
        dvs, dks = [], []
        for kv, (q, do, center, lse) in enumerate(heads):
            s = lax.dot_general(kb, q, NT, preferred_element_type=f32)
            dp = lax.dot_general(vb, do, NT, preferred_element_type=f32)
            if mask:
                s = jnp.where(off + lax.broadcasted_iota(jnp.int32, (bk, rows), 0) <= limit, s, -1e30)
            p = jnp.exp(s - lse)
            ds = (p * (dp - center)).astype(bf16)
            dvs.append(jnp.dot(p.astype(bf16), do, preferred_element_type=f32))
            dks.append(jnp.dot(ds, q, preferred_element_type=f32))
            dq_acc[kv] += lax.dot_general(ds, kb, TN, preferred_element_type=f32)
        dv_acc[pl.ds(off, bk), :] += dvs[0] + dvs[1]
        dk_acc[pl.ds(off, bk), :] += dks[0] + dks[1]
        return 0

    lax.fori_loop(0, full_blocks, functools.partial(step, mask=False), 0)
    lax.fori_loop(full_blocks, all_blocks, functools.partial(step, mask=True), 0)
    for kv in range(2):
        dq = dq_acc[kv] * HD ** (-0.5)
        one, two = dq[:bq], dq[bq:]
        if kv == 0:
            merged = jnp.where(low, one, pltpu.roll(two, HD, 1))
        else:
            merged = jnp.where(low, pltpu.roll(one, HD, 1), two)
        out_ref[pl.ds(pl.multiple_of(start, bq), bq), kv * 128 : kv * 128 + 128] = rope_wide(merged, cos_ref[...], -sin_ref[...]).astype(bf16)

    @pl.when(i == pl.num_programs(0) - 1)
    def _():
        for b in range(dk_acc.shape[0] // bq):
            r = pl.ds(b * bq, bq)
            out_ref[r, 256:384] = rope_wide(dk_acc[r, :], cosa_ref[r, :], -sina_ref[r, :]).astype(bf16)
            out_ref[r, 384:] = dv_acc[r, :].astype(bf16)

def attend_back(prefix, q, k, v, o, do, lse, cos, sin, bq=256, bk=256):
    L = k.shape[0]
    fullL = pl.BlockSpec((L, 128), lambda i, p: (0, 0))
    return pl.pallas_call(
        functools.partial(attend_back_kernel, bq, bk),
        grid_spec=pltpu.PrefetchScalarGridSpec(
            num_scalar_prefetch=1, grid=(L // bq,),
            in_specs=[pl.BlockSpec((4, bq, 128), lambda i, p: (0, i, 0)), fullL,
                      pl.BlockSpec((L, 256), lambda i, p: (0, 0)),
                      pl.BlockSpec((bq, 256), lambda i, p: (i, 0)),
                      pl.BlockSpec((bq, 256), lambda i, p: (i, 0)),
                      pl.BlockSpec((2, 8, 2 * bq), lambda i, p: (0, 0, i)),
                      pl.BlockSpec((bq, 128), lambda i, p: (i, 0)),
                      pl.BlockSpec((bq, 128), lambda i, p: (i, 0)), fullL, fullL],
            out_specs=pl.BlockSpec((L, 512), lambda i, p: (0, 0)),
            scratch_shapes=[pltpu.VMEM((L, 128), f32), pltpu.VMEM((L, 128), f32), pltpu.VMEM((2, 2 * bq, 128), f32)]),
        out_shape=jax.ShapeDtypeStruct((L, 512), bf16),
        compiler_params=pltpu.CompilerParams(vmem_limit_bytes=48 << 20),
        cost_estimate=busy(46),
        name="attend_back",
    )(prefix, q, k, v, o, do, lse, cos, sin, cos, sin)


def pick_kernel(experts, per, cap, pairs, shift_ref, *refs):
    in_ref, dyo_ref, gs_ref, gate_ref, code_ref, code_t, gate_t, rows_s, dy_s = refs[-9:]
    tokens, width = rows_s.shape

    @pl.when(pl.program_id(0) == 0)
    def _():
        if pairs:
            rows_ref, rows_other, side_ref, side_other, router_ref = refs[:5]
            first = shift_ref[experts] != 0
            rows = jnp.where(first, rows_ref[...], rows_other[...])
            side = jnp.where(first, side_ref[...], side_other[...])
        else:
            rows_ref, side_ref, router_ref = refs[:3]
            rows, side = rows_ref[...], side_ref[...]
        rows_s[...] = rows
        dy_s[...] = side[:, :width]
        code = side[:, width:].astype(f32)
        code_ref[...] = code
        logits = jnp.dot(rows, router_ref[...], preferred_element_type=f32)
        chosen = jnp.where(code >= 0, logits, -1e30)
        raised = jnp.where(code >= 0, jnp.exp(chosen - jnp.max(chosen, -1, keepdims=True)), 0.0)
        gate = raised / jnp.sum(raised, -1, keepdims=True)
        gate_ref[...] = gate
        gate_t[...] = gate.T
        code_t[...] = code.T

    hots = []
    for e in range(per):
        row = pl.ds(shift_ref[pl.program_id(0) * per + e], 1)
        hot = code_t[row, :] == lax.broadcasted_iota(jnp.int32, (cap, tokens), 0).astype(f32)
        gs = jnp.sum(jnp.where(hot, gate_t[row, :], 0.0), -1, keepdims=True)
        gs_ref[e] = jnp.broadcast_to(gs, (cap, 128))
        hots.append(hot.astype(bf16))
    hot = jnp.concatenate(hots, 0)
    in_ref[...] = jnp.dot(hot, rows_s[...], preferred_element_type=f32).astype(bf16).reshape(in_ref.shape)
    dyo_ref[...] = jnp.dot(hot, dy_s[...], preferred_element_type=f32).astype(bf16).reshape(dyo_ref.shape)


def pick(shift, rows, sides, router, cap):
    R, D = rows[0].shape
    E = shift.shape[0] - 1
    W = router.shape[1]
    per = 2
    operands = [*rows, *sides, router]
    whole = lambda a: pl.BlockSpec(a.shape, lambda e: (0, 0))
    some = lambda w: pl.BlockSpec((per, cap, w), lambda e: (e, 0, 0))
    wide = pl.BlockSpec((R, W), lambda e: (0, 0))
    return pl.pallas_call(
        functools.partial(pick_kernel, E, per, cap, len(rows) == 2),
        grid=(E // per,),
        in_specs=[pl.BlockSpec(memory_space=pltpu.SMEM)] + [whole(a) for a in operands],
        out_specs=[some(D), some(D), some(128), wide, wide],
        out_shape=[pltpu.HBM((E, cap, D), bf16), pltpu.HBM((E, cap, D), bf16),
                   pltpu.HBM((E, cap, 128), f32), jax.ShapeDtypeStruct((R, W), f32), jax.ShapeDtypeStruct((R, W), f32)],
        scratch_shapes=[pltpu.VMEM((W, R), f32), pltpu.VMEM((W, R), f32), pltpu.VMEM((R, D), bf16), pltpu.VMEM((R, D), bf16)],
        compiler_params=pltpu.CompilerParams(vmem_limit_bytes=40 << 20),
        cost_estimate=busy(4),
        name="pick",
    )(shift, *operands)


def ffn_kernel(n, blocks, *refs):
    rows_refs, dy_refs, gs_refs = refs[:n], refs[n : 2 * n], refs[2 * n : 3 * n]
    w_ref = refs[3 * n]
    eout_ref, drows_ref, dgs_ref, act_ref, dgu_ref = refs[-5:]
    cap, D = rows_refs[0].shape[1:]
    M = n * cap
    rows = jnp.concatenate([r[0] for r in rows_refs], 0)
    dy = jnp.concatenate([r[0] for r in dy_refs], 0)
    gs = jnp.concatenate([r[0] for r in gs_refs], 0)
    dout = (dy.astype(f32) * gs[:, :1]).astype(bf16)
    F = w_ref.shape[-1]
    eout = jnp.zeros((M, D), f32)
    drows = jnp.zeros((M, D), f32)
    for pair in range(0, blocks, 2):
        acts = []
        wd2 = jnp.concatenate([w_ref[0, pair, 2, 0], w_ref[0, pair + 1, 2, 0]], 1)
        dact2 = jnp.dot(dout, wd2, preferred_element_type=f32)
        for b in (pair, pair + 1):
            w = jnp.concatenate([w_ref[0, b, 0, 0], w_ref[0, b, 1, 0]], 1)
            gu = jnp.dot(rows, w, preferred_element_type=f32)
            g, u = gu[:, :F], gu[:, F:]
            sg = 1.0 / (1.0 + jnp.exp(-g))
            gsg = g * sg
            acts.append((gsg * u).astype(bf16))
            dact = dact2[:, (b - pair) * F : (b - pair + 1) * F]
            dg = dact * u * (sg + gsg * (1.0 - sg))
            du = dact * gsg
            dgu = jnp.concatenate([dg, du], 1).astype(bf16)
            dgu_ref[0, :, b * 2 * F : (b + 1) * 2 * F] = dgu
            drows = drows + lax.dot_general(dgu, w, NT, preferred_element_type=f32)
        act = jnp.concatenate(acts, 1)
        act_ref[0, :, pair * F : (pair + 2) * F] = act
        eout = eout + lax.dot_general(act, wd2, NT, preferred_element_type=f32)
    eout = eout.astype(bf16)
    eout_ref[0] = eout
    drows_ref[0] = drows.astype(bf16)
    dgs = jnp.sum(dy.astype(f32) * eout.astype(f32), -1, keepdims=True)
    dgs_ref[0] = jnp.broadcast_to(dgs, (M, 128))


def ffn(picked, weights, groups, before=()):
    n = len(picked)
    total, cap, D = picked[0][0].shape
    _, blocks, _, E, _, F = weights.shape
    H = blocks * F
    M = n * cap
    first = groups[0] * E
    spec = lambda w: pl.BlockSpec((1, cap, w), lambda e: (e + first, 0, 0))
    outs = lambda w: pl.BlockSpec((1, M, w), lambda e: (e + first, 0, 0))
    wsp = pl.BlockSpec((1, blocks, 3, 1, D, F), lambda e: ((e + first) // E, 0, 0, (e + first) % E, 0, 0))
    sh = lambda w, t: pltpu.HBM((total, M, w), t)
    operands = [p[i] for i in range(3) for p in picked] + [weights]
    return pl.pallas_call(
        functools.partial(ffn_kernel, n, blocks), grid=(len(groups) * E,),
        in_specs=[spec(D)] * (2 * n) + [spec(128)] * n + [wsp] + [pl.BlockSpec(memory_space=pl.ANY)] * len(before),
        out_specs=[outs(D), outs(D), outs(128), outs(H), outs(2 * H)],
        out_shape=[sh(D, bf16), sh(D, bf16), sh(128, f32), sh(H, bf16), sh(2 * H, bf16)],
        input_output_aliases={len(operands) + i: i for i in range(len(before))},
        compiler_params=pltpu.CompilerParams(vmem_limit_bytes=56 << 20),
        cost_estimate=busy(12 * len(groups)),
        name="ffn",
    )(*operands, *before)


def wgrad_kernel(n, halves, blocks, *refs):
    rows_refs, dy_refs, gs_refs = refs[:n], refs[n : 2 * n], refs[2 * n : 3 * n]
    act_refs, dgu_refs, out_ref = refs[3 * n : 3 * n + halves], refs[3 * n + halves : 3 * n + 2 * halves], refs[-1]
    rows = jnp.concatenate([r[0] for r in rows_refs], 0)
    dy = jnp.concatenate([r[0] for r in dy_refs], 0)
    gs = jnp.concatenate([r[0] for r in gs_refs], 0)
    dout = (dy.astype(f32) * gs[:, :1]).astype(bf16)
    F = act_refs[0].shape[2] // blocks
    for b in range(blocks):
        dgu = jnp.concatenate([r[0, :, b * 2 * F : (b + 1) * 2 * F] for r in dgu_refs], 0)
        g = lax.dot_general(rows, dgu, TN, preferred_element_type=f32).astype(bf16)
        out_ref[0, b, 0, 0] = g[:, :F]
        out_ref[0, b, 1, 0] = g[:, F:]
    for pair in range(0, blocks, 2):
        act = jnp.concatenate([r[0, :, pair * F : (pair + 2) * F] for r in act_refs], 0)
        gd = lax.dot_general(dout, act, TN, preferred_element_type=f32).astype(bf16)
        out_ref[0, pair, 2, 0] = gd[:, :F]
        out_ref[0, pair + 1, 2, 0] = gd[:, F:]


def wgrad(picked, acts, dgus, blocks, groups, group, before=()):
    n = len(picked)
    total, cap, D = picked[0][0].shape
    H = acts[0].shape[2]
    F = H // blocks
    E = total // groups
    spec = lambda w: pl.BlockSpec((1, cap, w), lambda e: (e + group * E, 0, 0))
    wide = lambda a: pl.BlockSpec((1,) + a.shape[1:], lambda e: (e + group * E, 0, 0))
    operands = [*[p[i] for i in range(3) for p in picked], *acts, *dgus]
    return pl.pallas_call(
        functools.partial(wgrad_kernel, n, len(acts), blocks),
        grid=(E,),
        in_specs=[spec(D)] * (2 * n) + [spec(128)] * n + [wide(a) for a in (*acts, *dgus)]
        + [pl.BlockSpec(memory_space=pl.ANY)] * len(before),
        out_specs=pl.BlockSpec((1, blocks, 3, 1, D, F), lambda e: (group, 0, 0, e, 0, 0)),
        out_shape=pltpu.HBM((groups, blocks, 3, E, D, F), bf16),
        input_output_aliases={len(operands) + i: i for i in range(len(before))},
        compiler_params=pltpu.CompilerParams(vmem_limit_bytes=56 << 20),
        cost_estimate=busy(13),
        name="wgrad",
    )(*operands, *before)


def hot_columns(code, shift, cap):
    col = jnp.sum(jnp.where(lanes(code.shape) == shift, code, 0.0), -1, keepdims=True)
    return col == lanes((code.shape[0], cap)).astype(f32)


def merge_back_kernel(n, E, cap, shift_ref, *refs):
    sides, (d_ref, g_ref), outs = refs[:n], refs[n : n + 2], refs[n + 2 :]
    D = d_ref.shape[2]
    lane = lanes((cap, 128))
    for source in range(n):

        @pl.when(pl.program_id(0) == source)
        def _():
            code = sides[source][...]
            total = jnp.zeros((code.shape[0], D), f32)
            gates = jnp.zeros((code.shape[0], 128), f32)
            for e0 in range(0, E, 4):
                some = range(e0, min(e0 + 4, E))
                hot = jnp.concatenate([hot_columns(code, shift_ref[e], cap).astype(bf16) for e in some], 1)
                rows = jnp.concatenate([d_ref[e] for e in some], 0)
                side = jnp.concatenate([jnp.where(lane == shift_ref[e], g_ref[e], 0.0).astype(bf16) for e in some], 0)
                total = total + jnp.dot(hot, rows, preferred_element_type=f32)
                gates = gates + jnp.dot(hot, side, preferred_element_type=f32)
            outs[source][:, :D] = total.astype(bf16)
            outs[source][:, D:] = gates.astype(bf16)


def merge_back(shift, codes, drows, dgs, cap):
    n = len(codes)
    R, W = codes[0].shape
    E, _, D = drows.shape
    part = lambda w: pl.BlockSpec((E, cap, w), lambda i: (0, i, 0))
    whole = lambda w: pl.BlockSpec((R, w), lambda i: (0, 0))
    return pl.pallas_call(
        functools.partial(merge_back_kernel, n, E, cap),
        grid=(n,),
        in_specs=[pl.BlockSpec(memory_space=pltpu.SMEM)] + [whole(W)] * n + [part(D), part(128)],
        out_specs=[whole(D + 128)] * n,
        out_shape=[jax.ShapeDtypeStruct((R, D + 128), bf16)] * n,
        compiler_params=pltpu.CompilerParams(vmem_limit_bytes=48 << 20),
        cost_estimate=busy(3 * n),
        name="merge_back",
    )(shift, *codes, drows, dgs)


def merge_out_kernel(n, E, cap, shift_ref, *refs):
    sides, gates, e_ref, outs = refs[:n], refs[n : 2 * n], refs[2 * n], refs[2 * n + 1 :]
    D = e_ref.shape[2]
    for source in range(n):

        @pl.when(pl.program_id(0) == source)
        def _():
            code = sides[source][...]
            gate = gates[source][...]
            total = jnp.zeros((code.shape[0], D), f32)
            for e0 in range(0, E, 4):
                some = range(e0, min(e0 + 4, E))
                parts = []
                for e in some:
                    g = jnp.sum(jnp.where(lanes(gate.shape) == shift_ref[e], gate, 0.0), -1, keepdims=True)
                    parts.append(jnp.where(hot_columns(code, shift_ref[e], cap), g, 0.0).astype(bf16))
                rows = jnp.concatenate([e_ref[e] for e in some], 0)
                total = total + jnp.dot(jnp.concatenate(parts, 1), rows, preferred_element_type=f32)
            outs[source][...] = total.astype(bf16)


def merge_out(shift, codes, gates, eout, cap):
    n = len(codes)
    R, W = codes[0].shape
    E, _, D = eout.shape
    whole = lambda w: pl.BlockSpec((R, w), lambda i: (0, 0))
    return pl.pallas_call(
        functools.partial(merge_out_kernel, n, E, cap),
        grid=(n,),
        in_specs=[pl.BlockSpec(memory_space=pltpu.SMEM)] + [whole(W)] * (2 * n)
        + [pl.BlockSpec((E, cap, D), lambda i: (0, i, 0))],
        out_specs=[whole(D)] * n,
        out_shape=[jax.ShapeDtypeStruct((R, D), bf16)] * n,
        compiler_params=pltpu.CompilerParams(vmem_limit_bytes=48 << 20),
        cost_estimate=busy(11),
        name="merge_out",
    )(shift, *codes, *gates, eout)


def finish_kernel(core_ref, sum_ref, x_ref, dh_ref, gain_ref, *refs):
    out_ref = refs[-1]
    x = x_ref[...].astype(f32)
    r = lax.rsqrt(jnp.mean(x * x, -1, keepdims=True) + EPSILON)
    scaled = sum_ref[...].astype(f32) * gain_ref[...].astype(f32)
    out_ref[...] = dh_ref[...].astype(f32) + r * scaled - x * (r * r * r * jnp.mean(scaled * x, -1, keepdims=True))


def finish(core, summed, tokens, hidden, gain, rows, before=()):
    L, D = tokens.shape
    half = rows // 2
    place = lambda i, p: ((i // 2) * 4 + p[0] * 2 + i % 2, 0)
    return pl.pallas_call(
        finish_kernel,
        grid_spec=pltpu.PrefetchScalarGridSpec(
            num_scalar_prefetch=1, grid=(L // rows,),
            in_specs=[pl.BlockSpec((half, D), lambda i, p: (i, 0)), pl.BlockSpec((half, D), place), pl.BlockSpec((half, D), place),
                      pl.BlockSpec((1, D), lambda i, p: (0, 0))] + [pl.BlockSpec(memory_space=pl.ANY)] * len(before),
            out_specs=pl.BlockSpec((half, D), place)),
        out_shape=jax.ShapeDtypeStruct((L, D), f32),
        input_output_aliases={5 + i: i for i in range(len(before))},
        compiler_params=pltpu.CompilerParams(vmem_limit_bytes=48 << 20),
        cost_estimate=busy(4),
        name="finish",
    )(core, summed, tokens, hidden, gain, *before)


def spread_kernel(n, more, rank_ref, att_ref, w_ref, *refs):
    blocks = refs[:n]
    hidden_ref, do_ref, og_ref = refs[-3:]
    i = pl.program_id(0)

    @pl.when(i == 0)
    def _():
        og_ref[...] = refs[n][...] if more else jnp.zeros_like(og_ref)

    for b in range(n):

        @pl.when(i == b)
        def _():
            block = blocks[b][...]
            hidden_ref[...] = block
            do_ref[...] = lax.dot_general(block, w_ref[...], NT, preferred_element_type=f32).astype(bf16)
            og_ref[...] += lax.dot_general(att_ref[...], block, TN, preferred_element_type=f32)


def spread(rank, first, blocks, attended, w_out, before=None):
    n = len(blocks)
    R, D = blocks[0].shape
    L, H = attended.shape
    place = lambda i, p: (p[0] ^ (i + first), 0)
    whole = lambda a: pl.BlockSpec(a.shape, lambda i, p: (0, 0))
    total = jax.ShapeDtypeStruct((H, D), f32)
    operands = [attended, w_out, *blocks]
    specs = [pl.BlockSpec((R, H), place), whole(w_out)] + [whole(b) for b in blocks]
    aliases = {}
    if before is not None:
        hidden, do, og = before
        operands += [og, hidden, do]
        specs += [whole(og)] + [pl.BlockSpec(memory_space=pl.ANY)] * 2
        aliases = {len(operands) - 1: 0, len(operands): 1}
    return pl.pallas_call(
        functools.partial(spread_kernel, n, before is not None),
        grid_spec=pltpu.PrefetchScalarGridSpec(
            num_scalar_prefetch=1, grid=(n,), in_specs=specs,
            out_specs=[pl.BlockSpec((R, D), place), pl.BlockSpec((R, H), place), whole(total)]),
        out_shape=[pltpu.HBM((L, D), bf16), pltpu.HBM((L, H), bf16), total],
        input_output_aliases=aliases,
        compiler_params=pltpu.CompilerParams(vmem_limit_bytes=32 << 20),
        cost_estimate=busy(3),
        name="spread",
    )(rank, *operands)


def grads_kernel(parts_ref, gate_ref, up_ref, down_ref):
    gate_ref[0] = parts_ref[0, 0].astype(f32)
    up_ref[0] = parts_ref[1, 0].astype(f32)
    down_ref[0] = parts_ref[2, 0].astype(f32).T


def expert_grads(parts):
    _, E, D, F = parts.shape
    one = lambda *s: pl.BlockSpec((1,) + s, lambda e: (e, 0, 0))
    return pl.pallas_call(
        grads_kernel,
        grid=(E,),
        in_specs=[pl.BlockSpec((3, 1, D, F), lambda e: (0, e, 0, 0))],
        out_specs=[one(D, F), one(D, F), one(F, D)],
        out_shape=[pltpu.HBM((E, D, F), f32), pltpu.HBM((E, D, F), f32), pltpu.HBM((E, F, D), f32)],
        compiler_params=pltpu.CompilerParams(vmem_limit_bytes=32 << 20),
        cost_estimate=busy(4),
        name="expert_grads",
    )(parts)


def out_kernel(rank_ref, a_ref, b_ref, w_ref, keep_ref, send_ref):
    keep_ref[...] = jnp.dot(a_ref[...], w_ref[...], preferred_element_type=f32)
    send_ref[...] = jnp.dot(b_ref[...], w_ref[...], preferred_element_type=f32).astype(bf16)


def out_pair(rank, bits, attended, w_out, rows):
    H, D = w_out.shape
    step = min(256, rows)
    n = rows // step
    block = lambda bit: pl.BlockSpec((step, H), lambda i, p: ((p[0] ^ bit) * n + i, 0))
    out = pl.BlockSpec((step, D), lambda i, p: (i, 0))
    return pl.pallas_call(
        out_kernel,
        grid_spec=pltpu.PrefetchScalarGridSpec(
            num_scalar_prefetch=1, grid=(n,),
            in_specs=[block(bits[0]), block(bits[1]), pl.BlockSpec((H, D), lambda i, p: (0, 0))],
            out_specs=[out, out]),
        out_shape=[jax.ShapeDtypeStruct((rows, D), f32), jax.ShapeDtypeStruct((rows, D), bf16)],
        compiler_params=pltpu.CompilerParams(vmem_limit_bytes=32 << 20),
        cost_estimate=busy(3),
        name="out_pair",
    )(rank, attended, attended, w_out)


def swap(x, axis, bit=1):
    count = lax.axis_size(axis)
    return lax.ppermute(x, axis, [(i, i ^ bit) for i in range(count)])


def total_over(x, axes):
    for axis in axes:
        bit = 1
        while bit < lax.axis_size(axis):
            low = x.astype(bf16)
            x = low.astype(f32) + swap(low, axis, bit).astype(f32)
            bit *= 2
    return x


def wide_tables(length):
    half = HD // 2
    angles = np.arange(length)[:, None] * THETA_BASE ** (-(np.arange(half) / half))[None, :]
    cos, sin = np.cos(angles), np.sin(angles)
    return (
        jnp.asarray(np.concatenate([cos, cos, cos, cos], 1), f32),
        jnp.asarray(np.concatenate([-sin, sin, -sin, sin], 1), f32),
    )


NEAR = [(0, 1), (1, 0), (2, 3), (3, 2)]
MIDDLE = [(1, 2), (2, 1)]
TO_ENDS = [(1, 0), (2, 3)]
FROM_ENDS = [(0, 1), (3, 2)]


def line_first(x):
    return lax.ppermute(x, "z", NEAR), lax.ppermute(x, "z", MIDDLE)


def line_second(near, across):
    return lax.ppermute(near, "z", MIDDLE), lax.ppermute(across, "z", TO_ENDS)


def line_third(across_far):
    return lax.ppermute(across_far, "z", TO_ENDS)


def hold(*arrays):
    return lax.optimization_barrier(arrays)


def line_out(parts):
    return lax.ppermute(parts[3], "z", FROM_ENDS), lax.ppermute(parts[2], "z", FROM_ENDS)


def add_low(a, b):
    return (a.astype(f32) + b.astype(f32)).astype(a.dtype)


def line_over(part, from_end):
    return lax.ppermute(add_low(part, from_end), "z", MIDDLE)


def line_in(part, across_far):
    return lax.ppermute(add_low(part, across_far), "z", NEAR)


def line_sum(parts, from_end_far, from_end):
    own, near, two, three = parts
    across_far = line_over(two, from_end_far)
    across = line_over(three, from_end)
    got = line_in(near, across_far)
    return own.astype(f32) + across.astype(f32) + got.astype(f32)


def per_device_fast(
    tokens,
    prefix,
    gain_attn,
    w_query,
    w_key,
    w_value,
    w_out,
    gain_moe,
    w_router,
    routes,
    fill_order,
    w_gate,
    w_up,
    w_down,
    cotangent,
):
    z, y, x, c = (lax.axis_index(a) for a in ("z", "y", "x", "c"))
    shards = lax.axis_size("x") * lax.axis_size("c")
    groups = lax.axis_size("y")
    rank = x * lax.axis_size("c") + c
    at_end = (z == 0) | (z == lax.axis_size("z") - 1)
    length, width = tokens.shape
    own_rows = routes.shape[0]
    local = w_gate.shape[0]
    cap = own_rows * TOPK // EXPERTS

    expert_ids = jnp.arange(EXPERTS, dtype=jnp.int32)
    member = jnp.sum((routes[:, :, None] == expert_ids[None, None, :]).astype(f32), 1)
    priority = fill_order[0]
    earlier = (priority[None, :] < priority[:, None]).astype(bf16)
    slot_full = jnp.dot(earlier, member.astype(bf16), preferred_element_type=f32)
    code = jnp.where(member > 0, jnp.minimum(slot_full, float(cap)), -1.0).astype(bf16)
    code = jnp.pad(code, ((0, 0), (0, 128 - EXPERTS)), constant_values=-1)
    side_own = jnp.concatenate([cotangent, code], 1)
    side_near, side_across = line_first(side_own)
    router_wide = jnp.pad(w_router, ((0, 0), (0, 128 - EXPERTS)))
    shift = z * groups * local + jnp.arange(groups * local, dtype=jnp.int32)
    shift_end = jnp.concatenate([shift, at_end.astype(jnp.int32)[None]])


    own_weights = jnp.stack([w_gate, w_up, w_down.transpose(0, 2, 1)])
    weights = lax.all_gather(own_weights, ("y", "x", "c"), axis=0, tiled=False)
    weights = weights.reshape((groups, shards) + own_weights.shape)

    cos, sin = wide_tables(length)
    normed_one, query, key, value = project(tokens, gain_attn[None], w_query, w_key, w_value, cos, sin)
    first_half = attend(prefix, query, key, value, 0, BQ, BK)
    *first_half, side_near, side_across = hold(*first_half, side_near, side_across)
    side_far, side_relay = line_second(side_near, side_across)
    attended, log_total = attend(prefix, query, key, value, 1, BQ, BK, first_half)
    rank_row = rank.astype(jnp.int32)[None]
    far_keep, far_send = out_pair(rank_row, (2, 3), attended, w_out, own_rows)
    far_keep, side_far = hold(far_keep, side_far)
    side_last = line_third(side_far)
    far_sum = far_keep + swap(far_send, "c").astype(f32)
    far_got = swap(far_sum.astype(bf16), "x")
    near_keep, near_send = out_pair(rank_row, (0, 1), attended, w_out, own_rows)
    near_sum = near_keep + swap(near_send, "c").astype(f32)
    near_sum, far_got, side_relay, side_last = hold(near_sum, far_got, side_relay, side_last)
    x_rows = lax.dynamic_slice_in_dim(tokens, rank * own_rows, own_rows, 0).astype(f32)
    hidden_in = x_rows + near_sum + far_got.astype(f32)
    rms_two = lax.rsqrt(jnp.mean(hidden_in * hidden_in, -1, keepdims=True) + EPSILON)
    gain_two = gain_moe.astype(f32)
    normed_two = (hidden_in * rms_two * gain_two).astype(bf16)

    near, across = line_first(normed_two)

    def pick_of(rows, sides):
        return pick(shift_end, rows, sides, router_wide, cap)

    pick_own = pick_of((normed_two,), (side_own,))
    near, across, *pick_own = hold(near, across, *pick_own)
    far, relay = line_second(near, across)
    close = [pick_own, pick_of((near,), (side_near,))]
    half_close = ffn(close, weights, (0,))
    far, relay, *half_close = hold(far, relay, *half_close)
    last = line_third(far)
    done_close = ffn(close, weights, (1,), half_close)
    apart = [pick_of((relay, far), (side_relay, side_far))]
    last, *done_close = hold(last, *done_close)
    apart.append(pick_of((last, across), (side_last, side_across)))
    done_apart = ffn(apart, weights, (0, 1))
    picked = close + apart
    gates = [p[3] for p in picked]
    codes = [p[4] for p in picked]
    far_back = merge_back(shift, codes[2:], done_apart[1], done_apart[2], cap)
    back = [*merge_back(shift, codes[:2], done_close[1], done_close[2], cap), *far_back]
    back_end_far, back_end = line_out(back)
    late_act, *_ = hold(done_apart[3], *far_back)
    used = (done_close[3], late_act), (done_close[4], done_apart[4]), shards, groups
    parts = wgrad(picked, *used, 0)
    parts = wgrad(picked, *used, 1, (parts,))
    back_end_far, parts = hold(back_end_far, parts)
    across_far = line_over(back[2], back_end_far)
    across = line_over(back[3], back_end)
    late_close, late_apart, _ = hold(done_close[0], done_apart[0], across_far)
    out_parts = [
        *merge_out(shift, codes[:2], gates[:2], late_close, cap),
        *merge_out(shift, codes[2:], gates[2:], late_apart, cap),
    ]
    got = line_in(back[1], across_far)
    got, across, *out_parts = hold(got, across, *out_parts)
    back_own = back[0].astype(f32) + across.astype(f32) + got.astype(f32)
    out_end_far, out_end = line_out(out_parts)
    part_sum = lax.psum_scatter(
        parts.reshape((groups * shards,) + parts.shape[2:]), ("y", "x", "c"), scatter_dimension=0, tiled=False
    )

    gate_own = gates[0]
    gate_grad = back_own[:, width:]
    logit_grad = gate_own * (gate_grad - jnp.sum(gate_own * gate_grad, -1, keepdims=True))
    logit_low = logit_grad.astype(bf16)
    normed_two_grad = back_own[:, :width] + lax.dot_general(
        logit_low, router_wide, (((1,), (1,)), ((), ())), preferred_element_type=f32
    )
    router_part = lax.dot_general(
        logit_low, normed_two, (((0,), (0,)), ((), ())), preferred_element_type=f32
    )[:EXPERTS]
    gain_two_part = jnp.sum(normed_two_grad * hidden_in * rms_two, 0)
    scaled_two = normed_two_grad * gain_two
    hidden_grad = (
        cotangent.astype(f32)
        + rms_two * scaled_two
        - hidden_in * rms_two**3 * jnp.mean(scaled_two * hidden_in, -1, keepdims=True)
    ).astype(bf16)
    small = jnp.concatenate([router_part, gain_two_part[None], jnp.zeros((7, width), f32)], 0)
    hidden_over_x = swap(hidden_grad, "x")
    near_done = spread(rank_row, 0, [hidden_grad, swap(hidden_grad, "c")], attended, w_out)
    *near_done, out_end_far, out_end = hold(*near_done, out_end_far, out_end)
    out_two, out_three = add_low(out_parts[2], out_end_far), add_low(out_parts[3], out_end)
    hidden_over_x, out_two, out_three, *near_done = hold(hidden_over_x, out_two, out_three, *near_done)
    hidden_all, attended_grad, out_grad = spread(
        rank_row, 2, [hidden_over_x, swap(hidden_over_x, "c")], attended, w_out, near_done
    )
    attended_grad, small, out_low = hold(attended_grad, small, out_grad.astype(bf16))
    out_far, out_across = (lax.ppermute(part, "z", MIDDLE) for part in (out_two, out_three))
    heads_back = attend_back(
        prefix, query, key, value, attended, attended_grad, log_total, cos, sin, BQ, BK_BACK
    )
    heads_in = jnp.concatenate([w_query, w_key, w_value], 1)
    heads_grad = jnp.einsum("id,ih->dh", normed_one, heads_back, preferred_element_type=f32)
    low = jnp.concatenate([heads_grad.astype(bf16), out_low.reshape(-1, heads_grad.shape[1])], 0)
    gain_one_part = jnp.sum(heads_grad * heads_in.astype(f32), 1) / gain_attn.astype(f32)
    small = jnp.concatenate([small[: EXPERTS + 1], gain_one_part[None], small[EXPERTS + 2 :]], 0)
    heads_back, low, part_sum, out_far, out_across = hold(heads_back, low, part_sum, out_far, out_across)
    out_got = line_in(out_parts[1], out_far)

    low_part = lax.psum_scatter(low, ("z", "y"), scatter_dimension=0, tiled=True)

    by_core = heads_back.reshape(shards // 2, 2, own_rows, -1)

    def rows_of(which):
        rows = lax.dynamic_index_in_dim(by_core, which, 1, keepdims=False)
        return lax.dot_general(rows, heads_in, (((2,), (1,)), ((), ())), preferred_element_type=f32)

    from_core = swap(rows_of(1 - c).astype(bf16), "c")
    core_sum = (rows_of(c) + from_core.astype(f32)).astype(bf16)
    core_got, low_part, out_got, small = hold(swap(core_sum, "x"), low_part, out_got, small)
    rest = total_over(small, ("c", "x", "y", "z"))
    moe_own = out_parts[0].astype(f32) + out_across.astype(f32) + out_got.astype(f32)
    block_output = (hidden_in + moe_own).astype(bf16)
    low_all = lax.all_gather(low_part, ("z", "y"), axis=0, tiled=True)
    summed_grads = expert_grads(part_sum)
    chip_sum = (core_sum.astype(f32) + core_got.astype(f32)).astype(bf16)
    other_sum = swap(chip_sum, "c")
    core = c.astype(jnp.int32)[None]
    gain_row = gain_attn[None]
    input_grad = finish(core, chip_sum.reshape(-1, width), tokens, hidden_all, gain_row, own_rows)
    other_sum, input_grad, *summed_grads = hold(other_sum, input_grad, *summed_grads)
    input_grad = finish(
        1 - core, other_sum.reshape(-1, width), tokens, hidden_all, gain_row, own_rows, (input_grad,)
    )
    low_all, input_grad, block_output, rest = hold(low_all, input_grad, block_output, rest)
    low_all = low_all.astype(f32)
    heads_total = low_all[:width]
    out_total = low_all[width:].reshape(out_grad.shape)
    cut = w_query.shape[1]
    return (
        block_output,
        input_grad,
        rest[EXPERTS + 1],
        heads_total[:, :cut],
        heads_total[:, cut : cut + w_key.shape[1]],
        heads_total[:, cut + w_key.shape[1] :],
        out_total,
        rest[EXPERTS],
        rest[:EXPERTS].T,
        *summed_grads,
    )


def group_gather(x, axes):
    return lax.all_gather(x, axes, axis=0, tiled=False)


def per_device_general(
    tokens,
    prefix,
    gain_attn,
    w_query,
    w_key,
    w_value,
    w_out,
    gain_moe,
    w_router,
    routes,
    fill_order,
    w_gate,
    w_up,
    w_down,
    cotangent,
):
    f32 = jnp.float32
    bf16 = jnp.bfloat16
    z_count = lax.axis_size("z")
    y_count = lax.axis_size("y")
    shards = lax.axis_size("x") * lax.axis_size("c")
    z_rank = lax.axis_index("z")
    tensor_rank = lax.axis_index("x") * lax.axis_size("c") + lax.axis_index("c")
    length = tokens.shape[0]
    model_width = tokens.shape[1]
    own_rows = routes.shape[0]
    local_experts = w_gate.shape[0]
    group_experts = local_experts * y_count
    capacity = own_rows * TOPK // EXPERTS
    heads_local = w_query.shape[1] // HD
    kv_local = w_key.shape[1] // HD
    group_size = heads_local // kv_local
    block_rows = min(512, length)
    block_count = length // block_rows
    score_scale = HD ** (-0.5)
    hidden = w_gate.shape[2] * shards

    expert_ids = jnp.arange(EXPERTS, dtype=jnp.int32)
    member = jnp.sum((routes[:, :, None] == expert_ids[None, None, :]).astype(f32), 1)
    priority = fill_order[0]
    earlier = (priority[None, :] < priority[:, None]).astype(bf16)
    slot_full = jnp.dot(earlier, member.astype(bf16), preferred_element_type=f32)
    slot_code = jnp.where(member > 0, jnp.minimum(slot_full, float(capacity)), -1.0).astype(bf16)

    weights_gate = group_gather(w_gate, ("y", "x", "c")).reshape(
        y_count, shards, local_experts, model_width, -1
    )
    weights_up = group_gather(w_up, ("y", "x", "c")).reshape(
        y_count, shards, local_experts, model_width, -1
    )
    weights_down = group_gather(w_down, ("y", "x", "c")).reshape(
        y_count, shards, local_experts, -1, model_width
    )
    weights_gate = weights_gate.transpose(0, 2, 3, 1, 4).reshape(group_experts, model_width, hidden)
    weights_up = weights_up.transpose(0, 2, 3, 1, 4).reshape(group_experts, model_width, hidden)
    weights_down = weights_down.transpose(0, 2, 1, 3, 4).reshape(group_experts, hidden, model_width)
    cot_all = lax.all_gather(cotangent, "z", axis=0, tiled=False)
    code_all = lax.all_gather(slot_code, "z", axis=0, tiled=False)

    x_full = tokens.astype(f32)
    rms_one = lax.rsqrt(jnp.mean(x_full * x_full, -1, keepdims=True) + EPSILON)
    gain_one = gain_attn.astype(f32)
    normed_one = (x_full * rms_one * gain_one).astype(bf16)
    query_raw = jnp.dot(normed_one, w_query, preferred_element_type=f32)
    key_raw = jnp.dot(normed_one, w_key, preferred_element_type=f32)
    values = (
        jnp.dot(normed_one, w_value, preferred_element_type=f32)
        .astype(bf16)
        .reshape(length, kv_local, HD)
    )
    cosine, sine = rope_tables(length, HD)
    query_rot = rotate(query_raw.reshape(length, heads_local, HD), cosine, sine, 1.0).astype(bf16)
    key_rot = rotate(key_raw.reshape(length, kv_local, HD), cosine, sine, 1.0).astype(bf16)
    query_blocks = query_rot.reshape(block_count, block_rows, kv_local, group_size, HD)
    block_starts = jnp.arange(block_count, dtype=jnp.int32) * block_rows
    positions = jnp.arange(length, dtype=jnp.int32)
    prefix_len = prefix[0]

    def block_scores(query_block, offset):
        query_pos = offset + jnp.arange(block_rows, dtype=jnp.int32)
        raw_scores = (
            jnp.einsum("igjd,kgd->gjik", query_block, key_rot, preferred_element_type=jnp.float32)
            * score_scale
        )
        visible = (positions[None, :] <= query_pos[:, None]) | (positions[None, :] < prefix_len)
        return jnp.where(visible[None, None], raw_scores, -1e30)

    def attend_block(inputs):
        query_block, offset = inputs
        scores = block_scores(query_block, offset)
        row_peak = jnp.max(scores, -1, keepdims=True)
        weights = jnp.exp(scores - row_peak)
        row_total = jnp.sum(weights, -1, keepdims=True)
        probabilities = (weights / row_total).astype(jnp.bfloat16)
        attended = jnp.einsum(
            "gjik,kgd->igjd", probabilities, values, preferred_element_type=jnp.float32
        )
        return (attended.astype(jnp.bfloat16), (row_peak + jnp.log(row_total))[..., 0])

    attended_blocks, log_totals = lax.map(attend_block, (query_blocks, block_starts))
    attended_all = attended_blocks.reshape(length, heads_local * HD)
    attention_rows = lax.psum_scatter(
        jnp.dot(attended_all, w_out, preferred_element_type=f32).astype(bf16),
        ("x", "c"),
        scatter_dimension=0,
        tiled=True,
    ).astype(f32)
    x_rows = lax.dynamic_slice_in_dim(tokens, tensor_rank * own_rows, own_rows, 0).astype(f32)
    hidden_in = x_rows + attention_rows
    rms_two = lax.rsqrt(jnp.mean(hidden_in * hidden_in, -1, keepdims=True) + EPSILON)
    gain_two = gain_moe.astype(f32)
    normed_two = (hidden_in * rms_two * gain_two).astype(bf16)
    normed_all = lax.all_gather(normed_two, "z", axis=0, tiled=False)

    def gates(rows, code):
        logits = jnp.dot(rows, w_router, preferred_element_type=f32)
        chosen = jnp.where(code >= 0, logits, -jnp.inf)
        raised = jnp.exp(chosen - jnp.max(chosen, -1, keepdims=True))
        return raised / jnp.sum(raised, -1, keepdims=True)

    gate_own = gates(normed_two, slot_code)
    first = z_rank * group_experts
    gate_all = jax.vmap(gates)(normed_all, code_all)
    gate_group = lax.dynamic_slice_in_dim(gate_all, first, group_experts, 2)
    code_group = lax.dynamic_slice_in_dim(code_all, first, group_experts, 2).astype(jnp.int32)
    slot_ids = jnp.arange(capacity, dtype=jnp.int32)
    hot = code_group.transpose(2, 0, 1)[:, :, None, :] == slot_ids[None, None, :, None]
    pick = hot.astype(bf16)
    pick_gate = jnp.where(hot, gate_group.transpose(2, 0, 1)[:, :, None, :], 0.0)
    gate_slot = jnp.sum(pick_gate, -1)
    rows_in = jnp.einsum("esci,sid->escd", pick, normed_all, preferred_element_type=f32).astype(bf16)
    rows_dy = jnp.einsum("esci,sid->escd", pick, cot_all, preferred_element_type=f32)
    gate_pre = jnp.einsum("escd,edf->escf", rows_in, weights_gate, preferred_element_type=f32)
    up_pre = jnp.einsum("escd,edf->escf", rows_in, weights_up, preferred_element_type=f32)
    activated = (gate_pre / (1.0 + jnp.exp(-gate_pre)) * up_pre).astype(bf16)
    expert_out = jnp.einsum(
        "escf,efd->escd", activated, weights_down, preferred_element_type=f32
    ).astype(bf16)
    out_grad_rows = (rows_dy * gate_slot[..., None]).astype(bf16)
    gate_grad_slot = jnp.sum(rows_dy * expert_out.astype(f32), -1)
    gate_grad = jnp.einsum("esci,esc->sie", pick.astype(f32), gate_grad_slot, precision=HIGHEST)
    moe_part = jnp.einsum(
        "esci,escd->sid", pick_gate.astype(bf16), expert_out, preferred_element_type=f32
    ).astype(bf16)
    hid_grad = jnp.einsum("escd,efd->escf", out_grad_rows, weights_down, preferred_element_type=f32)
    sigmoid_g = 1.0 / (1.0 + jnp.exp(-gate_pre))
    back_gate = (hid_grad * up_pre * sigmoid_g * (1.0 + gate_pre * (1.0 - sigmoid_g))).astype(bf16)
    back_up = (hid_grad * gate_pre * sigmoid_g).astype(bf16)
    rows_grad = (
        jnp.einsum("escf,edf->escd", back_gate, weights_gate, preferred_element_type=f32)
        + jnp.einsum("escf,edf->escd", back_up, weights_up, preferred_element_type=f32)
    ).astype(bf16)
    rows_part = jnp.einsum("esci,escd->sid", pick, rows_grad, preferred_element_type=f32).astype(bf16)
    down_part = jnp.einsum("escf,escd->efd", activated, out_grad_rows, preferred_element_type=f32)
    gate_part = jnp.einsum("escd,escf->edf", rows_in, back_gate, preferred_element_type=f32)
    up_part = jnp.einsum("escd,escf->edf", rows_in, back_up, preferred_element_type=f32)

    gate_grad_wide = lax.dynamic_update_slice_in_dim(
        jnp.zeros((z_count, own_rows, EXPERTS), f32), gate_grad, first, 2
    )
    back_pack = jnp.concatenate([rows_part, gate_grad_wide.astype(bf16)], -1)
    back_own = lax.psum_scatter(back_pack, "z", scatter_dimension=0, tiled=False).astype(f32)
    moe_own = lax.psum_scatter(moe_part, "z", scatter_dimension=0, tiled=False).astype(f32)
    block_output = (hidden_in + moe_own).astype(bf16)

    def shard_sum(part, dim):
        width = part.shape[dim] // shards
        split = part.reshape((y_count, local_experts) + part.shape[1:dim] + (shards, width) + part.shape[dim + 1 :])
        split = jnp.moveaxis(split, dim + 1, 1).astype(bf16)
        split = split.reshape((y_count * shards,) + split.shape[2:])
        return lax.psum_scatter(split, ("y", "x", "c"), scatter_dimension=0, tiled=False).astype(f32)

    grad_gate = shard_sum(gate_part, 2)
    grad_up = shard_sum(up_part, 2)
    grad_down = shard_sum(down_part, 1)

    normed_two_grad = back_own[:, :model_width]
    gate_grad_own = back_own[:, model_width:]
    logit_grad = gate_own * (
        gate_grad_own - jnp.sum(gate_own * gate_grad_own, -1, keepdims=True)
    )
    router_part = jnp.dot(normed_two.astype(f32).T, logit_grad, precision=HIGHEST)
    normed_two_grad = normed_two_grad + jnp.dot(
        logit_grad, w_router.astype(f32).T, precision=HIGHEST
    )
    gain_two_part = jnp.sum(normed_two_grad * hidden_in * rms_two, 0)
    scaled_two = normed_two_grad * gain_two
    grad_rows = cotangent.astype(f32)
    hidden_grad = (
        grad_rows
        + rms_two * scaled_two
        - hidden_in * rms_two**3 * jnp.mean(scaled_two * hidden_in, -1, keepdims=True)
    )
    shard_part = lax.all_gather(
        hidden_grad.astype(bf16), ("x", "c"), axis=0, tiled=True
    ).astype(f32)
    attended_part = jnp.einsum(
        "id,hd->ih", shard_part.astype(jnp.bfloat16), w_out, preferred_element_type=jnp.float32
    )
    attended_grad = attended_part.astype(jnp.bfloat16)
    out_grad = jnp.einsum(
        "ih,id->hd",
        attended_all,
        shard_part.astype(jnp.bfloat16),
        preferred_element_type=jnp.float32,
    )
    grad_blocks = attended_grad.reshape(block_count, block_rows, kv_local, group_size, HD)

    def back_block(running, inputs):
        key_acc, value_acc = running
        query_block, grad_block, log_block, offset = inputs
        scores = block_scores(query_block, offset)
        probabilities = jnp.exp(scores - log_block[..., None])
        prob_grad = jnp.einsum(
            "igjd,kgd->gjik", grad_block, values, preferred_element_type=jnp.float32
        )
        center = jnp.sum(prob_grad * probabilities, -1, keepdims=True)
        score_grad = (probabilities * (prob_grad - center)).astype(jnp.bfloat16)
        query_grad = (
            jnp.einsum("gjik,kgd->igjd", score_grad, key_rot, preferred_element_type=jnp.float32)
            * score_scale
        )
        key_acc = (
            key_acc
            + jnp.einsum(
                "gjik,igjd->kgd", score_grad, query_block, preferred_element_type=jnp.float32
            )
            * score_scale
        )
        value_acc = value_acc + jnp.einsum(
            "gjik,igjd->kgd",
            probabilities.astype(jnp.bfloat16),
            grad_block,
            preferred_element_type=jnp.float32,
        )
        return ((key_acc, value_acc), query_grad)

    zero_kv = jnp.zeros((length, kv_local, HD), jnp.float32)
    (key_grad, value_grad), query_grads = lax.scan(
        back_block, (zero_kv, zero_kv), (query_blocks, grad_blocks, log_totals, block_starts)
    )
    query_back = (
        rotate(query_grads.reshape(length, heads_local, HD), cosine, sine, -1.0)
        .reshape(length, heads_local * HD)
        .astype(jnp.bfloat16)
    )
    key_back = (
        rotate(key_grad, cosine, sine, -1.0).reshape(length, kv_local * HD).astype(jnp.bfloat16)
    )
    value_back = value_grad.reshape(length, kv_local * HD).astype(jnp.bfloat16)
    query_weight = jnp.einsum(
        "id,ih->dh", normed_one, query_back, preferred_element_type=jnp.float32
    )
    key_weight = jnp.einsum("id,ih->dh", normed_one, key_back, preferred_element_type=jnp.float32)
    value_weight = jnp.einsum(
        "id,ih->dh", normed_one, value_back, preferred_element_type=jnp.float32
    )
    normed_one_grad = jnp.einsum(
        "ih,dh->id", query_back, w_query, preferred_element_type=jnp.float32
    )
    normed_one_grad = normed_one_grad + jnp.einsum(
        "ih,dh->id", key_back, w_key, preferred_element_type=jnp.float32
    )
    normed_one_grad = normed_one_grad + jnp.einsum(
        "ih,dh->id", value_back, w_value, preferred_element_type=jnp.float32
    )
    total_one = lax.psum(normed_one_grad.astype(bf16), ("x", "c")).astype(f32)
    gain_one_part = jnp.sum(normed_one_grad * x_full * rms_one, 0)
    scaled_one = total_one * gain_one
    input_grad = (
        shard_part
        + rms_one * scaled_one
        - x_full * rms_one**3 * jnp.mean(scaled_one * x_full, -1, keepdims=True)
    )
    dp = ("z", "y")
    everyone = ("z", "y", "x", "c")
    summed = [
        lax.psum(part.astype(bf16), dp).astype(f32)
        for part in (query_weight, key_weight, value_weight, out_grad)
    ]
    router_total, gain_one_total, gain_two_total = (
        lax.psum(part.astype(bf16), everyone).astype(f32)
        for part in (router_part, gain_one_part, gain_two_part)
    )
    return (
        block_output,
        input_grad,
        gain_one_total,
        summed[0],
        summed[1],
        summed[2],
        summed[3],
        gain_two_total,
        router_total,
        grad_gate,
        grad_up,
        grad_down,
    )


def solution(mesh):
    dp_count, tensor_count = mesh.devices.shape
    mesh = jax.sharding.Mesh(
        mesh.devices.reshape(dp_count // 2, 2, tensor_count // 2, 2), ("z", "y", "x", "c")
    )
    fast = mesh.devices.shape == (4, 2, 2, 2)
    dp = ("z", "y")
    tensor = ("x", "c")
    both = dp + tensor
    return jax.shard_map(
        per_device_fast if fast else per_device_general,
        mesh=mesh,
        in_specs=(
            P(dp, None),
            P(dp),
            P(),
            P(None, tensor),
            P(None, tensor),
            P(None, tensor),
            P(tensor, None),
            P(),
            P(),
            P(both, None),
            P(both, None),
            P(dp, None, tensor),
            P(dp, None, tensor),
            P(dp, tensor, None),
            P(both, None),
        ),
        out_specs=(
            P(both, None),
            P(dp, None),
            P(),
            P(None, tensor),
            P(None, tensor),
            P(None, tensor),
            P(tensor, None),
            P(),
            P(),
            P(dp, None, tensor),
            P(dp, None, tensor),
            P(dp, tensor, None),
        ),
        check_vma=False,
    )
```

```python
import functools

import jax
import jax.numpy as jnp
import numpy as np
from jax import lax
from jax.experimental import pallas as pl
from jax.experimental.pallas import tpu as pltpu
from jax.sharding import PartitionSpec as P

HD = 64
EXPERTS = 32
TOPK = 8


EPSILON = 1e-06
THETA_BASE = 10000.0
HIGHEST = lax.Precision.HIGHEST


def rope_tables(length, width_in):
    half_width = width_in // 2
    frequency = THETA_BASE ** (-(jnp.arange(half_width, dtype=jnp.float32) / half_width))
    angles = jnp.arange(length, dtype=jnp.float32)[:, None] * frequency[None, :]
    return (jnp.cos(angles), jnp.sin(angles))


def rotate(vectors, cosine, sine, direction):
    half_width = vectors.shape[-1] // 2
    front_half = vectors[..., :half_width]
    back_half = vectors[..., half_width:]
    cos_part = cosine[:, None, :]
    sin_part = sine[:, None, :] * direction
    return jnp.concatenate(
        [
            front_half * cos_part - back_half * sin_part,
            back_half * cos_part + front_half * sin_part,
        ],
        -1,
    )


NT = (((1,), (1,)), ((), ()))
TN = (((0,), (0,)), ((), ()))
f32 = jnp.float32
bf16 = jnp.bfloat16
BQ = 512
BK = 1024
BK_BACK = 512

def from_hbm(*arrays):
    return [pltpu.with_memory_space_constraint(a, pltpu.HBM) for a in arrays]


def busy(us):
    return pl.CostEstimate(flops=int(us * 1e8), bytes_accessed=0, transcendentals=0)


def lanes(shape):
    return lax.broadcasted_iota(jnp.int32, shape, len(shape) - 1)

def rope_wide(v, cos, sin):
    low = lanes(v.shape) % HD < HD // 2
    swapped = jnp.where(low, pltpu.roll(v, 128 - HD // 2, 1), pltpu.roll(v, HD // 2, 1))
    return v * cos + swapped * sin

def project_kernel(x_ref, gain_ref, wq_ref, wk_ref, wv_ref, cos_ref, sin_ref, a_ref, q_ref, k_ref, v_ref):
    x = x_ref[...].astype(f32)
    r = lax.rsqrt(jnp.mean(x * x, -1, keepdims=True) + EPSILON)
    a = (x * r * gain_ref[...].astype(f32)).astype(bf16)
    a_ref[...] = a
    cos, sin = cos_ref[...], sin_ref[...]
    k = jnp.dot(a, wk_ref[...], preferred_element_type=f32)
    k_ref[...] = rope_wide(k, cos, sin).astype(bf16)
    v = jnp.dot(a, wv_ref[...], preferred_element_type=f32).astype(bf16)
    v_ref[:, :128] = v
    v_ref[:, 128:] = jnp.ones_like(v)
    low = lanes(k.shape) < HD
    for pair in range(2):
        q = jnp.dot(a, wq_ref[:, pair * 128 : pair * 128 + 128], preferred_element_type=f32)
        q = rope_wide(q, cos, sin) * HD ** (-0.5)
        other = pltpu.roll(q, HD, 1)
        mine = low if pair == 0 else ~low
        first, second = (q, other) if pair == 0 else (other, q)
        q_ref[2 * pair] = jnp.where(mine, first, 0.0).astype(bf16)
        q_ref[2 * pair + 1] = jnp.where(mine, second, 0.0).astype(bf16)

def project(tokens, gain, wq, wk, wv, cos, sin):
    L, D = tokens.shape
    B = 256
    full = lambda a: pl.BlockSpec(a.shape, lambda i: (0,) * a.ndim)
    rows = lambda w: pl.BlockSpec((B, w), lambda i: (i, 0))
    return pl.pallas_call(
        project_kernel, grid=(L // B,),
        in_specs=[rows(D), full(gain), full(wq), full(wk), full(wv), rows(128), rows(128)],
        out_specs=[rows(D), pl.BlockSpec((4, B, 128), lambda i: (0, i, 0)), rows(128), rows(256)],
        out_shape=[pltpu.HBM((L, D), bf16), pltpu.HBM((4, L, 128), bf16), pltpu.HBM((L, 128), bf16), pltpu.HBM((L, 256), bf16)],
        compiler_params=pltpu.CompilerParams(vmem_limit_bytes=40 << 20),
        cost_estimate=busy(9),
        name="project",
    )(*from_hbm(tokens), gain, wq, wk, wv, cos, sin)

def attend_kernel(bq, bk, kv, prefix_ref, q_ref, k_ref, v_ref, *refs):
    o_ref, lse_ref, s_ref = refs[-3:]
    i = pl.program_id(0)
    start = i * bq
    prefix = prefix_ref[0]
    full_blocks = jnp.maximum(start + 1, prefix) // bk
    all_blocks = (jnp.maximum(start + bq, prefix) + bk - 1) // bk
    rows = 2 * bq
    pos = start + lax.broadcasted_iota(jnp.int32, (rows, 1), 0) % bq
    limit = jnp.maximum(pos, prefix - 1)
    low = lanes((bq, 128)) < HD
    q = jnp.concatenate([q_ref[0], q_ref[1]], 0)

    def tile_max(s, peak):
        for c in range(bk // 128):
            peak = jnp.maximum(peak, s[:, c * 128 : c * 128 + 128])
        return peak

    def plain(j, peak):
        off = pl.multiple_of(j * bk, bk)
        s = lax.dot_general(q, k_ref[pl.ds(off, bk), :], NT, preferred_element_type=f32)
        s_ref[:, pl.ds(off, bk)] = s
        return tile_max(s, peak)

    def masked(j, peak):
        off = pl.multiple_of(j * bk, bk)
        s = lax.dot_general(q, k_ref[pl.ds(off, bk), :], NT, preferred_element_type=f32)
        s = jnp.where(lanes((rows, bk)) <= limit - off, s, -1e30)
        s_ref[:, pl.ds(off, bk)] = s
        return tile_max(s, peak)

    peak = jnp.full((rows, 128), -1e30, f32)
    peak = lax.fori_loop(0, full_blocks, plain, peak)
    peak = lax.fori_loop(full_blocks, all_blocks, masked, peak)
    peak = jnp.max(peak, -1, keepdims=True)

    def weigh(j, acc):
        off = pl.multiple_of(j * bk, bk)
        p = jnp.exp(s_ref[:, pl.ds(off, bk)] - peak).astype(bf16)
        return acc + jnp.dot(p, v_ref[pl.ds(off, bk), :], preferred_element_type=f32)

    acc = lax.fori_loop(0, all_blocks, weigh, jnp.zeros((rows, 256), f32))
    total = acc[:, 128:]
    out = acc[:, :128] / total
    one, two = out[:bq], out[bq:]
    if kv == 0:
        merged = jnp.where(low, one, pltpu.roll(two, HD, 1))
    else:
        merged = jnp.where(low, pltpu.roll(one, HD, 1), two)
    o_ref[...] = merged.astype(bf16)
    lse = (peak + jnp.log(total)).T
    lse_ref[0] = lse[:8]


def attend(prefix, q, k, v, kv, bq, bk, before=()):
    L = k.shape[0]
    return pl.pallas_call(
        functools.partial(attend_kernel, bq, bk, kv),
        grid_spec=pltpu.PrefetchScalarGridSpec(
            num_scalar_prefetch=1, grid=(L // bq,),
            in_specs=[pl.BlockSpec((2, bq, 128), lambda i, p: (kv, i, 0)),
                      pl.BlockSpec((L, 128), lambda i, p: (0, 0)),
                      pl.BlockSpec((L, 256), lambda i, p: (0, 0))]
            + [pl.BlockSpec(memory_space=pl.ANY)] * len(before),
            out_specs=[pl.BlockSpec((bq, 128), lambda i, p: (i, kv)),
                       pl.BlockSpec((1, 8, 2 * bq), lambda i, p: (kv, 0, i))],
            scratch_shapes=[pltpu.VMEM((2 * bq, L), f32)]),
        out_shape=[pltpu.HBM((L, 256), bf16), pltpu.HBM((2, 8, 2 * L), f32)],
        input_output_aliases={4 + i: i for i in range(len(before))},
        compiler_params=pltpu.CompilerParams(vmem_limit_bytes=48 << 20),
        cost_estimate=busy(14),
        name="attend",
    )(prefix, *from_hbm(q, k, v), *before)


def attend_back_kernel(bq, bk, prefix_ref, q_ref, k_ref, v_ref, o_ref, do_ref, lse_ref, cos_ref, sin_ref, cosa_ref, sina_ref,
                       out_ref, dk_acc, dv_acc, dq_acc):
    i = pl.program_id(0)
    start = i * bq
    prefix = prefix_ref[0]
    full_blocks = jnp.maximum(start + 1, prefix) // bk
    all_blocks = (jnp.maximum(start + bq, prefix) + bk - 1) // bk
    rows = 2 * bq
    pos = start + lax.broadcasted_iota(jnp.int32, (1, rows), 1) % bq
    limit = jnp.maximum(pos, prefix - 1)
    low = lanes((bq, 128)) < HD

    @pl.when(i == 0)
    def _():
        dk_acc[...] = jnp.zeros_like(dk_acc)
        dv_acc[...] = jnp.zeros_like(dv_acc)

    heads = []
    for kv in range(2):
        q = jnp.concatenate([q_ref[2 * kv], q_ref[2 * kv + 1]], 0)
        mine = low if kv == 0 else ~low
        pair = do_ref[:, kv * 128 : kv * 128 + 128].astype(f32)
        swap = pltpu.roll(pair, HD, 1)
        first, second = (pair, swap) if kv == 0 else (swap, pair)
        do = jnp.concatenate([jnp.where(mine, first, 0.0), jnp.where(mine, second, 0.0)], 0).astype(bf16)
        prod = pair * o_ref[:, kv * 128 : kv * 128 + 128].astype(f32)
        one = jnp.sum(jnp.where(low, prod, 0.0), -1, keepdims=True)
        two = jnp.sum(jnp.where(low, 0.0, prod), -1, keepdims=True)
        center = jnp.broadcast_to(jnp.concatenate([one, two], 0), (rows, 128)).T[:1]
        heads.append((q, do, center, lse_ref[kv, :1, :]))
    dq_acc[...] = jnp.zeros_like(dq_acc)

    def step(j, _, mask):
        off = pl.multiple_of(j * bk, bk)
        kb = k_ref[pl.ds(off, bk), :]
        vb = v_ref[pl.ds(off, bk), :128]
        dvs, dks = [], []
        for kv, (q, do, center, lse) in enumerate(heads):
            s = lax.dot_general(kb, q, NT, preferred_element_type=f32)
            dp = lax.dot_general(vb, do, NT, preferred_element_type=f32)
            if mask:
                s = jnp.where(off + lax.broadcasted_iota(jnp.int32, (bk, rows), 0) <= limit, s, -1e30)
            p = jnp.exp(s - lse)
            ds = (p * (dp - center)).astype(bf16)
            dvs.append(jnp.dot(p.astype(bf16), do, preferred_element_type=f32))
            dks.append(jnp.dot(ds, q, preferred_element_type=f32))
            dq_acc[kv] += lax.dot_general(ds, kb, TN, preferred_element_type=f32)
        dv_acc[pl.ds(off, bk), :] += dvs[0] + dvs[1]
        dk_acc[pl.ds(off, bk), :] += dks[0] + dks[1]
        return 0

    lax.fori_loop(0, full_blocks, functools.partial(step, mask=False), 0)
    lax.fori_loop(full_blocks, all_blocks, functools.partial(step, mask=True), 0)
    for kv in range(2):
        dq = dq_acc[kv] * HD ** (-0.5)
        one, two = dq[:bq], dq[bq:]
        if kv == 0:
            merged = jnp.where(low, one, pltpu.roll(two, HD, 1))
        else:
            merged = jnp.where(low, pltpu.roll(one, HD, 1), two)
        out_ref[pl.ds(pl.multiple_of(start, bq), bq), kv * 128 : kv * 128 + 128] = rope_wide(merged, cos_ref[...], -sin_ref[...]).astype(bf16)

    @pl.when(i == pl.num_programs(0) - 1)
    def _():
        for b in range(dk_acc.shape[0] // bq):
            r = pl.ds(b * bq, bq)
            out_ref[r, 256:384] = rope_wide(dk_acc[r, :], cosa_ref[r, :], -sina_ref[r, :]).astype(bf16)
            out_ref[r, 384:] = dv_acc[r, :].astype(bf16)

def attend_back(prefix, q, k, v, o, do, lse, cos, sin, bq=256, bk=256):
    L = k.shape[0]
    fullL = pl.BlockSpec((L, 128), lambda i, p: (0, 0))
    return pl.pallas_call(
        functools.partial(attend_back_kernel, bq, bk),
        grid_spec=pltpu.PrefetchScalarGridSpec(
            num_scalar_prefetch=1, grid=(L // bq,),
            in_specs=[pl.BlockSpec((4, bq, 128), lambda i, p: (0, i, 0)), fullL,
                      pl.BlockSpec((L, 256), lambda i, p: (0, 0)),
                      pl.BlockSpec((bq, 256), lambda i, p: (i, 0)),
                      pl.BlockSpec((bq, 256), lambda i, p: (i, 0)),
                      pl.BlockSpec((2, 8, 2 * bq), lambda i, p: (0, 0, i)),
                      pl.BlockSpec((bq, 128), lambda i, p: (i, 0)),
                      pl.BlockSpec((bq, 128), lambda i, p: (i, 0)), fullL, fullL],
            out_specs=pl.BlockSpec((L, 512), lambda i, p: (0, 0)),
            scratch_shapes=[pltpu.VMEM((L, 128), f32), pltpu.VMEM((L, 128), f32), pltpu.VMEM((2, 2 * bq, 128), f32)]),
        out_shape=jax.ShapeDtypeStruct((L, 512), bf16),
        compiler_params=pltpu.CompilerParams(vmem_limit_bytes=48 << 20),
        cost_estimate=busy(46),
        name="attend_back",
    )(prefix, q, k, v, o, do, lse, cos, sin, cos, sin)


def pick_kernel(experts, per, cap, pairs, shift_ref, *refs):
    in_ref, dyo_ref, gs_ref, gate_ref, code_ref, code_t, gate_t, rows_s, dy_s = refs[-9:]
    tokens, width = rows_s.shape

    @pl.when(pl.program_id(0) == 0)
    def _():
        if pairs:
            rows_ref, rows_other, side_ref, side_other, router_ref = refs[:5]
            first = shift_ref[experts] != 0
            rows = jnp.where(first, rows_ref[...], rows_other[...])
            side = jnp.where(first, side_ref[...], side_other[...])
        else:
            rows_ref, side_ref, router_ref = refs[:3]
            rows, side = rows_ref[...], side_ref[...]
        rows_s[...] = rows
        dy_s[...] = side[:, :width]
        code = side[:, width:].astype(f32)
        code_ref[...] = code
        logits = jnp.dot(rows, router_ref[...], preferred_element_type=f32)
        chosen = jnp.where(code >= 0, logits, -1e30)
        raised = jnp.where(code >= 0, jnp.exp(chosen - jnp.max(chosen, -1, keepdims=True)), 0.0)
        gate = raised / jnp.sum(raised, -1, keepdims=True)
        gate_ref[...] = gate
        gate_t[...] = gate.T
        code_t[...] = code.T

    hots = []
    for e in range(per):
        row = pl.ds(shift_ref[pl.program_id(0) * per + e], 1)
        hot = code_t[row, :] == lax.broadcasted_iota(jnp.int32, (cap, tokens), 0).astype(f32)
        gs = jnp.sum(jnp.where(hot, gate_t[row, :], 0.0), -1, keepdims=True)
        gs_ref[e] = jnp.broadcast_to(gs, (cap, 128))
        hots.append(hot.astype(bf16))
    hot = jnp.concatenate(hots, 0)
    in_ref[...] = jnp.dot(hot, rows_s[...], preferred_element_type=f32).astype(bf16).reshape(in_ref.shape)
    dyo_ref[...] = jnp.dot(hot, dy_s[...], preferred_element_type=f32).astype(bf16).reshape(dyo_ref.shape)


def pick(shift, rows, sides, router, cap):
    R, D = rows[0].shape
    E = shift.shape[0] - 1
    W = router.shape[1]
    per = 4
    operands = [*rows, *sides, router]
    whole = lambda a: pl.BlockSpec(a.shape, lambda e: (0, 0))
    some = lambda w: pl.BlockSpec((per, cap, w), lambda e: (e, 0, 0))
    wide = pl.BlockSpec((R, W), lambda e: (0, 0))
    return pl.pallas_call(
        functools.partial(pick_kernel, E, per, cap, len(rows) == 2),
        grid=(E // per,),
        in_specs=[pl.BlockSpec(memory_space=pltpu.SMEM)] + [whole(a) for a in operands],
        out_specs=[some(D), some(D), some(128), wide, wide],
        out_shape=[pltpu.HBM((E, cap, D), bf16), pltpu.HBM((E, cap, D), bf16),
                   pltpu.HBM((E, cap, 128), f32), jax.ShapeDtypeStruct((R, W), f32), jax.ShapeDtypeStruct((R, W), f32)],
        scratch_shapes=[pltpu.VMEM((W, R), f32), pltpu.VMEM((W, R), f32), pltpu.VMEM((R, D), bf16), pltpu.VMEM((R, D), bf16)],
        compiler_params=pltpu.CompilerParams(vmem_limit_bytes=40 << 20),
        cost_estimate=busy(4),
        name="pick",
    )(shift, *operands)


def ffn_kernel(n, blocks, *refs):
    rows_refs, dy_refs, gs_refs = refs[:n], refs[n : 2 * n], refs[2 * n : 3 * n]
    w_ref = refs[3 * n]
    eout_ref, drows_ref, dgs_ref, act_ref, dgu_ref = refs[-5:]
    cap, D = rows_refs[0].shape[1:]
    M = n * cap
    rows = jnp.concatenate([r[0] for r in rows_refs], 0)
    dy = jnp.concatenate([r[0] for r in dy_refs], 0)
    gs = jnp.concatenate([r[0] for r in gs_refs], 0)
    dout = (dy.astype(f32) * gs[:, :1]).astype(bf16)
    F = w_ref.shape[-1]
    w = jnp.concatenate([w_ref[0, b, part, 0] for b in range(blocks) for part in (0, 1)], 1)
    wd = jnp.concatenate([w_ref[0, b, 2, 0] for b in range(blocks)], 1)
    gu = jnp.dot(rows, w, preferred_element_type=f32)
    dacts = jnp.dot(dout, wd, preferred_element_type=f32)
    acts, dgus = [], []
    for b in range(blocks):
        g, u = gu[:, 2 * b * F : (2 * b + 1) * F], gu[:, (2 * b + 1) * F : (2 * b + 2) * F]
        dact = dacts[:, b * F : (b + 1) * F]
        sg = 1.0 / (1.0 + jnp.exp(-g))
        gsg = g * sg
        acts.append((gsg * u).astype(bf16))
        dgus.append((dact * u * (sg + gsg * (1.0 - sg))).astype(bf16))
        dgus.append((dact * gsg).astype(bf16))
    act = jnp.concatenate(acts, 1)
    dgu = jnp.concatenate(dgus, 1)
    act_ref[0] = act
    dgu_ref[0] = dgu
    drows = lax.dot_general(dgu, w, NT, preferred_element_type=f32)
    eout = lax.dot_general(act, wd, NT, preferred_element_type=f32)
    eout = eout.astype(bf16)
    eout_ref[0] = eout
    drows_ref[0] = drows.astype(bf16)
    dgs = jnp.sum(dy.astype(f32) * eout.astype(f32), -1, keepdims=True)
    dgs_ref[0] = jnp.broadcast_to(dgs, (M, 128))


def ffn(picked, weights, groups, before=()):
    n = len(picked)
    total, cap, D = picked[0][0].shape
    _, blocks, _, E, _, F = weights.shape
    H = blocks * F
    M = n * cap
    first = groups[0] * E
    spec = lambda w: pl.BlockSpec((1, cap, w), lambda e: (e + first, 0, 0))
    outs = lambda w: pl.BlockSpec((1, M, w), lambda e: (e + first, 0, 0))
    wsp = pl.BlockSpec((1, blocks, 3, 1, D, F), lambda e: ((e + first) // E, 0, 0, (e + first) % E, 0, 0))
    sh = lambda w, t: pltpu.HBM((total, M, w), t)
    operands = [p[i] for i in range(3) for p in picked] + [weights]
    return pl.pallas_call(
        functools.partial(ffn_kernel, n, blocks), grid=(len(groups) * E,),
        in_specs=[spec(D)] * (2 * n) + [spec(128)] * n + [wsp] + [pl.BlockSpec(memory_space=pl.ANY)] * len(before),
        out_specs=[outs(D), outs(D), outs(128), outs(H), outs(2 * H)],
        out_shape=[sh(D, bf16), sh(D, bf16), sh(128, f32), sh(H, bf16), sh(2 * H, bf16)],
        input_output_aliases={len(operands) + i: i for i in range(len(before))},
        compiler_params=pltpu.CompilerParams(vmem_limit_bytes=56 << 20),
        cost_estimate=busy(12 * len(groups)),
        name="ffn",
    )(*operands, *before)


def wgrad_kernel(n, halves, blocks, *refs):
    rows_refs, dy_refs, gs_refs = refs[:n], refs[n : 2 * n], refs[2 * n : 3 * n]
    act_refs, dgu_refs, out_ref = refs[3 * n : 3 * n + halves], refs[3 * n + halves : 3 * n + 2 * halves], refs[-1]
    rows = jnp.concatenate([r[0] for r in rows_refs], 0)
    dy = jnp.concatenate([r[0] for r in dy_refs], 0)
    gs = jnp.concatenate([r[0] for r in gs_refs], 0)
    dout = (dy.astype(f32) * gs[:, :1]).astype(bf16)
    F = act_refs[0].shape[2] // blocks
    for b in range(blocks):
        dgu = jnp.concatenate([r[0, :, b * 2 * F : (b + 1) * 2 * F] for r in dgu_refs], 0)
        g = lax.dot_general(rows, dgu, TN, preferred_element_type=f32).astype(bf16)
        out_ref[0, b, 0, 0] = g[:, :F]
        out_ref[0, b, 1, 0] = g[:, F:]
    for pair in range(0, blocks, 2):
        act = jnp.concatenate([r[0, :, pair * F : (pair + 2) * F] for r in act_refs], 0)
        gd = lax.dot_general(dout, act, TN, preferred_element_type=f32).astype(bf16)
        out_ref[0, pair, 2, 0] = gd[:, :F]
        out_ref[0, pair + 1, 2, 0] = gd[:, F:]


def wgrad(picked, acts, dgus, blocks, groups, group, before=()):
    n = len(picked)
    total, cap, D = picked[0][0].shape
    H = acts[0].shape[2]
    F = H // blocks
    E = total // groups
    spec = lambda w: pl.BlockSpec((1, cap, w), lambda e: (e + group * E, 0, 0))
    wide = lambda a: pl.BlockSpec((1,) + a.shape[1:], lambda e: (e + group * E, 0, 0))
    operands = [*[p[i] for i in range(3) for p in picked], *acts, *dgus]
    return pl.pallas_call(
        functools.partial(wgrad_kernel, n, len(acts), blocks),
        grid=(E,),
        in_specs=[spec(D)] * (2 * n) + [spec(128)] * n + [wide(a) for a in (*acts, *dgus)]
        + [pl.BlockSpec(memory_space=pl.ANY)] * len(before),
        out_specs=pl.BlockSpec((1, blocks, 3, 1, D, F), lambda e: (group, 0, 0, e, 0, 0)),
        out_shape=pltpu.HBM((groups, blocks, 3, E, D, F), bf16),
        input_output_aliases={len(operands) + i: i for i in range(len(before))},
        compiler_params=pltpu.CompilerParams(vmem_limit_bytes=56 << 20),
        cost_estimate=busy(13),
        name="wgrad",
    )(*operands, *before)


def hot_columns(code, shift, cap):
    col = jnp.sum(jnp.where(lanes(code.shape) == shift, code, 0.0), -1, keepdims=True)
    return col == lanes((code.shape[0], cap)).astype(f32)


def merge_back_kernel(n, E, cap, shift_ref, *refs):
    sides, (d_ref, g_ref), outs = refs[:n], refs[n : n + 2], refs[n + 2 :]
    D = d_ref.shape[2]
    lane = lanes((cap, 128))
    for source in range(n):

        @pl.when(pl.program_id(0) == source)
        def _():
            code = sides[source][...]
            total = jnp.zeros((code.shape[0], D), f32)
            gates = jnp.zeros((code.shape[0], 128), f32)
            for e0 in range(0, E, 4):
                some = range(e0, min(e0 + 4, E))
                hot = jnp.concatenate([hot_columns(code, shift_ref[e], cap).astype(bf16) for e in some], 1)
                rows = jnp.concatenate([d_ref[e] for e in some], 0)
                side = jnp.concatenate([jnp.where(lane == shift_ref[e], g_ref[e], 0.0).astype(bf16) for e in some], 0)
                total = total + jnp.dot(hot, rows, preferred_element_type=f32)
                gates = gates + jnp.dot(hot, side, preferred_element_type=f32)
            outs[source][:, :D] = total.astype(bf16)
            outs[source][:, D:] = gates.astype(bf16)


def merge_back(shift, codes, drows, dgs, cap):
    n = len(codes)
    R, W = codes[0].shape
    E, _, D = drows.shape
    part = lambda w: pl.BlockSpec((E, cap, w), lambda i: (0, i, 0))
    whole = lambda w: pl.BlockSpec((R, w), lambda i: (0, 0))
    return pl.pallas_call(
        functools.partial(merge_back_kernel, n, E, cap),
        grid=(n,),
        in_specs=[pl.BlockSpec(memory_space=pltpu.SMEM)] + [whole(W)] * n + [part(D), part(128)],
        out_specs=[whole(D + 128)] * n,
        out_shape=[jax.ShapeDtypeStruct((R, D + 128), bf16)] * n,
        compiler_params=pltpu.CompilerParams(vmem_limit_bytes=48 << 20),
        cost_estimate=busy(3 * n),
        name="merge_back",
    )(shift, *codes, drows, dgs)


def merge_out_kernel(n, E, cap, shift_ref, *refs):
    sides, gates, e_ref, outs = refs[:n], refs[n : 2 * n], refs[2 * n], refs[2 * n + 1 :]
    D = e_ref.shape[2]
    for source in range(n):

        @pl.when(pl.program_id(0) == source)
        def _():
            code = sides[source][...]
            gate = gates[source][...]
            total = jnp.zeros((code.shape[0], D), f32)
            for e0 in range(0, E, 4):
                some = range(e0, min(e0 + 4, E))
                parts = []
                for e in some:
                    g = jnp.sum(jnp.where(lanes(gate.shape) == shift_ref[e], gate, 0.0), -1, keepdims=True)
                    parts.append(jnp.where(hot_columns(code, shift_ref[e], cap), g, 0.0).astype(bf16))
                rows = jnp.concatenate([e_ref[e] for e in some], 0)
                total = total + jnp.dot(jnp.concatenate(parts, 1), rows, preferred_element_type=f32)
            outs[source][...] = total.astype(bf16)


def merge_out(shift, codes, gates, eout, cap):
    n = len(codes)
    R, W = codes[0].shape
    E, _, D = eout.shape
    whole = lambda w: pl.BlockSpec((R, w), lambda i: (0, 0))
    return pl.pallas_call(
        functools.partial(merge_out_kernel, n, E, cap),
        grid=(n,),
        in_specs=[pl.BlockSpec(memory_space=pltpu.SMEM)] + [whole(W)] * (2 * n)
        + [pl.BlockSpec((E, cap, D), lambda i: (0, i, 0))],
        out_specs=[whole(D)] * n,
        out_shape=[jax.ShapeDtypeStruct((R, D), bf16)] * n,
        compiler_params=pltpu.CompilerParams(vmem_limit_bytes=48 << 20),
        cost_estimate=busy(11),
        name="merge_out",
    )(shift, *codes, *gates, eout)


def finish_kernel(core_ref, sum_ref, x_ref, dh_ref, gain_ref, *refs):
    out_ref = refs[-1]
    x = x_ref[...].astype(f32)
    r = lax.rsqrt(jnp.mean(x * x, -1, keepdims=True) + EPSILON)
    scaled = sum_ref[...].astype(f32) * gain_ref[...].astype(f32)
    out_ref[...] = dh_ref[...].astype(f32) + r * scaled - x * (r * r * r * jnp.mean(scaled * x, -1, keepdims=True))


def finish(core, summed, tokens, hidden, gain, rows, before=()):
    L, D = tokens.shape
    half = rows // 2
    place = lambda i, p: ((i // 2) * 4 + p[0] * 2 + i % 2, 0)
    return pl.pallas_call(
        finish_kernel,
        grid_spec=pltpu.PrefetchScalarGridSpec(
            num_scalar_prefetch=1, grid=(L // rows,),
            in_specs=[pl.BlockSpec((half, D), lambda i, p: (i, 0)), pl.BlockSpec((half, D), place), pl.BlockSpec((half, D), place),
                      pl.BlockSpec((1, D), lambda i, p: (0, 0))] + [pl.BlockSpec(memory_space=pl.ANY)] * len(before),
            out_specs=pl.BlockSpec((half, D), place)),
        out_shape=jax.ShapeDtypeStruct((L, D), f32),
        input_output_aliases={5 + i: i for i in range(len(before))},
        compiler_params=pltpu.CompilerParams(vmem_limit_bytes=48 << 20),
        cost_estimate=busy(4),
        name="finish",
    )(core, summed, tokens, hidden, gain, *before)


def spread_kernel(n, more, rank_ref, att_ref, w_ref, *refs):
    blocks = refs[:n]
    hidden_ref, do_ref, og_ref = refs[-3:]
    i = pl.program_id(0)

    @pl.when(i == 0)
    def _():
        og_ref[...] = refs[n][...] if more else jnp.zeros_like(og_ref)

    for b in range(n):

        @pl.when(i == b)
        def _():
            block = blocks[b][...]
            hidden_ref[...] = block
            do_ref[...] = lax.dot_general(block, w_ref[...], NT, preferred_element_type=f32).astype(bf16)
            og_ref[...] += lax.dot_general(att_ref[...], block, TN, preferred_element_type=f32)


def spread(rank, first, blocks, attended, w_out, before=None):
    n = len(blocks)
    R, D = blocks[0].shape
    L, H = attended.shape
    place = lambda i, p: (p[0] ^ (i + first), 0)
    whole = lambda a: pl.BlockSpec(a.shape, lambda i, p: (0, 0))
    total = jax.ShapeDtypeStruct((H, D), f32)
    operands = [attended, w_out, *blocks]
    specs = [pl.BlockSpec((R, H), place), whole(w_out)] + [whole(b) for b in blocks]
    aliases = {}
    if before is not None:
        hidden, do, og = before
        operands += [og, hidden, do]
        specs += [whole(og)] + [pl.BlockSpec(memory_space=pl.ANY)] * 2
        aliases = {len(operands) - 1: 0, len(operands): 1}
    return pl.pallas_call(
        functools.partial(spread_kernel, n, before is not None),
        grid_spec=pltpu.PrefetchScalarGridSpec(
            num_scalar_prefetch=1, grid=(n,), in_specs=specs,
            out_specs=[pl.BlockSpec((R, D), place), pl.BlockSpec((R, H), place), whole(total)]),
        out_shape=[pltpu.HBM((L, D), bf16), pltpu.HBM((L, H), bf16), total],
        input_output_aliases=aliases,
        compiler_params=pltpu.CompilerParams(vmem_limit_bytes=32 << 20),
        cost_estimate=busy(3),
        name="spread",
    )(rank, *operands)


def grads_kernel(parts_ref, gate_ref, up_ref, down_ref):
    gate_ref[0] = parts_ref[0, 0].astype(f32)
    up_ref[0] = parts_ref[1, 0].astype(f32)
    down_ref[0] = parts_ref[2, 0].astype(f32).T


def expert_grads(parts):
    _, E, D, F = parts.shape
    one = lambda *s: pl.BlockSpec((1,) + s, lambda e: (e, 0, 0))
    return pl.pallas_call(
        grads_kernel,
        grid=(E,),
        in_specs=[pl.BlockSpec((3, 1, D, F), lambda e: (0, e, 0, 0))],
        out_specs=[one(D, F), one(D, F), one(F, D)],
        out_shape=[pltpu.HBM((E, D, F), f32), pltpu.HBM((E, D, F), f32), pltpu.HBM((E, F, D), f32)],
        compiler_params=pltpu.CompilerParams(vmem_limit_bytes=32 << 20),
        cost_estimate=busy(4),
        name="expert_grads",
    )(parts)


def out_kernel(rank_ref, a_ref, b_ref, w_ref, keep_ref, send_ref):
    keep_ref[...] = jnp.dot(a_ref[...], w_ref[...], preferred_element_type=f32)
    send_ref[...] = jnp.dot(b_ref[...], w_ref[...], preferred_element_type=f32).astype(bf16)


def out_pair(rank, bits, attended, w_out, rows):
    H, D = w_out.shape
    step = min(256, rows)
    n = rows // step
    block = lambda bit: pl.BlockSpec((step, H), lambda i, p: ((p[0] ^ bit) * n + i, 0))
    out = pl.BlockSpec((step, D), lambda i, p: (i, 0))
    return pl.pallas_call(
        out_kernel,
        grid_spec=pltpu.PrefetchScalarGridSpec(
            num_scalar_prefetch=1, grid=(n,),
            in_specs=[block(bits[0]), block(bits[1]), pl.BlockSpec((H, D), lambda i, p: (0, 0))],
            out_specs=[out, out]),
        out_shape=[jax.ShapeDtypeStruct((rows, D), f32), jax.ShapeDtypeStruct((rows, D), bf16)],
        compiler_params=pltpu.CompilerParams(vmem_limit_bytes=32 << 20),
        cost_estimate=busy(3),
        name="out_pair",
    )(rank, attended, attended, w_out)


def parted_kernel(cuts, low_ref, left_ref, right_ref, *outs):
    at = 0
    for out, cut in zip(outs[:-1], cuts):
        out[...] = low_ref[:, at : at + cut].astype(f32)
        at += cut
    half = left_ref.shape[1]
    outs[-1][:, :half] = left_ref[...].astype(f32)
    outs[-1][:, half:] = right_ref[...].astype(f32)


def parted(low, cuts):
    total, half = low.shape
    rows = 2 * half
    part = (total - rows) // 2
    n = 4
    block = lambda r, w, at: pl.BlockSpec((r // n, w), lambda i: (at * n // r + i, 0))
    return pl.pallas_call(
        functools.partial(parted_kernel, cuts),
        grid=(n,),
        in_specs=[block(rows, half, 0), block(part, half, rows), block(part, half, rows + part)],
        out_specs=[block(rows, cut, 0) for cut in cuts] + [block(part, 2 * half, 0)],
        out_shape=[pltpu.HBM((rows, cut), f32) for cut in cuts] + [pltpu.HBM((part, 2 * half), f32)],
        compiler_params=pltpu.CompilerParams(vmem_limit_bytes=32 << 20),
        cost_estimate=busy(3),
        name="parted",
    )(*from_hbm(low, low, low))


def swap(x, axis, bit=1):
    count = lax.axis_size(axis)
    return lax.ppermute(x, axis, [(i, i ^ bit) for i in range(count)])


def total_over(x, axes):
    for axis in axes:
        bit = 1
        while bit < lax.axis_size(axis):
            low = x.astype(bf16)
            x = low.astype(f32) + swap(low, axis, bit).astype(f32)
            bit *= 2
    return x


def wide_tables(length):
    half = HD // 2
    angles = np.arange(length)[:, None] * THETA_BASE ** (-(np.arange(half) / half))[None, :]
    cos, sin = np.cos(angles), np.sin(angles)
    return (
        jnp.asarray(np.concatenate([cos, cos, cos, cos], 1), f32),
        jnp.asarray(np.concatenate([-sin, sin, -sin, sin], 1), f32),
    )


NEAR = [(0, 1), (1, 0), (2, 3), (3, 2)]
MIDDLE = [(1, 2), (2, 1)]
TO_ENDS = [(1, 0), (2, 3)]
FROM_ENDS = [(0, 1), (3, 2)]


def line_first(x):
    return lax.ppermute(x, "z", NEAR), lax.ppermute(x, "z", MIDDLE)


def line_second(near, across):
    return lax.ppermute(near, "z", MIDDLE), lax.ppermute(across, "z", TO_ENDS)


def line_third(across_far):
    return lax.ppermute(across_far, "z", TO_ENDS)


def hold(*arrays):
    return lax.optimization_barrier(arrays)


def line_out(parts):
    return lax.ppermute(parts[3], "z", FROM_ENDS), lax.ppermute(parts[2], "z", FROM_ENDS)


def add_low(a, b):
    return (a.astype(f32) + b.astype(f32)).astype(a.dtype)


def line_over(part, from_end):
    return lax.ppermute(add_low(part, from_end), "z", MIDDLE)


def line_in(part, across_far):
    return lax.ppermute(add_low(part, across_far), "z", NEAR)


def line_sum(parts, from_end_far, from_end):
    own, near, two, three = parts
    across_far = line_over(two, from_end_far)
    across = line_over(three, from_end)
    got = line_in(near, across_far)
    return own.astype(f32) + across.astype(f32) + got.astype(f32)


def per_device_fast(
    tokens,
    prefix,
    gain_attn,
    w_query,
    w_key,
    w_value,
    w_out,
    gain_moe,
    w_router,
    routes,
    fill_order,
    w_gate,
    w_up,
    w_down,
    cotangent,
):
    z, y, x, c = (lax.axis_index(a) for a in ("z", "y", "x", "c"))
    shards = lax.axis_size("x") * lax.axis_size("c")
    groups = lax.axis_size("y")
    rank = x * lax.axis_size("c") + c
    at_end = (z == 0) | (z == lax.axis_size("z") - 1)
    length, width = tokens.shape
    own_rows = routes.shape[0]
    local = w_gate.shape[0]
    cap = own_rows * TOPK // EXPERTS

    expert_ids = jnp.arange(EXPERTS, dtype=jnp.int32)
    member = jnp.sum((routes[:, :, None] == expert_ids[None, None, :]).astype(f32), 1)
    priority = fill_order[0]
    earlier = (priority[None, :] < priority[:, None]).astype(bf16)
    slot_full = jnp.dot(earlier, member.astype(bf16), preferred_element_type=f32)
    code = jnp.where(member > 0, jnp.minimum(slot_full, float(cap)), -1.0).astype(bf16)
    code = jnp.pad(code, ((0, 0), (0, 128 - EXPERTS)), constant_values=-1)
    side_own = jnp.concatenate([cotangent, code], 1)
    side_near, side_across = line_first(side_own)
    router_wide = jnp.pad(w_router, ((0, 0), (0, 128 - EXPERTS)))
    shift = z * groups * local + jnp.arange(groups * local, dtype=jnp.int32)
    shift_end = jnp.concatenate([shift, at_end.astype(jnp.int32)[None]])


    own_weights = jnp.stack([w_gate, w_up, w_down.transpose(0, 2, 1)])
    weights = lax.all_gather(own_weights, ("y", "x", "c"), axis=0, tiled=False)
    weights = weights.reshape((groups, shards) + own_weights.shape)

    cos, sin = wide_tables(length)
    normed_one, query, key, value = project(tokens, gain_attn[None], w_query, w_key, w_value, cos, sin)
    first_half = attend(prefix, query, key, value, 0, BQ, BK)
    *first_half, side_near, side_across = hold(*first_half, side_near, side_across)
    side_far, side_relay = line_second(side_near, side_across)
    attended, log_total = attend(prefix, query, key, value, 1, BQ, BK, first_half)
    rank_row = rank.astype(jnp.int32)[None]
    far_keep, far_send = out_pair(rank_row, (2, 3), attended, w_out, own_rows)
    far_keep, side_far = hold(far_keep, side_far)
    side_last = line_third(side_far)
    far_sum = far_keep + swap(far_send, "c").astype(f32)
    far_got = swap(far_sum.astype(bf16), "x")
    near_keep, near_send = out_pair(rank_row, (0, 1), attended, w_out, own_rows)
    near_sum = near_keep + swap(near_send, "c").astype(f32)
    near_sum, far_got, side_relay, side_last = hold(near_sum, far_got, side_relay, side_last)
    x_rows = lax.dynamic_slice_in_dim(tokens, rank * own_rows, own_rows, 0).astype(f32)
    hidden_in = x_rows + near_sum + far_got.astype(f32)
    rms_two = lax.rsqrt(jnp.mean(hidden_in * hidden_in, -1, keepdims=True) + EPSILON)
    gain_two = gain_moe.astype(f32)
    normed_two = (hidden_in * rms_two * gain_two).astype(bf16)

    near, across = line_first(normed_two)

    def pick_of(rows, sides):
        return pick(shift_end, rows, sides, router_wide, cap)

    pick_own = pick_of((normed_two,), (side_own,))
    near, across, *pick_own = hold(near, across, *pick_own)
    far, relay = line_second(near, across)
    close = [pick_own, pick_of((near,), (side_near,))]
    half_close = ffn(close, weights, (0,))
    far, relay, *half_close = hold(far, relay, *half_close)
    last = line_third(far)
    done_close = ffn(close, weights, (1,), half_close)
    apart = [pick_of((relay, far), (side_relay, side_far))]
    last, *done_close = hold(last, *done_close)
    apart.append(pick_of((last, across), (side_last, side_across)))
    done_apart = ffn(apart, weights, (0, 1))
    picked = close + apart
    gates = [p[3] for p in picked]
    codes = [p[4] for p in picked]
    far_back = merge_back(shift, codes[2:], done_apart[1], done_apart[2], cap)
    back = [*merge_back(shift, codes[:2], done_close[1], done_close[2], cap), *far_back]
    back_end_far, back_end = line_out(back)
    late_act, *_ = hold(done_apart[3], *far_back)
    used = (done_close[3], late_act), (done_close[4], done_apart[4]), shards, groups
    parts = wgrad(picked, *used, 0)
    parts = wgrad(picked, *used, 1, (parts,))
    back_end_far, parts = hold(back_end_far, parts)
    across_far = line_over(back[2], back_end_far)
    across = line_over(back[3], back_end)
    late_close, late_apart, _ = hold(done_close[0], done_apart[0], across_far)
    out_parts = [
        *merge_out(shift, codes[:2], gates[:2], late_close, cap),
        *merge_out(shift, codes[2:], gates[2:], late_apart, cap),
    ]
    got = line_in(back[1], across_far)
    got, across, *out_parts = hold(got, across, *out_parts)
    back_own = back[0].astype(f32) + across.astype(f32) + got.astype(f32)
    out_end_far, out_end = line_out(out_parts)
    part_sum = lax.psum_scatter(
        parts.reshape((groups * shards,) + parts.shape[2:]), ("y", "x", "c"), scatter_dimension=0, tiled=False
    )

    gate_own = gates[0]
    gate_grad = back_own[:, width:]
    logit_grad = gate_own * (gate_grad - jnp.sum(gate_own * gate_grad, -1, keepdims=True))
    logit_low = logit_grad.astype(bf16)
    normed_two_grad = back_own[:, :width] + lax.dot_general(
        logit_low, router_wide, (((1,), (1,)), ((), ())), preferred_element_type=f32
    )
    router_part = lax.dot_general(
        logit_low, normed_two, (((0,), (0,)), ((), ())), preferred_element_type=f32
    )[:EXPERTS]
    gain_two_part = jnp.sum(normed_two_grad * hidden_in * rms_two, 0)
    scaled_two = normed_two_grad * gain_two
    hidden_grad = (
        cotangent.astype(f32)
        + rms_two * scaled_two
        - hidden_in * rms_two**3 * jnp.mean(scaled_two * hidden_in, -1, keepdims=True)
    ).astype(bf16)
    small = jnp.concatenate([router_part, gain_two_part[None], jnp.zeros((7, width), f32)], 0)
    hidden_over_x = swap(hidden_grad, "x")
    near_done = spread(rank_row, 0, [hidden_grad, swap(hidden_grad, "c")], attended, w_out)
    *near_done, out_end_far, out_end = hold(*near_done, out_end_far, out_end)
    out_two, out_three = add_low(out_parts[2], out_end_far), add_low(out_parts[3], out_end)
    hidden_over_x, out_two, out_three, *near_done = hold(hidden_over_x, out_two, out_three, *near_done)
    hidden_all, attended_grad, out_grad = spread(
        rank_row, 2, [hidden_over_x, swap(hidden_over_x, "c")], attended, w_out, near_done
    )
    attended_grad, small, out_low = hold(attended_grad, small, out_grad.astype(bf16))
    out_far, out_across = (lax.ppermute(part, "z", MIDDLE) for part in (out_two, out_three))
    heads_back = attend_back(
        prefix, query, key, value, attended, attended_grad, log_total, cos, sin, BQ, BK_BACK
    )
    heads_in = jnp.concatenate([w_query, w_key, w_value], 1)
    heads_grad = jnp.einsum("id,ih->dh", normed_one, heads_back, preferred_element_type=f32)
    low = jnp.concatenate([heads_grad.astype(bf16), out_low[:, : width // 2], out_low[:, width // 2 :]], 0)
    gain_one_part = jnp.sum(heads_grad * heads_in.astype(f32), 1) / gain_attn.astype(f32)
    small = jnp.concatenate([small[: EXPERTS + 1], gain_one_part[None], small[EXPERTS + 2 :]], 0)
    heads_back, low, part_sum, out_far, out_across = hold(heads_back, low, part_sum, out_far, out_across)
    out_got = line_in(out_parts[1], out_far)

    low_part = lax.psum_scatter(low, ("z", "y"), scatter_dimension=0, tiled=True)

    by_core = heads_back.reshape(shards // 2, 2, own_rows, -1)

    def rows_of(which):
        rows = lax.dynamic_index_in_dim(by_core, which, 1, keepdims=False)
        return lax.dot_general(rows, heads_in, (((2,), (1,)), ((), ())), preferred_element_type=f32)

    from_core = swap(rows_of(1 - c).astype(bf16), "c")
    core_sum = (rows_of(c) + from_core.astype(f32)).astype(bf16)
    core_got, low_part, out_got, small = hold(swap(core_sum, "x"), low_part, out_got, small)
    rest = total_over(small, ("c", "x", "y", "z"))
    moe_own = out_parts[0].astype(f32) + out_across.astype(f32) + out_got.astype(f32)
    block_output = (hidden_in + moe_own).astype(bf16)
    low_all = lax.all_gather(low_part, ("z", "y"), axis=0, tiled=True)
    summed_grads = expert_grads(part_sum)
    chip_sum = (core_sum.astype(f32) + core_got.astype(f32)).astype(bf16)
    other_sum = swap(chip_sum, "c")
    core = c.astype(jnp.int32)[None]
    gain_row = gain_attn[None]
    input_grad = finish(core, chip_sum.reshape(-1, width), tokens, hidden_all, gain_row, own_rows)
    other_sum, input_grad, *summed_grads = hold(other_sum, input_grad, *summed_grads)
    input_grad = finish(
        1 - core, other_sum.reshape(-1, width), tokens, hidden_all, gain_row, own_rows, (input_grad,)
    )
    smalls = rest[EXPERTS + 1], rest[EXPERTS], rest[:EXPERTS].T
    low_all, input_grad, block_output, *smalls = hold(low_all, input_grad, block_output, *smalls)
    heads = parted(low_all, (w_query.shape[1], w_key.shape[1], w_value.shape[1]))
    return (
        block_output,
        input_grad,
        smalls[0],
        *heads,
        smalls[1],
        smalls[2],
        *summed_grads,
    )


def group_gather(x, axes):
    return lax.all_gather(x, axes, axis=0, tiled=False)


def per_device_general(
    tokens,
    prefix,
    gain_attn,
    w_query,
    w_key,
    w_value,
    w_out,
    gain_moe,
    w_router,
    routes,
    fill_order,
    w_gate,
    w_up,
    w_down,
    cotangent,
):
    f32 = jnp.float32
    bf16 = jnp.bfloat16
    z_count = lax.axis_size("z")
    y_count = lax.axis_size("y")
    shards = lax.axis_size("x") * lax.axis_size("c")
    z_rank = lax.axis_index("z")
    tensor_rank = lax.axis_index("x") * lax.axis_size("c") + lax.axis_index("c")
    length = tokens.shape[0]
    model_width = tokens.shape[1]
    own_rows = routes.shape[0]
    local_experts = w_gate.shape[0]
    group_experts = local_experts * y_count
    capacity = own_rows * TOPK // EXPERTS
    heads_local = w_query.shape[1] // HD
    kv_local = w_key.shape[1] // HD
    group_size = heads_local // kv_local
    block_rows = min(512, length)
    block_count = length // block_rows
    score_scale = HD ** (-0.5)
    hidden = w_gate.shape[2] * shards

    expert_ids = jnp.arange(EXPERTS, dtype=jnp.int32)
    member = jnp.sum((routes[:, :, None] == expert_ids[None, None, :]).astype(f32), 1)
    priority = fill_order[0]
    earlier = (priority[None, :] < priority[:, None]).astype(bf16)
    slot_full = jnp.dot(earlier, member.astype(bf16), preferred_element_type=f32)
    slot_code = jnp.where(member > 0, jnp.minimum(slot_full, float(capacity)), -1.0).astype(bf16)

    weights_gate = group_gather(w_gate, ("y", "x", "c")).reshape(
        y_count, shards, local_experts, model_width, -1
    )
    weights_up = group_gather(w_up, ("y", "x", "c")).reshape(
        y_count, shards, local_experts, model_width, -1
    )
    weights_down = group_gather(w_down, ("y", "x", "c")).reshape(
        y_count, shards, local_experts, -1, model_width
    )
    weights_gate = weights_gate.transpose(0, 2, 3, 1, 4).reshape(group_experts, model_width, hidden)
    weights_up = weights_up.transpose(0, 2, 3, 1, 4).reshape(group_experts, model_width, hidden)
    weights_down = weights_down.transpose(0, 2, 1, 3, 4).reshape(group_experts, hidden, model_width)
    cot_all = lax.all_gather(cotangent, "z", axis=0, tiled=False)
    code_all = lax.all_gather(slot_code, "z", axis=0, tiled=False)

    x_full = tokens.astype(f32)
    rms_one = lax.rsqrt(jnp.mean(x_full * x_full, -1, keepdims=True) + EPSILON)
    gain_one = gain_attn.astype(f32)
    normed_one = (x_full * rms_one * gain_one).astype(bf16)
    query_raw = jnp.dot(normed_one, w_query, preferred_element_type=f32)
    key_raw = jnp.dot(normed_one, w_key, preferred_element_type=f32)
    values = (
        jnp.dot(normed_one, w_value, preferred_element_type=f32)
        .astype(bf16)
        .reshape(length, kv_local, HD)
    )
    cosine, sine = rope_tables(length, HD)
    query_rot = rotate(query_raw.reshape(length, heads_local, HD), cosine, sine, 1.0).astype(bf16)
    key_rot = rotate(key_raw.reshape(length, kv_local, HD), cosine, sine, 1.0).astype(bf16)
    query_blocks = query_rot.reshape(block_count, block_rows, kv_local, group_size, HD)
    block_starts = jnp.arange(block_count, dtype=jnp.int32) * block_rows
    positions = jnp.arange(length, dtype=jnp.int32)
    prefix_len = prefix[0]

    def block_scores(query_block, offset):
        query_pos = offset + jnp.arange(block_rows, dtype=jnp.int32)
        raw_scores = (
            jnp.einsum("igjd,kgd->gjik", query_block, key_rot, preferred_element_type=jnp.float32)
            * score_scale
        )
        visible = (positions[None, :] <= query_pos[:, None]) | (positions[None, :] < prefix_len)
        return jnp.where(visible[None, None], raw_scores, -1e30)

    def attend_block(inputs):
        query_block, offset = inputs
        scores = block_scores(query_block, offset)
        row_peak = jnp.max(scores, -1, keepdims=True)
        weights = jnp.exp(scores - row_peak)
        row_total = jnp.sum(weights, -1, keepdims=True)
        probabilities = (weights / row_total).astype(jnp.bfloat16)
        attended = jnp.einsum(
            "gjik,kgd->igjd", probabilities, values, preferred_element_type=jnp.float32
        )
        return (attended.astype(jnp.bfloat16), (row_peak + jnp.log(row_total))[..., 0])

    attended_blocks, log_totals = lax.map(attend_block, (query_blocks, block_starts))
    attended_all = attended_blocks.reshape(length, heads_local * HD)
    attention_rows = lax.psum_scatter(
        jnp.dot(attended_all, w_out, preferred_element_type=f32).astype(bf16),
        ("x", "c"),
        scatter_dimension=0,
        tiled=True,
    ).astype(f32)
    x_rows = lax.dynamic_slice_in_dim(tokens, tensor_rank * own_rows, own_rows, 0).astype(f32)
    hidden_in = x_rows + attention_rows
    rms_two = lax.rsqrt(jnp.mean(hidden_in * hidden_in, -1, keepdims=True) + EPSILON)
    gain_two = gain_moe.astype(f32)
    normed_two = (hidden_in * rms_two * gain_two).astype(bf16)
    normed_all = lax.all_gather(normed_two, "z", axis=0, tiled=False)

    def gates(rows, code):
        logits = jnp.dot(rows, w_router, preferred_element_type=f32)
        chosen = jnp.where(code >= 0, logits, -jnp.inf)
        raised = jnp.exp(chosen - jnp.max(chosen, -1, keepdims=True))
        return raised / jnp.sum(raised, -1, keepdims=True)

    gate_own = gates(normed_two, slot_code)
    first = z_rank * group_experts
    gate_all = jax.vmap(gates)(normed_all, code_all)
    gate_group = lax.dynamic_slice_in_dim(gate_all, first, group_experts, 2)
    code_group = lax.dynamic_slice_in_dim(code_all, first, group_experts, 2).astype(jnp.int32)
    slot_ids = jnp.arange(capacity, dtype=jnp.int32)
    hot = code_group.transpose(2, 0, 1)[:, :, None, :] == slot_ids[None, None, :, None]
    pick = hot.astype(bf16)
    pick_gate = jnp.where(hot, gate_group.transpose(2, 0, 1)[:, :, None, :], 0.0)
    gate_slot = jnp.sum(pick_gate, -1)
    rows_in = jnp.einsum("esci,sid->escd", pick, normed_all, preferred_element_type=f32).astype(bf16)
    rows_dy = jnp.einsum("esci,sid->escd", pick, cot_all, preferred_element_type=f32)
    gate_pre = jnp.einsum("escd,edf->escf", rows_in, weights_gate, preferred_element_type=f32)
    up_pre = jnp.einsum("escd,edf->escf", rows_in, weights_up, preferred_element_type=f32)
    activated = (gate_pre / (1.0 + jnp.exp(-gate_pre)) * up_pre).astype(bf16)
    expert_out = jnp.einsum(
        "escf,efd->escd", activated, weights_down, preferred_element_type=f32
    ).astype(bf16)
    out_grad_rows = (rows_dy * gate_slot[..., None]).astype(bf16)
    gate_grad_slot = jnp.sum(rows_dy * expert_out.astype(f32), -1)
    gate_grad = jnp.einsum("esci,esc->sie", pick.astype(f32), gate_grad_slot, precision=HIGHEST)
    moe_part = jnp.einsum(
        "esci,escd->sid", pick_gate.astype(bf16), expert_out, preferred_element_type=f32
    ).astype(bf16)
    hid_grad = jnp.einsum("escd,efd->escf", out_grad_rows, weights_down, preferred_element_type=f32)
    sigmoid_g = 1.0 / (1.0 + jnp.exp(-gate_pre))
    back_gate = (hid_grad * up_pre * sigmoid_g * (1.0 + gate_pre * (1.0 - sigmoid_g))).astype(bf16)
    back_up = (hid_grad * gate_pre * sigmoid_g).astype(bf16)
    rows_grad = (
        jnp.einsum("escf,edf->escd", back_gate, weights_gate, preferred_element_type=f32)
        + jnp.einsum("escf,edf->escd", back_up, weights_up, preferred_element_type=f32)
    ).astype(bf16)
    rows_part = jnp.einsum("esci,escd->sid", pick, rows_grad, preferred_element_type=f32).astype(bf16)
    down_part = jnp.einsum("escf,escd->efd", activated, out_grad_rows, preferred_element_type=f32)
    gate_part = jnp.einsum("escd,escf->edf", rows_in, back_gate, preferred_element_type=f32)
    up_part = jnp.einsum("escd,escf->edf", rows_in, back_up, preferred_element_type=f32)

    gate_grad_wide = lax.dynamic_update_slice_in_dim(
        jnp.zeros((z_count, own_rows, EXPERTS), f32), gate_grad, first, 2
    )
    back_pack = jnp.concatenate([rows_part, gate_grad_wide.astype(bf16)], -1)
    back_own = lax.psum_scatter(back_pack, "z", scatter_dimension=0, tiled=False).astype(f32)
    moe_own = lax.psum_scatter(moe_part, "z", scatter_dimension=0, tiled=False).astype(f32)
    block_output = (hidden_in + moe_own).astype(bf16)

    def shard_sum(part, dim):
        width = part.shape[dim] // shards
        split = part.reshape((y_count, local_experts) + part.shape[1:dim] + (shards, width) + part.shape[dim + 1 :])
        split = jnp.moveaxis(split, dim + 1, 1).astype(bf16)
        split = split.reshape((y_count * shards,) + split.shape[2:])
        return lax.psum_scatter(split, ("y", "x", "c"), scatter_dimension=0, tiled=False).astype(f32)

    grad_gate = shard_sum(gate_part, 2)
    grad_up = shard_sum(up_part, 2)
    grad_down = shard_sum(down_part, 1)

    normed_two_grad = back_own[:, :model_width]
    gate_grad_own = back_own[:, model_width:]
    logit_grad = gate_own * (
        gate_grad_own - jnp.sum(gate_own * gate_grad_own, -1, keepdims=True)
    )
    router_part = jnp.dot(normed_two.astype(f32).T, logit_grad, precision=HIGHEST)
    normed_two_grad = normed_two_grad + jnp.dot(
        logit_grad, w_router.astype(f32).T, precision=HIGHEST
    )
    gain_two_part = jnp.sum(normed_two_grad * hidden_in * rms_two, 0)
    scaled_two = normed_two_grad * gain_two
    grad_rows = cotangent.astype(f32)
    hidden_grad = (
        grad_rows
        + rms_two * scaled_two
        - hidden_in * rms_two**3 * jnp.mean(scaled_two * hidden_in, -1, keepdims=True)
    )
    shard_part = lax.all_gather(
        hidden_grad.astype(bf16), ("x", "c"), axis=0, tiled=True
    ).astype(f32)
    attended_part = jnp.einsum(
        "id,hd->ih", shard_part.astype(jnp.bfloat16), w_out, preferred_element_type=jnp.float32
    )
    attended_grad = attended_part.astype(jnp.bfloat16)
    out_grad = jnp.einsum(
        "ih,id->hd",
        attended_all,
        shard_part.astype(jnp.bfloat16),
        preferred_element_type=jnp.float32,
    )
    grad_blocks = attended_grad.reshape(block_count, block_rows, kv_local, group_size, HD)

    def back_block(running, inputs):
        key_acc, value_acc = running
        query_block, grad_block, log_block, offset = inputs
        scores = block_scores(query_block, offset)
        probabilities = jnp.exp(scores - log_block[..., None])
        prob_grad = jnp.einsum(
            "igjd,kgd->gjik", grad_block, values, preferred_element_type=jnp.float32
        )
        center = jnp.sum(prob_grad * probabilities, -1, keepdims=True)
        score_grad = (probabilities * (prob_grad - center)).astype(jnp.bfloat16)
        query_grad = (
            jnp.einsum("gjik,kgd->igjd", score_grad, key_rot, preferred_element_type=jnp.float32)
            * score_scale
        )
        key_acc = (
            key_acc
            + jnp.einsum(
                "gjik,igjd->kgd", score_grad, query_block, preferred_element_type=jnp.float32
            )
            * score_scale
        )
        value_acc = value_acc + jnp.einsum(
            "gjik,igjd->kgd",
            probabilities.astype(jnp.bfloat16),
            grad_block,
            preferred_element_type=jnp.float32,
        )
        return ((key_acc, value_acc), query_grad)

    zero_kv = jnp.zeros((length, kv_local, HD), jnp.float32)
    (key_grad, value_grad), query_grads = lax.scan(
        back_block, (zero_kv, zero_kv), (query_blocks, grad_blocks, log_totals, block_starts)
    )
    query_back = (
        rotate(query_grads.reshape(length, heads_local, HD), cosine, sine, -1.0)
        .reshape(length, heads_local * HD)
        .astype(jnp.bfloat16)
    )
    key_back = (
        rotate(key_grad, cosine, sine, -1.0).reshape(length, kv_local * HD).astype(jnp.bfloat16)
    )
    value_back = value_grad.reshape(length, kv_local * HD).astype(jnp.bfloat16)
    query_weight = jnp.einsum(
        "id,ih->dh", normed_one, query_back, preferred_element_type=jnp.float32
    )
    key_weight = jnp.einsum("id,ih->dh", normed_one, key_back, preferred_element_type=jnp.float32)
    value_weight = jnp.einsum(
        "id,ih->dh", normed_one, value_back, preferred_element_type=jnp.float32
    )
    normed_one_grad = jnp.einsum(
        "ih,dh->id", query_back, w_query, preferred_element_type=jnp.float32
    )
    normed_one_grad = normed_one_grad + jnp.einsum(
        "ih,dh->id", key_back, w_key, preferred_element_type=jnp.float32
    )
    normed_one_grad = normed_one_grad + jnp.einsum(
        "ih,dh->id", value_back, w_value, preferred_element_type=jnp.float32
    )
    total_one = lax.psum(normed_one_grad.astype(bf16), ("x", "c")).astype(f32)
    gain_one_part = jnp.sum(normed_one_grad * x_full * rms_one, 0)
    scaled_one = total_one * gain_one
    input_grad = (
        shard_part
        + rms_one * scaled_one
        - x_full * rms_one**3 * jnp.mean(scaled_one * x_full, -1, keepdims=True)
    )
    dp = ("z", "y")
    everyone = ("z", "y", "x", "c")
    summed = [
        lax.psum(part.astype(bf16), dp).astype(f32)
        for part in (query_weight, key_weight, value_weight, out_grad)
    ]
    router_total, gain_one_total, gain_two_total = (
        lax.psum(part.astype(bf16), everyone).astype(f32)
        for part in (router_part, gain_one_part, gain_two_part)
    )
    return (
        block_output,
        input_grad,
        gain_one_total,
        summed[0],
        summed[1],
        summed[2],
        summed[3],
        gain_two_total,
        router_total,
        grad_gate,
        grad_up,
        grad_down,
    )


def solution(mesh):
    dp_count, tensor_count = mesh.devices.shape
    mesh = jax.sharding.Mesh(
        mesh.devices.reshape(dp_count // 2, 2, tensor_count // 2, 2), ("z", "y", "x", "c")
    )
    fast = mesh.devices.shape == (4, 2, 2, 2)
    dp = ("z", "y")
    tensor = ("x", "c")
    both = dp + tensor
    return jax.shard_map(
        per_device_fast if fast else per_device_general,
        mesh=mesh,
        in_specs=(
            P(dp, None),
            P(dp),
            P(),
            P(None, tensor),
            P(None, tensor),
            P(None, tensor),
            P(tensor, None),
            P(),
            P(),
            P(both, None),
            P(both, None),
            P(dp, None, tensor),
            P(dp, None, tensor),
            P(dp, tensor, None),
            P(both, None),
        ),
        out_specs=(
            P(both, None),
            P(dp, None),
            P(),
            P(None, tensor),
            P(None, tensor),
            P(None, tensor),
            P(tensor, None),
            P(),
            P(),
            P(dp, None, tensor),
            P(dp, None, tensor),
            P(dp, tensor, None),
        ),
        check_vma=False,
    )
```

```python
import functools

import jax
import jax.numpy as jnp
import numpy as np
from jax import lax
from jax.experimental import pallas as pl
from jax.experimental.pallas import tpu as pltpu
from jax.sharding import PartitionSpec as P

HD = 64
EXPERTS = 32
TOPK = 8


EPSILON = 1e-06
THETA_BASE = 10000.0
HIGHEST = lax.Precision.HIGHEST


def rope_tables(length, width_in):
    half_width = width_in // 2
    frequency = THETA_BASE ** (-(jnp.arange(half_width, dtype=jnp.float32) / half_width))
    angles = jnp.arange(length, dtype=jnp.float32)[:, None] * frequency[None, :]
    return (jnp.cos(angles), jnp.sin(angles))


def rotate(vectors, cosine, sine, direction):
    half_width = vectors.shape[-1] // 2
    front_half = vectors[..., :half_width]
    back_half = vectors[..., half_width:]
    cos_part = cosine[:, None, :]
    sin_part = sine[:, None, :] * direction
    return jnp.concatenate(
        [
            front_half * cos_part - back_half * sin_part,
            back_half * cos_part + front_half * sin_part,
        ],
        -1,
    )


NT = (((1,), (1,)), ((), ()))
TN = (((0,), (0,)), ((), ()))
f32 = jnp.float32
bf16 = jnp.bfloat16
BQ = 512
BK = 1024
BK_BACK = 512

def from_hbm(*arrays):
    return [pltpu.with_memory_space_constraint(a, pltpu.HBM) for a in arrays]


def busy(us):
    return pl.CostEstimate(flops=int(us * 1e8), bytes_accessed=0, transcendentals=0)


def lanes(shape):
    return lax.broadcasted_iota(jnp.int32, shape, len(shape) - 1)

def rope_wide(v, cos, sin):
    low = lanes(v.shape) % HD < HD // 2
    swapped = jnp.where(low, pltpu.roll(v, 128 - HD // 2, 1), pltpu.roll(v, HD // 2, 1))
    return v * cos + swapped * sin

def project_kernel(x_ref, gain_ref, wq_ref, wk_ref, wv_ref, cos_ref, sin_ref, a_ref, q_ref, k_ref, v_ref):
    x = x_ref[...].astype(f32)
    r = lax.rsqrt(jnp.mean(x * x, -1, keepdims=True) + EPSILON)
    a = (x * r * gain_ref[...].astype(f32)).astype(bf16)
    a_ref[...] = a
    cos, sin = cos_ref[...], sin_ref[...]
    k = jnp.dot(a, wk_ref[...], preferred_element_type=f32)
    k_ref[...] = rope_wide(k, cos, sin).astype(bf16)
    v = jnp.dot(a, wv_ref[...], preferred_element_type=f32).astype(bf16)
    v_ref[:, :128] = v
    v_ref[:, 128:] = jnp.ones_like(v)
    low = lanes(k.shape) < HD
    for pair in range(2):
        q = jnp.dot(a, wq_ref[:, pair * 128 : pair * 128 + 128], preferred_element_type=f32)
        q = rope_wide(q, cos, sin) * HD ** (-0.5)
        other = pltpu.roll(q, HD, 1)
        mine = low if pair == 0 else ~low
        first, second = (q, other) if pair == 0 else (other, q)
        q_ref[2 * pair] = jnp.where(mine, first, 0.0).astype(bf16)
        q_ref[2 * pair + 1] = jnp.where(mine, second, 0.0).astype(bf16)

def project(tokens, gain, wq, wk, wv, cos, sin):
    L, D = tokens.shape
    B = 256
    full = lambda a: pl.BlockSpec(a.shape, lambda i: (0,) * a.ndim)
    rows = lambda w: pl.BlockSpec((B, w), lambda i: (i, 0))
    return pl.pallas_call(
        project_kernel, grid=(L // B,),
        in_specs=[rows(D), full(gain), full(wq), full(wk), full(wv), rows(128), rows(128)],
        out_specs=[rows(D), pl.BlockSpec((4, B, 128), lambda i: (0, i, 0)), rows(128), rows(256)],
        out_shape=[pltpu.HBM((L, D), bf16), pltpu.HBM((4, L, 128), bf16), pltpu.HBM((L, 128), bf16), pltpu.HBM((L, 256), bf16)],
        compiler_params=pltpu.CompilerParams(vmem_limit_bytes=40 << 20),
        cost_estimate=busy(9),
        name="project",
    )(*from_hbm(tokens), gain, wq, wk, wv, cos, sin)

def attend_kernel(bq, bk, kv, prefix_ref, q_ref, k_ref, v_ref, *refs):
    o_ref, lse_ref, s_ref = refs[-3:]
    i = pl.program_id(0)
    start = i * bq
    prefix = prefix_ref[0]
    full_blocks = jnp.maximum(start + 1, prefix) // bk
    all_blocks = (jnp.maximum(start + bq, prefix) + bk - 1) // bk
    rows = 2 * bq
    pos = start + lax.broadcasted_iota(jnp.int32, (rows, 1), 0) % bq
    limit = jnp.maximum(pos, prefix - 1)
    low = lanes((bq, 128)) < HD
    q = jnp.concatenate([q_ref[0], q_ref[1]], 0)

    def tile_max(s, peak):
        for c in range(bk // 128):
            peak = jnp.maximum(peak, s[:, c * 128 : c * 128 + 128])
        return peak

    def plain(j, peak):
        off = pl.multiple_of(j * bk, bk)
        s = lax.dot_general(q, k_ref[pl.ds(off, bk), :], NT, preferred_element_type=f32)
        s_ref[:, pl.ds(off, bk)] = s
        return tile_max(s, peak)

    def masked(j, peak):
        off = pl.multiple_of(j * bk, bk)
        s = lax.dot_general(q, k_ref[pl.ds(off, bk), :], NT, preferred_element_type=f32)
        s = jnp.where(lanes((rows, bk)) <= limit - off, s, -1e30)
        s_ref[:, pl.ds(off, bk)] = s
        return tile_max(s, peak)

    peak = jnp.full((rows, 128), -1e30, f32)
    peak = lax.fori_loop(0, full_blocks, plain, peak)
    peak = lax.fori_loop(full_blocks, all_blocks, masked, peak)
    peak = jnp.max(peak, -1, keepdims=True)

    def weigh(j, acc):
        off = pl.multiple_of(j * bk, bk)
        p = jnp.exp(s_ref[:, pl.ds(off, bk)] - peak).astype(bf16)
        return acc + jnp.dot(p, v_ref[pl.ds(off, bk), :], preferred_element_type=f32)

    acc = lax.fori_loop(0, all_blocks, weigh, jnp.zeros((rows, 256), f32))
    total = acc[:, 128:]
    out = acc[:, :128] / total
    one, two = out[:bq], out[bq:]
    if kv == 0:
        merged = jnp.where(low, one, pltpu.roll(two, HD, 1))
    else:
        merged = jnp.where(low, pltpu.roll(one, HD, 1), two)
    o_ref[...] = merged.astype(bf16)
    lse = (peak + jnp.log(total)).T
    lse_ref[0] = lse[:8]


def attend(prefix, q, k, v, kv, bq, bk, before=()):
    L = k.shape[0]
    return pl.pallas_call(
        functools.partial(attend_kernel, bq, bk, kv),
        grid_spec=pltpu.PrefetchScalarGridSpec(
            num_scalar_prefetch=1, grid=(L // bq,),
            in_specs=[pl.BlockSpec((2, bq, 128), lambda i, p: (kv, i, 0)),
                      pl.BlockSpec((L, 128), lambda i, p: (0, 0)),
                      pl.BlockSpec((L, 256), lambda i, p: (0, 0))]
            + [pl.BlockSpec(memory_space=pl.ANY)] * len(before),
            out_specs=[pl.BlockSpec((bq, 128), lambda i, p: (i, kv)),
                       pl.BlockSpec((1, 8, 2 * bq), lambda i, p: (kv, 0, i))],
            scratch_shapes=[pltpu.VMEM((2 * bq, L), f32)]),
        out_shape=[pltpu.HBM((L, 256), bf16), pltpu.HBM((2, 8, 2 * L), f32)],
        input_output_aliases={4 + i: i for i in range(len(before))},
        compiler_params=pltpu.CompilerParams(vmem_limit_bytes=48 << 20),
        cost_estimate=busy(14),
        name="attend",
    )(prefix, *from_hbm(q, k, v), *before)


def attend_back_kernel(bq, bk, prefix_ref, q_ref, k_ref, v_ref, o_ref, do_ref, lse_ref, cos_ref, sin_ref, cosa_ref, sina_ref,
                       out_ref, dk_acc, dv_acc, dq_acc):
    i = pl.program_id(0)
    start = i * bq
    prefix = prefix_ref[0]
    full_blocks = jnp.maximum(start + 1, prefix) // bk
    all_blocks = (jnp.maximum(start + bq, prefix) + bk - 1) // bk
    rows = 2 * bq
    pos = start + lax.broadcasted_iota(jnp.int32, (1, rows), 1) % bq
    limit = jnp.maximum(pos, prefix - 1)
    low = lanes((bq, 128)) < HD

    @pl.when(i == 0)
    def _():
        dk_acc[...] = jnp.zeros_like(dk_acc)
        dv_acc[...] = jnp.zeros_like(dv_acc)

    heads = []
    for kv in range(2):
        q = jnp.concatenate([q_ref[2 * kv], q_ref[2 * kv + 1]], 0)
        mine = low if kv == 0 else ~low
        pair = do_ref[:, kv * 128 : kv * 128 + 128].astype(f32)
        swap = pltpu.roll(pair, HD, 1)
        first, second = (pair, swap) if kv == 0 else (swap, pair)
        do = jnp.concatenate([jnp.where(mine, first, 0.0), jnp.where(mine, second, 0.0)], 0).astype(bf16)
        prod = pair * o_ref[:, kv * 128 : kv * 128 + 128].astype(f32)
        one = jnp.sum(jnp.where(low, prod, 0.0), -1, keepdims=True)
        two = jnp.sum(jnp.where(low, 0.0, prod), -1, keepdims=True)
        center = jnp.broadcast_to(jnp.concatenate([one, two], 0), (rows, 128)).T[:1]
        heads.append((q, do, center, lse_ref[kv, :1, :]))
    dq_acc[...] = jnp.zeros_like(dq_acc)

    def step(j, _, mask):
        off = pl.multiple_of(j * bk, bk)
        kb = k_ref[pl.ds(off, bk), :]
        vb = v_ref[pl.ds(off, bk), :128]
        dvs, dks = [], []
        for kv, (q, do, center, lse) in enumerate(heads):
            s = lax.dot_general(kb, q, NT, preferred_element_type=f32)
            dp = lax.dot_general(vb, do, NT, preferred_element_type=f32)
            if mask:
                s = jnp.where(off + lax.broadcasted_iota(jnp.int32, (bk, rows), 0) <= limit, s, -1e30)
            p = jnp.exp(s - lse)
            ds = (p * (dp - center)).astype(bf16)
            dvs.append(jnp.dot(p.astype(bf16), do, preferred_element_type=f32))
            dks.append(jnp.dot(ds, q, preferred_element_type=f32))
            dq_acc[kv] += lax.dot_general(ds, kb, TN, preferred_element_type=f32)
        dv_acc[pl.ds(off, bk), :] += dvs[0] + dvs[1]
        dk_acc[pl.ds(off, bk), :] += dks[0] + dks[1]
        return 0

    lax.fori_loop(0, full_blocks, functools.partial(step, mask=False), 0)
    lax.fori_loop(full_blocks, all_blocks, functools.partial(step, mask=True), 0)
    for kv in range(2):
        dq = dq_acc[kv] * HD ** (-0.5)
        one, two = dq[:bq], dq[bq:]
        if kv == 0:
            merged = jnp.where(low, one, pltpu.roll(two, HD, 1))
        else:
            merged = jnp.where(low, pltpu.roll(one, HD, 1), two)
        out_ref[pl.ds(pl.multiple_of(start, bq), bq), kv * 128 : kv * 128 + 128] = rope_wide(merged, cos_ref[...], -sin_ref[...]).astype(bf16)

    @pl.when(i == pl.num_programs(0) - 1)
    def _():
        for b in range(dk_acc.shape[0] // bq):
            r = pl.ds(b * bq, bq)
            out_ref[r, 256:384] = rope_wide(dk_acc[r, :], cosa_ref[r, :], -sina_ref[r, :]).astype(bf16)
            out_ref[r, 384:] = dv_acc[r, :].astype(bf16)

def attend_back(prefix, q, k, v, o, do, lse, cos, sin, bq=256, bk=256):
    L = k.shape[0]
    fullL = pl.BlockSpec((L, 128), lambda i, p: (0, 0))
    return pl.pallas_call(
        functools.partial(attend_back_kernel, bq, bk),
        grid_spec=pltpu.PrefetchScalarGridSpec(
            num_scalar_prefetch=1, grid=(L // bq,),
            in_specs=[pl.BlockSpec((4, bq, 128), lambda i, p: (0, i, 0)), fullL,
                      pl.BlockSpec((L, 256), lambda i, p: (0, 0)),
                      pl.BlockSpec((bq, 256), lambda i, p: (i, 0)),
                      pl.BlockSpec((bq, 256), lambda i, p: (i, 0)),
                      pl.BlockSpec((2, 8, 2 * bq), lambda i, p: (0, 0, i)),
                      pl.BlockSpec((bq, 128), lambda i, p: (i, 0)),
                      pl.BlockSpec((bq, 128), lambda i, p: (i, 0)), fullL, fullL],
            out_specs=pl.BlockSpec((L, 512), lambda i, p: (0, 0)),
            scratch_shapes=[pltpu.VMEM((L, 128), f32), pltpu.VMEM((L, 128), f32), pltpu.VMEM((2, 2 * bq, 128), f32)]),
        out_shape=jax.ShapeDtypeStruct((L, 512), bf16),
        compiler_params=pltpu.CompilerParams(vmem_limit_bytes=48 << 20),
        cost_estimate=busy(46),
        name="attend_back",
    )(prefix, q, k, v, o, do, lse, cos, sin, cos, sin)


def pick_kernel(experts, per, cap, pairs, shift_ref, *refs):
    in_ref, dyo_ref, gs_ref, gate_ref, code_ref, code_t, gate_t, rows_s, dy_s = refs[-9:]
    tokens, width = rows_s.shape

    @pl.when(pl.program_id(0) == 0)
    def _():
        if pairs:
            rows_ref, rows_other, side_ref, side_other, router_ref = refs[:5]
            first = shift_ref[experts] != 0
            rows = jnp.where(first, rows_ref[...], rows_other[...])
            side = jnp.where(first, side_ref[...], side_other[...])
        else:
            rows_ref, side_ref, router_ref = refs[:3]
            rows, side = rows_ref[...], side_ref[...]
        rows_s[...] = rows
        dy_s[...] = side[:, :width]
        code = side[:, width:].astype(f32)
        code_ref[...] = code
        logits = jnp.dot(rows, router_ref[...], preferred_element_type=f32)
        chosen = jnp.where(code >= 0, logits, -1e30)
        raised = jnp.where(code >= 0, jnp.exp(chosen - jnp.max(chosen, -1, keepdims=True)), 0.0)
        gate = raised / jnp.sum(raised, -1, keepdims=True)
        gate_ref[...] = gate
        gate_t[...] = gate.T
        code_t[...] = code.T

    hots = []
    for e in range(per):
        row = pl.ds(shift_ref[pl.program_id(0) * per + e], 1)
        hot = code_t[row, :] == lax.broadcasted_iota(jnp.int32, (cap, tokens), 0).astype(f32)
        gs = jnp.sum(jnp.where(hot, gate_t[row, :], 0.0), -1, keepdims=True)
        gs_ref[e] = jnp.broadcast_to(gs, (cap, 128))
        hots.append(hot.astype(bf16))
    hot = jnp.concatenate(hots, 0)
    in_ref[...] = jnp.dot(hot, rows_s[...], preferred_element_type=f32).astype(bf16).reshape(in_ref.shape)
    dyo_ref[...] = jnp.dot(hot, dy_s[...], preferred_element_type=f32).astype(bf16).reshape(dyo_ref.shape)


def pick(shift, rows, sides, router, cap):
    R, D = rows[0].shape
    E = shift.shape[0] - 1
    W = router.shape[1]
    per = 4
    operands = [*rows, *sides, router]
    whole = lambda a: pl.BlockSpec(a.shape, lambda e: (0, 0))
    some = lambda w: pl.BlockSpec((per, cap, w), lambda e: (e, 0, 0))
    wide = pl.BlockSpec((R, W), lambda e: (0, 0))
    return pl.pallas_call(
        functools.partial(pick_kernel, E, per, cap, len(rows) == 2),
        grid=(E // per,),
        in_specs=[pl.BlockSpec(memory_space=pltpu.SMEM)] + [whole(a) for a in operands],
        out_specs=[some(D), some(D), some(128), wide, wide],
        out_shape=[pltpu.HBM((E, cap, D), bf16), pltpu.HBM((E, cap, D), bf16),
                   pltpu.HBM((E, cap, 128), f32), jax.ShapeDtypeStruct((R, W), f32), jax.ShapeDtypeStruct((R, W), f32)],
        scratch_shapes=[pltpu.VMEM((W, R), f32), pltpu.VMEM((W, R), f32), pltpu.VMEM((R, D), bf16), pltpu.VMEM((R, D), bf16)],
        compiler_params=pltpu.CompilerParams(vmem_limit_bytes=40 << 20),
        cost_estimate=busy(4),
        name="pick",
    )(shift, *operands)


def ffn_kernel(n, blocks, *refs):
    rows_refs, dy_refs, gs_refs = refs[:n], refs[n : 2 * n], refs[2 * n : 3 * n]
    w_ref = refs[3 * n]
    eout_ref, drows_ref, dgs_ref, act_ref, dgu_ref = refs[-5:]
    cap, D = rows_refs[0].shape[1:]
    M = n * cap
    rows = jnp.concatenate([r[0] for r in rows_refs], 0)
    dy = jnp.concatenate([r[0] for r in dy_refs], 0)
    gs = jnp.concatenate([r[0] for r in gs_refs], 0)
    dout = (dy.astype(f32) * gs[:, :1]).astype(bf16)
    F = w_ref.shape[-1]
    w = jnp.concatenate([w_ref[0, b, part, 0] for b in range(blocks) for part in (0, 1)], 1)
    wd = jnp.concatenate([w_ref[0, b, 2, 0] for b in range(blocks)], 1)
    gu = jnp.dot(rows, w, preferred_element_type=f32)
    dacts = jnp.dot(dout, wd, preferred_element_type=f32)
    acts, dgus = [], []
    for b in range(blocks):
        g, u = gu[:, 2 * b * F : (2 * b + 1) * F], gu[:, (2 * b + 1) * F : (2 * b + 2) * F]
        dact = dacts[:, b * F : (b + 1) * F]
        sg = 1.0 / (1.0 + jnp.exp(-g))
        gsg = g * sg
        acts.append((gsg * u).astype(bf16))
        dgus.append((dact * u * (sg + gsg * (1.0 - sg))).astype(bf16))
        dgus.append((dact * gsg).astype(bf16))
    act = jnp.concatenate(acts, 1)
    dgu = jnp.concatenate(dgus, 1)
    act_ref[0] = act
    dgu_ref[0] = dgu
    drows = lax.dot_general(dgu, w, NT, preferred_element_type=f32)
    eout = lax.dot_general(act, wd, NT, preferred_element_type=f32)
    eout = eout.astype(bf16)
    eout_ref[0] = eout
    drows_ref[0] = drows.astype(bf16)
    dgs = jnp.sum(dy.astype(f32) * eout.astype(f32), -1, keepdims=True)
    dgs_ref[0] = jnp.broadcast_to(dgs, (M, 128))


def ffn(picked, weights, groups, before=()):
    n = len(picked)
    total, cap, D = picked[0][0].shape
    _, blocks, _, E, _, F = weights.shape
    H = blocks * F
    M = n * cap
    first = groups[0] * E
    spec = lambda w: pl.BlockSpec((1, cap, w), lambda e: (e + first, 0, 0))
    outs = lambda w: pl.BlockSpec((1, M, w), lambda e: (e + first, 0, 0))
    wsp = pl.BlockSpec((1, blocks, 3, 1, D, F), lambda e: ((e + first) // E, 0, 0, (e + first) % E, 0, 0))
    sh = lambda w, t: pltpu.HBM((total, M, w), t)
    operands = [p[i] for i in range(3) for p in picked] + [weights]
    return pl.pallas_call(
        functools.partial(ffn_kernel, n, blocks), grid=(len(groups) * E,),
        in_specs=[spec(D)] * (2 * n) + [spec(128)] * n + [wsp] + [pl.BlockSpec(memory_space=pl.ANY)] * len(before),
        out_specs=[outs(D), outs(D), outs(128), outs(H), outs(2 * H)],
        out_shape=[sh(D, bf16), sh(D, bf16), sh(128, f32), sh(H, bf16), sh(2 * H, bf16)],
        input_output_aliases={len(operands) + i: i for i in range(len(before))},
        compiler_params=pltpu.CompilerParams(vmem_limit_bytes=56 << 20),
        cost_estimate=busy(12 * len(groups)),
        name="ffn",
    )(*operands, *before)


def wgrad_kernel(n, halves, blocks, *refs):
    rows_refs, dy_refs, gs_refs = refs[:n], refs[n : 2 * n], refs[2 * n : 3 * n]
    act_refs, dgu_refs, out_ref = refs[3 * n : 3 * n + halves], refs[3 * n + halves : 3 * n + 2 * halves], refs[-1]
    rows = jnp.concatenate([r[0] for r in rows_refs], 0)
    dy = jnp.concatenate([r[0] for r in dy_refs], 0)
    gs = jnp.concatenate([r[0] for r in gs_refs], 0)
    dout = (dy.astype(f32) * gs[:, :1]).astype(bf16)
    F = act_refs[0].shape[2] // blocks
    for b in range(blocks):
        dgu = jnp.concatenate([r[0, :, b * 2 * F : (b + 1) * 2 * F] for r in dgu_refs], 0)
        g = lax.dot_general(rows, dgu, TN, preferred_element_type=f32).astype(bf16)
        out_ref[0, b, 0, 0] = g[:, :F]
        out_ref[0, b, 1, 0] = g[:, F:]
    for pair in range(0, blocks, 2):
        act = jnp.concatenate([r[0, :, pair * F : (pair + 2) * F] for r in act_refs], 0)
        gd = lax.dot_general(dout, act, TN, preferred_element_type=f32).astype(bf16)
        out_ref[0, pair, 2, 0] = gd[:, :F]
        out_ref[0, pair + 1, 2, 0] = gd[:, F:]


def wgrad(picked, acts, dgus, blocks, groups):
    n = len(picked)
    total, cap, D = picked[0][0].shape
    H = acts[0].shape[2]
    F = H // blocks
    E = total // groups
    spec = lambda w: pl.BlockSpec((1, cap, w), lambda e: (e, 0, 0))
    wide = lambda a: pl.BlockSpec((1,) + a.shape[1:], lambda e: (e, 0, 0))
    operands = [*[p[i] for i in range(3) for p in picked], *acts, *dgus]
    return pl.pallas_call(
        functools.partial(wgrad_kernel, n, len(acts), blocks),
        grid=(total,),
        in_specs=[spec(D)] * (2 * n) + [spec(128)] * n + [wide(a) for a in (*acts, *dgus)],
        out_specs=pl.BlockSpec((1, blocks, 3, 1, D, F), lambda e: (e // E, 0, 0, e % E, 0, 0)),
        out_shape=pltpu.HBM((groups, blocks, 3, E, D, F), bf16),
        compiler_params=pltpu.CompilerParams(vmem_limit_bytes=56 << 20),
        cost_estimate=busy(26),
        name="wgrad",
    )(*operands)


def hot_columns(code, shift, cap):
    col = jnp.sum(jnp.where(lanes(code.shape) == shift, code, 0.0), -1, keepdims=True)
    return col == lanes((code.shape[0], cap)).astype(f32)


def merge_back_kernel(n, E, cap, shift_ref, *refs):
    sides, (d_ref, g_ref), outs = refs[:n], refs[n : n + 2], refs[n + 2 :]
    D = d_ref.shape[2]
    lane = lanes((cap, 128))
    for source in range(n):

        @pl.when(pl.program_id(0) == source)
        def _():
            code = sides[source][...]
            total = jnp.zeros((code.shape[0], D), f32)
            gates = jnp.zeros((code.shape[0], 128), f32)
            for e0 in range(0, E, 4):
                some = range(e0, min(e0 + 4, E))
                hot = jnp.concatenate([hot_columns(code, shift_ref[e], cap).astype(bf16) for e in some], 1)
                rows = jnp.concatenate([d_ref[e] for e in some], 0)
                side = jnp.concatenate([jnp.where(lane == shift_ref[e], g_ref[e], 0.0).astype(bf16) for e in some], 0)
                total = total + jnp.dot(hot, rows, preferred_element_type=f32)
                gates = gates + jnp.dot(hot, side, preferred_element_type=f32)
            outs[source][:, :D] = total.astype(bf16)
            outs[source][:, D:] = gates.astype(bf16)


def merge_back(shift, codes, drows, dgs, cap):
    n = len(codes)
    R, W = codes[0].shape
    E, _, D = drows.shape
    part = lambda w: pl.BlockSpec((E, cap, w), lambda i: (0, i, 0))
    whole = lambda w: pl.BlockSpec((R, w), lambda i: (0, 0))
    return pl.pallas_call(
        functools.partial(merge_back_kernel, n, E, cap),
        grid=(n,),
        in_specs=[pl.BlockSpec(memory_space=pltpu.SMEM)] + [whole(W)] * n + [part(D), part(128)],
        out_specs=[whole(D + 128)] * n,
        out_shape=[jax.ShapeDtypeStruct((R, D + 128), bf16)] * n,
        compiler_params=pltpu.CompilerParams(vmem_limit_bytes=48 << 20),
        cost_estimate=busy(3 * n),
        name="merge_back",
    )(shift, *codes, drows, dgs)


def merge_out_kernel(n, E, cap, shift_ref, *refs):
    sides, gates, e_ref, outs = refs[:n], refs[n : 2 * n], refs[2 * n], refs[2 * n + 1 :]
    D = e_ref.shape[2]
    for source in range(n):

        @pl.when(pl.program_id(0) == source)
        def _():
            code = sides[source][...]
            gate = gates[source][...]
            total = jnp.zeros((code.shape[0], D), f32)
            for e0 in range(0, E, 4):
                some = range(e0, min(e0 + 4, E))
                parts = []
                for e in some:
                    g = jnp.sum(jnp.where(lanes(gate.shape) == shift_ref[e], gate, 0.0), -1, keepdims=True)
                    parts.append(jnp.where(hot_columns(code, shift_ref[e], cap), g, 0.0).astype(bf16))
                rows = jnp.concatenate([e_ref[e] for e in some], 0)
                total = total + jnp.dot(jnp.concatenate(parts, 1), rows, preferred_element_type=f32)
            outs[source][...] = total.astype(bf16)


def merge_out(shift, codes, gates, eout, cap):
    n = len(codes)
    R, W = codes[0].shape
    E, _, D = eout.shape
    whole = lambda w: pl.BlockSpec((R, w), lambda i: (0, 0))
    return pl.pallas_call(
        functools.partial(merge_out_kernel, n, E, cap),
        grid=(n,),
        in_specs=[pl.BlockSpec(memory_space=pltpu.SMEM)] + [whole(W)] * (2 * n)
        + [pl.BlockSpec((E, cap, D), lambda i: (0, i, 0))],
        out_specs=[whole(D)] * n,
        out_shape=[jax.ShapeDtypeStruct((R, D), bf16)] * n,
        compiler_params=pltpu.CompilerParams(vmem_limit_bytes=48 << 20),
        cost_estimate=busy(11),
        name="merge_out",
    )(shift, *codes, *gates, eout)


def finish_kernel(core_ref, sum_ref, x_ref, dh_ref, gain_ref, *refs):
    out_ref = refs[-1]
    x = x_ref[...].astype(f32)
    r = lax.rsqrt(jnp.mean(x * x, -1, keepdims=True) + EPSILON)
    scaled = sum_ref[...].astype(f32) * gain_ref[...].astype(f32)
    out_ref[...] = dh_ref[...].astype(f32) + r * scaled - x * (r * r * r * jnp.mean(scaled * x, -1, keepdims=True))


def finish(core, summed, tokens, hidden, gain, rows, before=()):
    L, D = tokens.shape
    half = rows // 2
    place = lambda i, p: ((i // 2) * 4 + p[0] * 2 + i % 2, 0)
    return pl.pallas_call(
        finish_kernel,
        grid_spec=pltpu.PrefetchScalarGridSpec(
            num_scalar_prefetch=1, grid=(L // rows,),
            in_specs=[pl.BlockSpec((half, D), lambda i, p: (i, 0)), pl.BlockSpec((half, D), place), pl.BlockSpec((half, D), place),
                      pl.BlockSpec((1, D), lambda i, p: (0, 0))] + [pl.BlockSpec(memory_space=pl.ANY)] * len(before),
            out_specs=pl.BlockSpec((half, D), place)),
        out_shape=jax.ShapeDtypeStruct((L, D), f32),
        input_output_aliases={5 + i: i for i in range(len(before))},
        compiler_params=pltpu.CompilerParams(vmem_limit_bytes=48 << 20),
        cost_estimate=busy(4),
        name="finish",
    )(core, summed, tokens, hidden, gain, *before)


def spread_kernel(n, more, rank_ref, att_ref, w_ref, *refs):
    blocks = refs[:n]
    hidden_ref, do_ref, og_ref = refs[-3:]
    i = pl.program_id(0)

    @pl.when(i == 0)
    def _():
        og_ref[...] = refs[n][...] if more else jnp.zeros_like(og_ref)

    for b in range(n):

        @pl.when(i == b)
        def _():
            block = blocks[b][...]
            hidden_ref[...] = block
            do_ref[...] = lax.dot_general(block, w_ref[...], NT, preferred_element_type=f32).astype(bf16)
            og_ref[...] += lax.dot_general(att_ref[...], block, TN, preferred_element_type=f32)


def spread(rank, first, blocks, attended, w_out, before=None):
    n = len(blocks)
    R, D = blocks[0].shape
    L, H = attended.shape
    place = lambda i, p: (p[0] ^ (i + first), 0)
    whole = lambda a: pl.BlockSpec(a.shape, lambda i, p: (0, 0))
    total = jax.ShapeDtypeStruct((H, D), f32)
    operands = [attended, w_out, *blocks]
    specs = [pl.BlockSpec((R, H), place), whole(w_out)] + [whole(b) for b in blocks]
    aliases = {}
    if before is not None:
        hidden, do, og = before
        operands += [og, hidden, do]
        specs += [whole(og)] + [pl.BlockSpec(memory_space=pl.ANY)] * 2
        aliases = {len(operands) - 1: 0, len(operands): 1}
    return pl.pallas_call(
        functools.partial(spread_kernel, n, before is not None),
        grid_spec=pltpu.PrefetchScalarGridSpec(
            num_scalar_prefetch=1, grid=(n,), in_specs=specs,
            out_specs=[pl.BlockSpec((R, D), place), pl.BlockSpec((R, H), place), whole(total)]),
        out_shape=[pltpu.HBM((L, D), bf16), pltpu.HBM((L, H), bf16), total],
        input_output_aliases=aliases,
        compiler_params=pltpu.CompilerParams(vmem_limit_bytes=32 << 20),
        cost_estimate=busy(3),
        name="spread",
    )(rank, *operands)


def grads_kernel(parts_ref, gate_ref, up_ref, down_ref):
    gate_ref[0] = parts_ref[0, 0].astype(f32)
    up_ref[0] = parts_ref[1, 0].astype(f32)
    down_ref[0] = parts_ref[2, 0].astype(f32).T


def expert_grads(parts):
    _, E, D, F = parts.shape
    one = lambda *s: pl.BlockSpec((1,) + s, lambda e: (e, 0, 0))
    return pl.pallas_call(
        grads_kernel,
        grid=(E,),
        in_specs=[pl.BlockSpec((3, 1, D, F), lambda e: (0, e, 0, 0))],
        out_specs=[one(D, F), one(D, F), one(F, D)],
        out_shape=[pltpu.HBM((E, D, F), f32), pltpu.HBM((E, D, F), f32), pltpu.HBM((E, F, D), f32)],
        compiler_params=pltpu.CompilerParams(vmem_limit_bytes=32 << 20),
        cost_estimate=busy(4),
        name="expert_grads",
    )(parts)


def out_kernel(rank_ref, a_ref, b_ref, w_ref, keep_ref, send_ref):
    keep_ref[...] = jnp.dot(a_ref[...], w_ref[...], preferred_element_type=f32)
    send_ref[...] = jnp.dot(b_ref[...], w_ref[...], preferred_element_type=f32).astype(bf16)


def out_pair(rank, bits, attended, w_out, rows):
    H, D = w_out.shape
    step = min(256, rows)
    n = rows // step
    block = lambda bit: pl.BlockSpec((step, H), lambda i, p: ((p[0] ^ bit) * n + i, 0))
    out = pl.BlockSpec((step, D), lambda i, p: (i, 0))
    return pl.pallas_call(
        out_kernel,
        grid_spec=pltpu.PrefetchScalarGridSpec(
            num_scalar_prefetch=1, grid=(n,),
            in_specs=[block(bits[0]), block(bits[1]), pl.BlockSpec((H, D), lambda i, p: (0, 0))],
            out_specs=[out, out]),
        out_shape=[jax.ShapeDtypeStruct((rows, D), f32), jax.ShapeDtypeStruct((rows, D), bf16)],
        compiler_params=pltpu.CompilerParams(vmem_limit_bytes=32 << 20),
        cost_estimate=busy(3),
        name="out_pair",
    )(rank, attended, attended, w_out)


def parted_kernel(cuts, low_ref, left_ref, right_ref, *outs):
    at = 0
    for out, cut in zip(outs[:-1], cuts):
        out[...] = low_ref[:, at : at + cut].astype(f32)
        at += cut
    half = left_ref.shape[1]
    outs[-1][:, :half] = left_ref[...].astype(f32)
    outs[-1][:, half:] = right_ref[...].astype(f32)


def parted(low, cuts):
    total, half = low.shape
    rows = 2 * half
    part = (total - rows) // 2
    n = 4
    block = lambda r, w, at: pl.BlockSpec((r // n, w), lambda i: (at * n // r + i, 0))
    return pl.pallas_call(
        functools.partial(parted_kernel, cuts),
        grid=(n,),
        in_specs=[block(rows, half, 0), block(part, half, rows), block(part, half, rows + part)],
        out_specs=[block(rows, cut, 0) for cut in cuts] + [block(part, 2 * half, 0)],
        out_shape=[pltpu.HBM((rows, cut), f32) for cut in cuts] + [pltpu.HBM((part, 2 * half), f32)],
        compiler_params=pltpu.CompilerParams(vmem_limit_bytes=32 << 20),
        cost_estimate=busy(3),
        name="parted",
    )(*from_hbm(low, low, low))


def swap(x, axis, bit=1):
    count = lax.axis_size(axis)
    return lax.ppermute(x, axis, [(i, i ^ bit) for i in range(count)])


def total_over(x, axes):
    for axis in axes:
        bit = 1
        while bit < lax.axis_size(axis):
            low = x.astype(bf16)
            x = low.astype(f32) + swap(low, axis, bit).astype(f32)
            bit *= 2
    return x


def wide_tables(length):
    half = HD // 2
    angles = np.arange(length)[:, None] * THETA_BASE ** (-(np.arange(half) / half))[None, :]
    cos, sin = np.cos(angles), np.sin(angles)
    return (
        jnp.asarray(np.concatenate([cos, cos, cos, cos], 1), f32),
        jnp.asarray(np.concatenate([-sin, sin, -sin, sin], 1), f32),
    )


NEAR = [(0, 1), (1, 0), (2, 3), (3, 2)]
MIDDLE = [(1, 2), (2, 1)]
TO_ENDS = [(1, 0), (2, 3)]
FROM_ENDS = [(0, 1), (3, 2)]


def line_first(x):
    return lax.ppermute(x, "z", NEAR), lax.ppermute(x, "z", MIDDLE)


def line_second(near, across):
    return lax.ppermute(near, "z", MIDDLE), lax.ppermute(across, "z", TO_ENDS)


def line_third(across_far):
    return lax.ppermute(across_far, "z", TO_ENDS)


def hold(*arrays):
    return lax.optimization_barrier(arrays)


def line_out(parts):
    return lax.ppermute(parts[3], "z", FROM_ENDS), lax.ppermute(parts[2], "z", FROM_ENDS)


def add_low(a, b):
    return (a.astype(f32) + b.astype(f32)).astype(a.dtype)


def line_over(part, from_end):
    return lax.ppermute(add_low(part, from_end), "z", MIDDLE)


def line_in(part, across_far):
    return lax.ppermute(add_low(part, across_far), "z", NEAR)


def line_sum(parts, from_end_far, from_end):
    own, near, two, three = parts
    across_far = line_over(two, from_end_far)
    across = line_over(three, from_end)
    got = line_in(near, across_far)
    return own.astype(f32) + across.astype(f32) + got.astype(f32)


def per_device_fast(
    tokens,
    prefix,
    gain_attn,
    w_query,
    w_key,
    w_value,
    w_out,
    gain_moe,
    w_router,
    routes,
    fill_order,
    w_gate,
    w_up,
    w_down,
    cotangent,
):
    z, y, x, c = (lax.axis_index(a) for a in ("z", "y", "x", "c"))
    shards = lax.axis_size("x") * lax.axis_size("c")
    groups = lax.axis_size("y")
    rank = x * lax.axis_size("c") + c
    at_end = (z == 0) | (z == lax.axis_size("z") - 1)
    length, width = tokens.shape
    own_rows = routes.shape[0]
    local = w_gate.shape[0]
    cap = own_rows * TOPK // EXPERTS

    expert_ids = jnp.arange(EXPERTS, dtype=jnp.int32)
    member = jnp.sum((routes[:, :, None] == expert_ids[None, None, :]).astype(f32), 1)
    priority = fill_order[0]
    earlier = (priority[None, :] < priority[:, None]).astype(bf16)
    slot_full = jnp.dot(earlier, member.astype(bf16), preferred_element_type=f32)
    code = jnp.where(member > 0, jnp.minimum(slot_full, float(cap)), -1.0).astype(bf16)
    code = jnp.pad(code, ((0, 0), (0, 128 - EXPERTS)), constant_values=-1)
    side_own = jnp.concatenate([cotangent, code], 1)
    side_near, side_across = line_first(side_own)
    router_wide = jnp.pad(w_router, ((0, 0), (0, 128 - EXPERTS)))
    shift = z * groups * local + jnp.arange(groups * local, dtype=jnp.int32)
    shift_end = jnp.concatenate([shift, at_end.astype(jnp.int32)[None]])


    own_weights = jnp.stack([w_gate, w_up, w_down.transpose(0, 2, 1)])
    weights = lax.all_gather(own_weights, ("y", "x", "c"), axis=0, tiled=False)
    weights = weights.reshape((groups, shards) + own_weights.shape)

    cos, sin = wide_tables(length)
    normed_one, query, key, value = project(tokens, gain_attn[None], w_query, w_key, w_value, cos, sin)
    first_half = attend(prefix, query, key, value, 0, BQ, BK)
    *first_half, side_near, side_across = hold(*first_half, side_near, side_across)
    side_far, side_relay = line_second(side_near, side_across)
    attended, log_total = attend(prefix, query, key, value, 1, BQ, BK, first_half)
    rank_row = rank.astype(jnp.int32)[None]
    far_keep, far_send = out_pair(rank_row, (2, 3), attended, w_out, own_rows)
    far_keep, side_far = hold(far_keep, side_far)
    side_last = line_third(side_far)
    far_sum = far_keep + swap(far_send, "c").astype(f32)
    far_got = swap(far_sum.astype(bf16), "x")
    near_keep, near_send = out_pair(rank_row, (0, 1), attended, w_out, own_rows)
    near_sum = near_keep + swap(near_send, "c").astype(f32)
    near_sum, far_got, side_relay, side_last = hold(near_sum, far_got, side_relay, side_last)
    x_rows = lax.dynamic_slice_in_dim(tokens, rank * own_rows, own_rows, 0).astype(f32)
    hidden_in = x_rows + near_sum + far_got.astype(f32)
    rms_two = lax.rsqrt(jnp.mean(hidden_in * hidden_in, -1, keepdims=True) + EPSILON)
    gain_two = gain_moe.astype(f32)
    normed_two = (hidden_in * rms_two * gain_two).astype(bf16)

    near, across = line_first(normed_two)

    def pick_of(rows, sides):
        return pick(shift_end, rows, sides, router_wide, cap)

    pick_own = pick_of((normed_two,), (side_own,))
    near, across, *pick_own = hold(near, across, *pick_own)
    far, relay = line_second(near, across)
    close = [pick_own, pick_of((near,), (side_near,))]
    half_close = ffn(close, weights, (0,))
    far, relay, *half_close = hold(far, relay, *half_close)
    last = line_third(far)
    done_close = ffn(close, weights, (1,), half_close)
    apart = [pick_of((relay, far), (side_relay, side_far))]
    last, *done_close = hold(last, *done_close)
    apart.append(pick_of((last, across), (side_last, side_across)))
    done_apart = ffn(apart, weights, (0, 1))
    picked = close + apart
    gates = [p[3] for p in picked]
    codes = [p[4] for p in picked]
    far_back = merge_back(shift, codes[2:], done_apart[1], done_apart[2], cap)
    back = [*merge_back(shift, codes[:2], done_close[1], done_close[2], cap), *far_back]
    back_end_far, back_end = line_out(back)
    late_act, *_ = hold(done_apart[3], *far_back)
    used = (done_close[3], late_act), (done_close[4], done_apart[4]), shards, groups
    parts = wgrad(picked, *used)
    back_end_far, parts = hold(back_end_far, parts)
    across_far = line_over(back[2], back_end_far)
    across = line_over(back[3], back_end)
    late_close, late_apart, _ = hold(done_close[0], done_apart[0], across_far)
    out_parts = [
        *merge_out(shift, codes[:2], gates[:2], late_close, cap),
        *merge_out(shift, codes[2:], gates[2:], late_apart, cap),
    ]
    got = line_in(back[1], across_far)
    got, across, *out_parts = hold(got, across, *out_parts)
    back_own = back[0].astype(f32) + across.astype(f32) + got.astype(f32)
    out_end_far, out_end = line_out(out_parts)
    part_sum = lax.psum_scatter(
        parts.reshape((groups * shards,) + parts.shape[2:]), ("y", "x", "c"), scatter_dimension=0, tiled=False
    )

    gate_own = gates[0]
    gate_grad = back_own[:, width:]
    logit_grad = gate_own * (gate_grad - jnp.sum(gate_own * gate_grad, -1, keepdims=True))
    logit_low = logit_grad.astype(bf16)
    normed_two_grad = back_own[:, :width] + lax.dot_general(
        logit_low, router_wide, (((1,), (1,)), ((), ())), preferred_element_type=f32
    )
    router_part = lax.dot_general(
        logit_low, normed_two, (((0,), (0,)), ((), ())), preferred_element_type=f32
    )[:EXPERTS]
    gain_two_part = jnp.sum(normed_two_grad * hidden_in * rms_two, 0)
    scaled_two = normed_two_grad * gain_two
    hidden_grad = (
        cotangent.astype(f32)
        + rms_two * scaled_two
        - hidden_in * rms_two**3 * jnp.mean(scaled_two * hidden_in, -1, keepdims=True)
    ).astype(bf16)
    small = jnp.concatenate([router_part, gain_two_part[None], jnp.zeros((7, width), f32)], 0)
    hidden_over_x = swap(hidden_grad, "x")
    near_done = spread(rank_row, 0, [hidden_grad, swap(hidden_grad, "c")], attended, w_out)
    *near_done, out_end_far, out_end = hold(*near_done, out_end_far, out_end)
    out_two, out_three = add_low(out_parts[2], out_end_far), add_low(out_parts[3], out_end)
    hidden_over_x, out_two, out_three, *near_done = hold(hidden_over_x, out_two, out_three, *near_done)
    hidden_all, attended_grad, out_grad = spread(
        rank_row, 2, [hidden_over_x, swap(hidden_over_x, "c")], attended, w_out, near_done
    )
    attended_grad, small, out_low = hold(attended_grad, small, out_grad.astype(bf16))
    out_far, out_across = (lax.ppermute(part, "z", MIDDLE) for part in (out_two, out_three))
    heads_back = attend_back(
        prefix, query, key, value, attended, attended_grad, log_total, cos, sin, BQ, BK_BACK
    )
    heads_in = jnp.concatenate([w_query, w_key, w_value], 1)
    heads_grad = jnp.einsum("id,ih->dh", normed_one, heads_back, preferred_element_type=f32)
    low = jnp.concatenate([heads_grad.astype(bf16), out_low[:, : width // 2], out_low[:, width // 2 :]], 0)
    gain_one_part = jnp.sum(heads_grad * heads_in.astype(f32), 1) / gain_attn.astype(f32)
    small = jnp.concatenate([small[: EXPERTS + 1], gain_one_part[None], small[EXPERTS + 2 :]], 0)
    heads_back, low, part_sum, out_far, out_across = hold(heads_back, low, part_sum, out_far, out_across)
    out_got = line_in(out_parts[1], out_far)

    low_part = lax.psum_scatter(low, ("z", "y"), scatter_dimension=0, tiled=True)

    by_core = heads_back.reshape(shards // 2, 2, own_rows, -1)

    def rows_of(which):
        rows = lax.dynamic_index_in_dim(by_core, which, 1, keepdims=False)
        return lax.dot_general(rows, heads_in, (((2,), (1,)), ((), ())), preferred_element_type=f32)

    from_core = swap(rows_of(1 - c).astype(bf16), "c")
    core_sum = (rows_of(c) + from_core.astype(f32)).astype(bf16)
    core_got, low_part, out_got, small = hold(swap(core_sum, "x"), low_part, out_got, small)
    rest = total_over(small, ("c", "x", "y", "z"))
    moe_own = out_parts[0].astype(f32) + out_across.astype(f32) + out_got.astype(f32)
    block_output = (hidden_in + moe_own).astype(bf16)
    low_all = lax.all_gather(low_part, ("z", "y"), axis=0, tiled=True)
    summed_grads = expert_grads(part_sum)
    chip_sum = (core_sum.astype(f32) + core_got.astype(f32)).astype(bf16)
    other_sum = swap(chip_sum, "c")
    core = c.astype(jnp.int32)[None]
    gain_row = gain_attn[None]
    input_grad = finish(core, chip_sum.reshape(-1, width), tokens, hidden_all, gain_row, own_rows)
    other_sum, input_grad, *summed_grads = hold(other_sum, input_grad, *summed_grads)
    input_grad = finish(
        1 - core, other_sum.reshape(-1, width), tokens, hidden_all, gain_row, own_rows, (input_grad,)
    )
    smalls = rest[EXPERTS + 1], rest[EXPERTS], rest[:EXPERTS].T
    low_all, input_grad, block_output, *smalls = hold(low_all, input_grad, block_output, *smalls)
    heads = parted(low_all, (w_query.shape[1], w_key.shape[1], w_value.shape[1]))
    return (
        block_output,
        input_grad,
        smalls[0],
        *heads,
        smalls[1],
        smalls[2],
        *summed_grads,
    )


def group_gather(x, axes):
    return lax.all_gather(x, axes, axis=0, tiled=False)


def per_device_general(
    tokens,
    prefix,
    gain_attn,
    w_query,
    w_key,
    w_value,
    w_out,
    gain_moe,
    w_router,
    routes,
    fill_order,
    w_gate,
    w_up,
    w_down,
    cotangent,
):
    f32 = jnp.float32
    bf16 = jnp.bfloat16
    z_count = lax.axis_size("z")
    y_count = lax.axis_size("y")
    shards = lax.axis_size("x") * lax.axis_size("c")
    z_rank = lax.axis_index("z")
    tensor_rank = lax.axis_index("x") * lax.axis_size("c") + lax.axis_index("c")
    length = tokens.shape[0]
    model_width = tokens.shape[1]
    own_rows = routes.shape[0]
    local_experts = w_gate.shape[0]
    group_experts = local_experts * y_count
    capacity = own_rows * TOPK // EXPERTS
    heads_local = w_query.shape[1] // HD
    kv_local = w_key.shape[1] // HD
    group_size = heads_local // kv_local
    block_rows = min(512, length)
    block_count = length // block_rows
    score_scale = HD ** (-0.5)
    hidden = w_gate.shape[2] * shards

    expert_ids = jnp.arange(EXPERTS, dtype=jnp.int32)
    member = jnp.sum((routes[:, :, None] == expert_ids[None, None, :]).astype(f32), 1)
    priority = fill_order[0]
    earlier = (priority[None, :] < priority[:, None]).astype(bf16)
    slot_full = jnp.dot(earlier, member.astype(bf16), preferred_element_type=f32)
    slot_code = jnp.where(member > 0, jnp.minimum(slot_full, float(capacity)), -1.0).astype(bf16)

    weights_gate = group_gather(w_gate, ("y", "x", "c")).reshape(
        y_count, shards, local_experts, model_width, -1
    )
    weights_up = group_gather(w_up, ("y", "x", "c")).reshape(
        y_count, shards, local_experts, model_width, -1
    )
    weights_down = group_gather(w_down, ("y", "x", "c")).reshape(
        y_count, shards, local_experts, -1, model_width
    )
    weights_gate = weights_gate.transpose(0, 2, 3, 1, 4).reshape(group_experts, model_width, hidden)
    weights_up = weights_up.transpose(0, 2, 3, 1, 4).reshape(group_experts, model_width, hidden)
    weights_down = weights_down.transpose(0, 2, 1, 3, 4).reshape(group_experts, hidden, model_width)
    cot_all = lax.all_gather(cotangent, "z", axis=0, tiled=False)
    code_all = lax.all_gather(slot_code, "z", axis=0, tiled=False)

    x_full = tokens.astype(f32)
    rms_one = lax.rsqrt(jnp.mean(x_full * x_full, -1, keepdims=True) + EPSILON)
    gain_one = gain_attn.astype(f32)
    normed_one = (x_full * rms_one * gain_one).astype(bf16)
    query_raw = jnp.dot(normed_one, w_query, preferred_element_type=f32)
    key_raw = jnp.dot(normed_one, w_key, preferred_element_type=f32)
    values = (
        jnp.dot(normed_one, w_value, preferred_element_type=f32)
        .astype(bf16)
        .reshape(length, kv_local, HD)
    )
    cosine, sine = rope_tables(length, HD)
    query_rot = rotate(query_raw.reshape(length, heads_local, HD), cosine, sine, 1.0).astype(bf16)
    key_rot = rotate(key_raw.reshape(length, kv_local, HD), cosine, sine, 1.0).astype(bf16)
    query_blocks = query_rot.reshape(block_count, block_rows, kv_local, group_size, HD)
    block_starts = jnp.arange(block_count, dtype=jnp.int32) * block_rows
    positions = jnp.arange(length, dtype=jnp.int32)
    prefix_len = prefix[0]

    def block_scores(query_block, offset):
        query_pos = offset + jnp.arange(block_rows, dtype=jnp.int32)
        raw_scores = (
            jnp.einsum("igjd,kgd->gjik", query_block, key_rot, preferred_element_type=jnp.float32)
            * score_scale
        )
        visible = (positions[None, :] <= query_pos[:, None]) | (positions[None, :] < prefix_len)
        return jnp.where(visible[None, None], raw_scores, -1e30)

    def attend_block(inputs):
        query_block, offset = inputs
        scores = block_scores(query_block, offset)
        row_peak = jnp.max(scores, -1, keepdims=True)
        weights = jnp.exp(scores - row_peak)
        row_total = jnp.sum(weights, -1, keepdims=True)
        probabilities = (weights / row_total).astype(jnp.bfloat16)
        attended = jnp.einsum(
            "gjik,kgd->igjd", probabilities, values, preferred_element_type=jnp.float32
        )
        return (attended.astype(jnp.bfloat16), (row_peak + jnp.log(row_total))[..., 0])

    attended_blocks, log_totals = lax.map(attend_block, (query_blocks, block_starts))
    attended_all = attended_blocks.reshape(length, heads_local * HD)
    attention_rows = lax.psum_scatter(
        jnp.dot(attended_all, w_out, preferred_element_type=f32).astype(bf16),
        ("x", "c"),
        scatter_dimension=0,
        tiled=True,
    ).astype(f32)
    x_rows = lax.dynamic_slice_in_dim(tokens, tensor_rank * own_rows, own_rows, 0).astype(f32)
    hidden_in = x_rows + attention_rows
    rms_two = lax.rsqrt(jnp.mean(hidden_in * hidden_in, -1, keepdims=True) + EPSILON)
    gain_two = gain_moe.astype(f32)
    normed_two = (hidden_in * rms_two * gain_two).astype(bf16)
    normed_all = lax.all_gather(normed_two, "z", axis=0, tiled=False)

    def gates(rows, code):
        logits = jnp.dot(rows, w_router, preferred_element_type=f32)
        chosen = jnp.where(code >= 0, logits, -jnp.inf)
        raised = jnp.exp(chosen - jnp.max(chosen, -1, keepdims=True))
        return raised / jnp.sum(raised, -1, keepdims=True)

    gate_own = gates(normed_two, slot_code)
    first = z_rank * group_experts
    gate_all = jax.vmap(gates)(normed_all, code_all)
    gate_group = lax.dynamic_slice_in_dim(gate_all, first, group_experts, 2)
    code_group = lax.dynamic_slice_in_dim(code_all, first, group_experts, 2).astype(jnp.int32)
    slot_ids = jnp.arange(capacity, dtype=jnp.int32)
    hot = code_group.transpose(2, 0, 1)[:, :, None, :] == slot_ids[None, None, :, None]
    pick = hot.astype(bf16)
    pick_gate = jnp.where(hot, gate_group.transpose(2, 0, 1)[:, :, None, :], 0.0)
    gate_slot = jnp.sum(pick_gate, -1)
    rows_in = jnp.einsum("esci,sid->escd", pick, normed_all, preferred_element_type=f32).astype(bf16)
    rows_dy = jnp.einsum("esci,sid->escd", pick, cot_all, preferred_element_type=f32)
    gate_pre = jnp.einsum("escd,edf->escf", rows_in, weights_gate, preferred_element_type=f32)
    up_pre = jnp.einsum("escd,edf->escf", rows_in, weights_up, preferred_element_type=f32)
    activated = (gate_pre / (1.0 + jnp.exp(-gate_pre)) * up_pre).astype(bf16)
    expert_out = jnp.einsum(
        "escf,efd->escd", activated, weights_down, preferred_element_type=f32
    ).astype(bf16)
    out_grad_rows = (rows_dy * gate_slot[..., None]).astype(bf16)
    gate_grad_slot = jnp.sum(rows_dy * expert_out.astype(f32), -1)
    gate_grad = jnp.einsum("esci,esc->sie", pick.astype(f32), gate_grad_slot, precision=HIGHEST)
    moe_part = jnp.einsum(
        "esci,escd->sid", pick_gate.astype(bf16), expert_out, preferred_element_type=f32
    ).astype(bf16)
    hid_grad = jnp.einsum("escd,efd->escf", out_grad_rows, weights_down, preferred_element_type=f32)
    sigmoid_g = 1.0 / (1.0 + jnp.exp(-gate_pre))
    back_gate = (hid_grad * up_pre * sigmoid_g * (1.0 + gate_pre * (1.0 - sigmoid_g))).astype(bf16)
    back_up = (hid_grad * gate_pre * sigmoid_g).astype(bf16)
    rows_grad = (
        jnp.einsum("escf,edf->escd", back_gate, weights_gate, preferred_element_type=f32)
        + jnp.einsum("escf,edf->escd", back_up, weights_up, preferred_element_type=f32)
    ).astype(bf16)
    rows_part = jnp.einsum("esci,escd->sid", pick, rows_grad, preferred_element_type=f32).astype(bf16)
    down_part = jnp.einsum("escf,escd->efd", activated, out_grad_rows, preferred_element_type=f32)
    gate_part = jnp.einsum("escd,escf->edf", rows_in, back_gate, preferred_element_type=f32)
    up_part = jnp.einsum("escd,escf->edf", rows_in, back_up, preferred_element_type=f32)

    gate_grad_wide = lax.dynamic_update_slice_in_dim(
        jnp.zeros((z_count, own_rows, EXPERTS), f32), gate_grad, first, 2
    )
    back_pack = jnp.concatenate([rows_part, gate_grad_wide.astype(bf16)], -1)
    back_own = lax.psum_scatter(back_pack, "z", scatter_dimension=0, tiled=False).astype(f32)
    moe_own = lax.psum_scatter(moe_part, "z", scatter_dimension=0, tiled=False).astype(f32)
    block_output = (hidden_in + moe_own).astype(bf16)

    def shard_sum(part, dim):
        width = part.shape[dim] // shards
        split = part.reshape((y_count, local_experts) + part.shape[1:dim] + (shards, width) + part.shape[dim + 1 :])
        split = jnp.moveaxis(split, dim + 1, 1).astype(bf16)
        split = split.reshape((y_count * shards,) + split.shape[2:])
        return lax.psum_scatter(split, ("y", "x", "c"), scatter_dimension=0, tiled=False).astype(f32)

    grad_gate = shard_sum(gate_part, 2)
    grad_up = shard_sum(up_part, 2)
    grad_down = shard_sum(down_part, 1)

    normed_two_grad = back_own[:, :model_width]
    gate_grad_own = back_own[:, model_width:]
    logit_grad = gate_own * (
        gate_grad_own - jnp.sum(gate_own * gate_grad_own, -1, keepdims=True)
    )
    router_part = jnp.dot(normed_two.astype(f32).T, logit_grad, precision=HIGHEST)
    normed_two_grad = normed_two_grad + jnp.dot(
        logit_grad, w_router.astype(f32).T, precision=HIGHEST
    )
    gain_two_part = jnp.sum(normed_two_grad * hidden_in * rms_two, 0)
    scaled_two = normed_two_grad * gain_two
    grad_rows = cotangent.astype(f32)
    hidden_grad = (
        grad_rows
        + rms_two * scaled_two
        - hidden_in * rms_two**3 * jnp.mean(scaled_two * hidden_in, -1, keepdims=True)
    )
    shard_part = lax.all_gather(
        hidden_grad.astype(bf16), ("x", "c"), axis=0, tiled=True
    ).astype(f32)
    attended_part = jnp.einsum(
        "id,hd->ih", shard_part.astype(jnp.bfloat16), w_out, preferred_element_type=jnp.float32
    )
    attended_grad = attended_part.astype(jnp.bfloat16)
    out_grad = jnp.einsum(
        "ih,id->hd",
        attended_all,
        shard_part.astype(jnp.bfloat16),
        preferred_element_type=jnp.float32,
    )
    grad_blocks = attended_grad.reshape(block_count, block_rows, kv_local, group_size, HD)

    def back_block(running, inputs):
        key_acc, value_acc = running
        query_block, grad_block, log_block, offset = inputs
        scores = block_scores(query_block, offset)
        probabilities = jnp.exp(scores - log_block[..., None])
        prob_grad = jnp.einsum(
            "igjd,kgd->gjik", grad_block, values, preferred_element_type=jnp.float32
        )
        center = jnp.sum(prob_grad * probabilities, -1, keepdims=True)
        score_grad = (probabilities * (prob_grad - center)).astype(jnp.bfloat16)
        query_grad = (
            jnp.einsum("gjik,kgd->igjd", score_grad, key_rot, preferred_element_type=jnp.float32)
            * score_scale
        )
        key_acc = (
            key_acc
            + jnp.einsum(
                "gjik,igjd->kgd", score_grad, query_block, preferred_element_type=jnp.float32
            )
            * score_scale
        )
        value_acc = value_acc + jnp.einsum(
            "gjik,igjd->kgd",
            probabilities.astype(jnp.bfloat16),
            grad_block,
            preferred_element_type=jnp.float32,
        )
        return ((key_acc, value_acc), query_grad)

    zero_kv = jnp.zeros((length, kv_local, HD), jnp.float32)
    (key_grad, value_grad), query_grads = lax.scan(
        back_block, (zero_kv, zero_kv), (query_blocks, grad_blocks, log_totals, block_starts)
    )
    query_back = (
        rotate(query_grads.reshape(length, heads_local, HD), cosine, sine, -1.0)
        .reshape(length, heads_local * HD)
        .astype(jnp.bfloat16)
    )
    key_back = (
        rotate(key_grad, cosine, sine, -1.0).reshape(length, kv_local * HD).astype(jnp.bfloat16)
    )
    value_back = value_grad.reshape(length, kv_local * HD).astype(jnp.bfloat16)
    query_weight = jnp.einsum(
        "id,ih->dh", normed_one, query_back, preferred_element_type=jnp.float32
    )
    key_weight = jnp.einsum("id,ih->dh", normed_one, key_back, preferred_element_type=jnp.float32)
    value_weight = jnp.einsum(
        "id,ih->dh", normed_one, value_back, preferred_element_type=jnp.float32
    )
    normed_one_grad = jnp.einsum(
        "ih,dh->id", query_back, w_query, preferred_element_type=jnp.float32
    )
    normed_one_grad = normed_one_grad + jnp.einsum(
        "ih,dh->id", key_back, w_key, preferred_element_type=jnp.float32
    )
    normed_one_grad = normed_one_grad + jnp.einsum(
        "ih,dh->id", value_back, w_value, preferred_element_type=jnp.float32
    )
    total_one = lax.psum(normed_one_grad.astype(bf16), ("x", "c")).astype(f32)
    gain_one_part = jnp.sum(normed_one_grad * x_full * rms_one, 0)
    scaled_one = total_one * gain_one
    input_grad = (
        shard_part
        + rms_one * scaled_one
        - x_full * rms_one**3 * jnp.mean(scaled_one * x_full, -1, keepdims=True)
    )
    dp = ("z", "y")
    everyone = ("z", "y", "x", "c")
    summed = [
        lax.psum(part.astype(bf16), dp).astype(f32)
        for part in (query_weight, key_weight, value_weight, out_grad)
    ]
    router_total, gain_one_total, gain_two_total = (
        lax.psum(part.astype(bf16), everyone).astype(f32)
        for part in (router_part, gain_one_part, gain_two_part)
    )
    return (
        block_output,
        input_grad,
        gain_one_total,
        summed[0],
        summed[1],
        summed[2],
        summed[3],
        gain_two_total,
        router_total,
        grad_gate,
        grad_up,
        grad_down,
    )


def solution(mesh):
    dp_count, tensor_count = mesh.devices.shape
    mesh = jax.sharding.Mesh(
        mesh.devices.reshape(dp_count // 2, 2, tensor_count // 2, 2), ("z", "y", "x", "c")
    )
    fast = mesh.devices.shape == (4, 2, 2, 2)
    dp = ("z", "y")
    tensor = ("x", "c")
    both = dp + tensor
    return jax.shard_map(
        per_device_fast if fast else per_device_general,
        mesh=mesh,
        in_specs=(
            P(dp, None),
            P(dp),
            P(),
            P(None, tensor),
            P(None, tensor),
            P(None, tensor),
            P(tensor, None),
            P(),
            P(),
            P(both, None),
            P(both, None),
            P(dp, None, tensor),
            P(dp, None, tensor),
            P(dp, tensor, None),
            P(both, None),
        ),
        out_specs=(
            P(both, None),
            P(dp, None),
            P(),
            P(None, tensor),
            P(None, tensor),
            P(None, tensor),
            P(tensor, None),
            P(),
            P(),
            P(dp, None, tensor),
            P(dp, None, tensor),
            P(dp, tensor, None),
        ),
        check_vma=False,
    )
```
